32 devices in a mesh: dp: 8 (over z, x), head: 4 (over y, core).
Axes of the slice: x: 2, y: 2, z: 4, core: 2. Of those that a mesh axis runs over, the one named last changes fastest.
Arguments:
- layer_input: bfloat16 [512, 32, 768], P('head', 'dp'), may hold values from -6 to 6
- lengths: int32 [32], P('dp'), may hold values from 64 to 512, as said below
- cotangent: bfloat16 [512, 32, 768], P('head', 'dp'), may hold values from -6 to 6
- w_qkv: float32 [3, 768, 768], P(None, 'dp', 'head'), may hold values from -0.21875 to 0.21875
- w_out: float32 [768, 768], P('head', 'dp'), may hold values from -1.75 to 1.75
- w_up: float32 [768, 3072], P(None, ('dp', 'head')), may hold values from -0.21875 to 0.21875
- w_down: float32 [3072, 768], P(('dp', 'head')), may hold values from -0.109375 to 0.109375
- vectors: float32 [9216], P(('dp', 'head')), may hold values from -0.6 to 1.45
- mom_qkv: float32 [3, 768, 768], P(None, 'dp', 'head'), may hold values from -160 to 160
- mom_out: float32 [768, 768], P('head', 'dp'), may hold values from -80 to 80
- mom_up: float32 [768, 3072], P(None, ('dp', 'head')), may hold values from -80 to 80
- mom_down: float32 [3072, 768], P(('dp', 'head')), may hold values from -160 to 160
- mom_vec: float32 [9216], P(('dp', 'head')), may hold values from -384 to 384
- avg_qkv: float32 [3, 768, 768], P(None, 'dp', 'head'), may hold values from -0.21875 to 0.21875
- avg_out: float32 [768, 768], P('head', 'dp'), may hold values from -1.75 to 1.75
- avg_up: float32 [768, 3072], P(None, ('dp', 'head')), may hold values from -0.21875 to 0.21875
- avg_down: float32 [3072, 768], P(('dp', 'head')), may hold values from -0.109375 to 0.109375
- avg_vec: float32 [9216], P(('dp', 'head')), may hold values from -3 to 3
Outputs:
- layer_output: bfloat16 [512, 32, 768], P('head', 'dp')
- grad_input: float32 [512, 32, 768], P('head', 'dp')
- grad_qkv: float32 [3, 768, 768], P(None, 'dp', 'head')
- grad_out: float32 [768, 768], P('head', 'dp')
- grad_up: float32 [768, 3072], P(None, ('dp', 'head'))
- grad_down: float32 [3072, 768], P(('dp', 'head'))
- grad_vec: float32 [9216], P(('dp', 'head'))
- new_qkv: float32 [3, 768, 768], P(None, 'dp', 'head')
- new_out: float32 [768, 768], P('head', 'dp')
- new_up: float32 [768, 3072], P(None, ('dp', 'head'))
- new_down: float32 [3072, 768], P(('dp', 'head'))
- new_vec: float32 [9216], P(('dp', 'head'))
- new_mom_qkv: float32 [3, 768, 768], P(None, 'dp', 'head')
- new_mom_out: float32 [768, 768], P('head', 'dp')
- new_mom_up: float32 [768, 3072], P(None, ('dp', 'head'))
- new_mom_down: float32 [3072, 768], P(('dp', 'head'))
- new_mom_vec: float32 [9216], P(('dp', 'head'))
- new_avg_qkv: float32 [3, 768, 768], P(None, 'dp', 'head')
- new_avg_out: float32 [768, 768], P('head', 'dp')
- new_avg_up: float32 [768, 3072], P(None, ('dp', 'head'))
- new_avg_down: float32 [3072, 768], P(('dp', 'head'))
- new_avg_vec: float32 [9216], P(('dp', 'head'))
The draws below stay inside these ranges and needn't reach their ends.
Inputs may be any that keep to these rules, and one draw needn't show every extreme that they name: `lengths`: in each aligned block of 2 documents at least one has length 512.
All inputs are finite; a program needn't handle non-finite values.
Results may differ from the reference program's by a relative error of at most 0.013.
The reference program's roundings to bfloat16 on the way count: a program that leaves them out, or rounds other values in their place, can miss the bound.
Values may be sent and summed in bfloat16 or wider, within the bound.
No kernel may reach another device: no remote copies, remote signals or barrier semaphores. Data moves between devices by JAX's collectives and lax.ppermute only.
A program may use at most 192 MiB of HBM per device.

```python
import math
import jax
import jax.numpy as jnp
from jax import lax

D = 768
H = 12
HD = 64
FF = 3072
LEN = 512
MIN_LEN = 64
MICRO = 2
DOC_DEV = 4
DOCS = 32
VEC = 9216


def draw_lengths(key, part):
    key = jax.random.fold_in(key, 11)
    key_values, key_chosen = jax.random.split(key)
    block_docs = DOC_DEV // MICRO
    values = jax.random.randint(key_values, (DOCS // block_docs, block_docs), MIN_LEN, LEN + 1)
    chosen = jax.random.randint(key_chosen, (DOCS // block_docs, 1), 0, block_docs)
    longest = jnp.arange(block_docs)[None, :] == chosen
    return jnp.where(longest, LEN, values).reshape(DOCS).astype(jnp.int32)


def draw_vectors(key, part):
    key = jax.random.fold_in(key, 23)
    sample = jnp.clip(jax.random.normal(key, (12, D), jnp.float32), -3.0, 3.0) / 3.0
    gain_rows = (jnp.arange(12) == 3) | (jnp.arange(12) == 10)
    values = jnp.where(gain_rows[:, None], 1.0 + 0.45 * sample, 0.6 * sample)
    return values.reshape(12 * D).astype(jnp.float32)


def levels(key, dims, cuts, low, largest):
    loudness, own = 1.0, jax.random.fold_in(key, 6)
    for axis_at, parts in cuts:
        draws = jnp.exp(jax.random.uniform(jax.random.fold_in(own, axis_at), (parts,), jnp.float32, low / len(cuts), largest / len(cuts)))
        loudness = loudness * jnp.repeat(draws, dims[axis_at] // parts).reshape([-1 if axis == axis_at else 1 for axis in range(len(dims))])
    return loudness


def scatter_about(rng, extent, scale, reach, cuts=(), dtype=jnp.bfloat16):
    values = scale * jax.random.normal(rng, extent, jnp.float32)
    if cuts:
        values = values * levels(rng, extent, cuts, -0.22, 0.18)
    return jnp.clip(values, -reach, reach).astype(dtype)


def setup_inputs(seed: int = 0) -> dict:
    streams_of = jax.random.split(jax.random.key(seed), 19)
    layer_input = scatter_about(streams_of[0], (LEN, DOCS, D), 1.0, 6.0, ((0, 4), (1, 8)))
    lengths = draw_lengths(jax.random.fold_in(streams_of[18], 71), 0)
    cotangent = scatter_about(streams_of[2], (LEN, DOCS, D), 1.0, 6.0, ((0, 4), (1, 8)))
    w_qkv = scatter_about(streams_of[3], (3, D, D), D ** -0.5, 0.21875, ((1, 8), (2, 4)), jnp.float32)
    w_out = scatter_about(streams_of[4], (D, D), (max(1, D * 8 // LEN)) ** -0.5, 1.75, ((0, 4), (1, 8)), jnp.float32)
    w_up = scatter_about(streams_of[5], (D, FF), D ** -0.5, 0.21875, ((1, 32),), jnp.float32)
    w_down = scatter_about(streams_of[6], (FF, D), FF ** -0.5, 0.109375, ((0, 32),), jnp.float32)
    vectors = draw_vectors(jax.random.fold_in(streams_of[18], 71), 0)
    mom_qkv = scatter_about(streams_of[8], (3, D, D), (0.2 * (LEN * DOCS) ** 0.5), 160.0, ((1, 8), (2, 4)), jnp.float32)
    mom_out = scatter_about(streams_of[9], (D, D), (0.1 * (LEN * DOCS) ** 0.5), 80.0, ((0, 4), (1, 8)), jnp.float32)
    mom_up = scatter_about(streams_of[10], (D, FF), (0.1 * (LEN * DOCS) ** 0.5), 80.0, ((1, 32),), jnp.float32)
    mom_down = scatter_about(streams_of[11], (FF, D), (0.2 * (LEN * DOCS) ** 0.5), 160.0, ((0, 32),), jnp.float32)
    mom_vec = scatter_about(streams_of[12], (VEC,), (0.5 * (LEN * DOCS) ** 0.5), 384.0, ((0, 32),), jnp.float32)
    avg_qkv = scatter_about(streams_of[13], (3, D, D), D ** -0.5, 0.21875, ((1, 8), (2, 4)), jnp.float32)
    avg_out = scatter_about(streams_of[14], (D, D), (max(1, D * 8 // LEN)) ** -0.5, 1.75, ((0, 4), (1, 8)), jnp.float32)
    avg_up = scatter_about(streams_of[15], (D, FF), D ** -0.5, 0.21875, ((1, 32),), jnp.float32)
    avg_down = scatter_about(streams_of[16], (FF, D), FF ** -0.5, 0.109375, ((0, 32),), jnp.float32)
    avg_vec = scatter_about(streams_of[17], (VEC,), 0.5, 3.0, ((0, 32),), jnp.float32)
    return {"layer_input": layer_input, "lengths": lengths, "cotangent": cotangent, "w_qkv": w_qkv, "w_out": w_out, "w_up": w_up, "w_down": w_down, "vectors": vectors, "mom_qkv": mom_qkv, "mom_out": mom_out, "mom_up": mom_up, "mom_down": mom_down, "mom_vec": mom_vec, "avg_qkv": avg_qkv, "avg_out": avg_out, "avg_up": avg_up, "avg_down": avg_down, "avg_vec": avg_vec}


@jax.custom_vjp
def low(v):
    return lax.optimization_barrier(v.astype(jnp.bfloat16)).astype(jnp.float32)

@jax.custom_vjp
def low_back(v):
    return v

def low_keep(v):
    return (low(v), None)

def low_pass(kept, grad):
    return (grad,)

def back_keep(v):
    return (v, None)

def back_low(kept, grad):
    return (low(grad),)
low.defvjp(low_keep, low_pass)
low_back.defvjp(back_keep, back_low)
EPSILON = 1e-05
MOMENTUM = 0.9
AVERAGE = 0.9
DECAY = 0.01
RATE_BASE = 0.05
HIGH = lax.Precision.HIGHEST

def layer_norm(values, gain, shift):
    center = values - lax.optimization_barrier(jnp.mean(values, -1, keepdims=True))
    spread = lax.optimization_barrier(jnp.mean(center * center, -1, keepdims=True))
    return center * lax.rsqrt(spread + EPSILON) * gain + shift

@jax.checkpoint
def attend(queries, key_heads, value_heads, doc_lengths):
    length = queries.shape[0]
    scores = low_back(jnp.einsum('lbhe,mbhe->bhlm', queries, key_heads, precision=HIGH)) * HD ** (-0.5)
    allowed = (jnp.arange(length)[None, :] < doc_lengths[:, None])[:, None, None, :]
    scores = jnp.where(allowed, scores, -1e+30)
    log_total = jax.nn.logsumexp(scores, axis=-1, keepdims=True)
    weights = low(jnp.exp(scores - log_total))
    mixed = jnp.einsum('bhlm,mbhe->lbhe', weights, value_heads, precision=HIGH)
    return low(low_back(mixed))

def layer(params, inputs, doc_lengths):
    w_qkv, w_out, w_up, w_down, vectors = params
    rows_vec = low(vectors).reshape(12, D)
    length, batch = (inputs.shape[0], inputs.shape[1])
    projected = low_back(jnp.einsum('lbd,jde->jlbe', inputs, low(w_qkv), precision=HIGH))
    queries = low(projected[0] + rows_vec[0]).reshape(length, batch, H, HD)
    key_heads = low(projected[1]).reshape(length, batch, H, HD)
    value_heads = low(projected[2] + rows_vec[1]).reshape(length, batch, H, HD)
    context = attend(queries, key_heads, value_heads, doc_lengths).reshape(length, batch, D)
    attn_mix = low_back(jnp.einsum('lbk,kd->lbd', context, low(w_out), precision=HIGH))
    hidden_one = layer_norm(inputs + attn_mix + rows_vec[2], rows_vec[3], rows_vec[4])
    up_pre = low_back(jnp.einsum('lbd,df->lbf', low(hidden_one), low(w_up), precision=HIGH)) + rows_vec[5:9].reshape(FF)
    activation = low(jax.nn.gelu(up_pre, approximate=False))
    ffn_out = low_back(jnp.einsum('lbf,fd->lbd', activation, low(w_down), precision=HIGH)) + rows_vec[9]
    return layer_norm(hidden_one + ffn_out, rows_vec[10], rows_vec[11])

def advance(weight, grad, moment, average, decay, rate):
    step_grad = grad + decay * weight
    moment_new = MOMENTUM * moment + step_grad
    weight_new = weight - rate * (step_grad + MOMENTUM * moment_new)
    average_new = AVERAGE * average + (1.0 - AVERAGE) * weight_new
    return (weight_new, moment_new, average_new)

def reference(layer_input, lengths, cotangent, w_qkv, w_out, w_up, w_down, vectors, mom_qkv, mom_out, mom_up, mom_down, mom_vec, avg_qkv, avg_out, avg_up, avg_down, avg_vec):
    group = math.gcd(DOCS, max(1, 4096 // LEN))
    count = DOCS // group
    inputs_all = layer_input.astype(jnp.float32).reshape(LEN, count, group, D).transpose(1, 0, 2, 3)
    cots_all = cotangent.astype(jnp.float32).reshape(LEN, count, group, D).transpose(1, 0, 2, 3)
    lens_all = lengths.reshape(count, group)
    params = (w_qkv, w_out, w_up, w_down, vectors)

    def one_group(carry, item):
        inputs, cots, doc_lengths = item
        output, pullback = jax.vjp(lambda prm, inp: layer(prm, inp, doc_lengths), params, inputs)
        alive = (jnp.arange(LEN)[:, None] < doc_lengths[None, :])[:, :, None]
        seed_grad = jnp.where(alive, cots, 0.0)
        grad_params, grad_inputs = pullback(seed_grad)
        carry = jax.tree.map(jnp.add, carry, grad_params)
        return (carry, (output.astype(jnp.bfloat16), grad_inputs))
    zeros_init = jax.tree.map(jnp.zeros_like, params)
    grads, (outs_all, dins_all) = lax.scan(one_group, zeros_init, (inputs_all, cots_all, lens_all))
    layer_output = outs_all.transpose(1, 0, 2, 3).reshape(LEN, DOCS, D)
    grad_input = dins_all.transpose(1, 0, 2, 3).reshape(LEN, DOCS, D)
    grad_qkv, grad_out, grad_up, grad_down, grad_vec = grads
    rate = RATE_BASE / math.sqrt(LEN * DOCS)
    rate_out = rate * math.sqrt(LEN / 8.0)
    new_qkv, new_mom_qkv, new_avg_qkv = advance(w_qkv, grad_qkv, mom_qkv, avg_qkv, DECAY, rate)
    new_out, new_mom_out, new_avg_out = advance(w_out, grad_out, mom_out, avg_out, DECAY, rate_out)
    new_up, new_mom_up, new_avg_up = advance(w_up, grad_up, mom_up, avg_up, DECAY, rate)
    new_down, new_mom_down, new_avg_down = advance(w_down, grad_down, mom_down, avg_down, DECAY, rate)
    new_vec, new_mom_vec, new_avg_vec = advance(vectors, grad_vec, mom_vec, avg_vec, 0.0, rate)
    return (layer_output, grad_input, grad_qkv, grad_out, grad_up, grad_down, grad_vec, new_qkv, new_out, new_up, new_down, new_vec, new_mom_qkv, new_mom_out, new_mom_up, new_mom_down, new_mom_vec, new_avg_qkv, new_avg_out, new_avg_up, new_avg_down, new_avg_vec)
```

```python
import functools
import math

import jax
import jax.numpy as jnp
from jax import lax
from jax.experimental import pallas as pl
from jax.experimental.pallas import tpu as pltpu
from jax.sharding import Mesh
from jax.sharding import PartitionSpec as P

D = 768
HD = 64
FF = 3072
LEN = 512

EPSILON = 1e-05
MOMENTUM = 0.9
AVERAGE = 0.9
DECAY = 0.01
RATE_BASE = 0.05

BF = jnp.bfloat16
F32 = jnp.float32
NT = (((1,), (1,)), ((), ()))
NN = (((1,), (0,)), ((), ()))
DIM = {"c": 0, "x": 1, "y": 2, "z": 3}


def send(values, axis, shift):
    size = lax.axis_size(axis)
    return lax.ppermute(values, axis, [(i, (i + shift) % size) for i in range(size)])


def flip_order(axis):
    size = lax.axis_size(axis)
    return (lax.axis_index(axis) - jnp.arange(size)) % size


def gather_axis(values, axis):
    dim = DIM[axis]
    size = lax.axis_size(axis)
    if size > 4:
        whole = lax.all_gather(values, axis, axis=dim, tiled=True)
        return jnp.take(whole, flip_order(axis), axis=dim)
    return jnp.concatenate([values] + [send(values, axis, k) for k in range(1, size)], dim)


def gather(shard, order):
    values = shard[None, None, None, None]
    for axis in order:
        values = gather_axis(values, axis)
    return values


def scatter_axis(values, axis, last):
    dim = DIM[axis]
    size = lax.axis_size(axis)
    if size > 4:
        whole = jnp.take(values, flip_order(axis), axis=dim)
        parts = lax.all_to_all(whole, axis, dim, dim, tiled=True)
        total = jnp.sum(parts.astype(F32), dim, keepdims=True)
    else:
        part = lambda k: lax.slice_in_dim(values, k, k + 1, axis=dim)
        total = part(0).astype(F32)
        for k in range(1, size):
            total = total + send(part(k), axis, -k).astype(F32)
    return total if last else total.astype(BF)


def scatter(values, order):
    for axis in order:
        values = scatter_axis(values, axis, axis == order[-1])
    return values[0, 0, 0, 0]


def to_documents(values):
    y, c = lax.axis_index("y"), lax.axis_index("c")
    docs = values.transpose(1, 0, 2).reshape(2, 2, values.shape[0], values.shape[2])
    mine = lax.dynamic_index_in_dim(docs, y, 0, keepdims=False)
    theirs = lax.dynamic_index_in_dim(docs, 1 - y, 0, keepdims=False)
    pair = jnp.stack([mine, send(theirs, "y", 1)], 1)
    own = lax.dynamic_index_in_dim(pair, c, 0, keepdims=False)
    other = lax.dynamic_index_in_dim(pair, 1 - c, 0, keepdims=False)
    return jnp.stack([own, send(other, "c", 1)], 0)


def from_documents(values):
    y, c = lax.axis_index("y"), lax.axis_index("c")
    got = send(values[1], "c", 1)
    pair = jnp.stack([jnp.where(c == 0, values[0], got), jnp.where(c == 0, got, values[0])], 0)
    got = send(pair[:, 1], "y", 1)
    own = pair[:, 0]
    docs = jnp.stack([jnp.where(y == 0, own, got), jnp.where(y == 0, got, own)], 0)
    return docs.reshape(4, docs.shape[2], docs.shape[3]).transpose(1, 0, 2)


def dot(a, b, dims):
    return lax.dot_general(a, b, dims, preferred_element_type=F32)


def place_weights(place_ref, source, target, rows):
    across, deep = source.shape[1], source.shape[3]
    for i in range(across):
        for k in range(deep):
            start = place_ref[i * deep + k] * rows
            if rows % 32 == 0:
                start = pl.multiple_of(start, 32)
            target[pl.ds(start, rows), :] = source[0, i, 0, k, :rows]


def forward_kernel(
    rows,
    place_ref,
    x_ref,
    qk_ref,
    vo_ref,
    bias_ref,
    mask_ref,
    qkv_ref,
    lse_ref,
    context_ref,
    mix_ref,
    w_qk,
    w_vo,
):
    step = pl.program_id(0)
    place_weights(place_ref, qk_ref, w_qk, rows)
    place_weights(place_ref, vo_ref, w_vo, rows)
    x = x_ref[...]
    width = w_qk.shape[1] // 2
    bias = bias_ref[0]
    qk = dot(x, w_qk[...], NN)
    v = (dot(x, w_vo[:, :width], NN) + bias[1:2, :width]).astype(BF)
    q = ((qk[:, :width] + bias[0:1, :width]).astype(BF).astype(F32) * HD ** (-0.5)).astype(BF)
    k = qk[:, width:].astype(BF)
    qkv_ref[0, :, :width] = q
    qkv_ref[0, :, width : 2 * width] = k
    qkv_ref[0, :, 2 * width :] = v
    mask = mask_ref[...]
    length = x.shape[0]
    contexts, logs = [], []
    for head in range(width // HD):
        cols = slice(head * HD, (head + 1) * HD)
        s = dot(q[:, cols], k[:, cols], NT) + mask
        peak = jnp.max(s, -1, keepdims=True)
        total = jnp.sum(jnp.exp(s - peak), -1, keepdims=True)
        log_total = peak + jnp.log(total)
        p = jnp.exp(s - log_total).astype(BF)
        contexts.append(dot(p, v[:, cols], NN).astype(BF))
        logs.append(log_total)
    context = jnp.concatenate(contexts, 1)
    context_ref[0] = context
    lanes = lax.broadcasted_iota(jnp.int32, (length, 128), 1)
    packed = jnp.zeros((length, 128), F32)
    for head, log_total in enumerate(logs):
        packed = jnp.where(lanes == head, log_total, packed)
    lse_ref[0] = packed.T[:8]
    mix = dot(context, w_vo[:, width:], NT)

    @pl.when(step == 0)
    def _():
        mix_ref[...] = mix

    @pl.when(step > 0)
    def _():
        mix_ref[...] += mix


def backward_kernel(
    rows,
    place_ref,
    x_ref,
    gr_ref,
    qk_ref,
    vo_ref,
    qkv_ref,
    lse_ref,
    context_ref,
    mask_ref,
    gqk_ref,
    gvo_ref,
    bias_ref,
    gin_ref,
    w_qk,
    w_vo,
    x_t,
    gr_t,
    g_qkv,
):
    step = pl.program_id(0)
    place_weights(place_ref, qk_ref, w_qk, rows)
    place_weights(place_ref, vo_ref, w_vo, rows)

    @pl.when(step == 0)
    def _():
        x_t[...] = x_ref[...].T
        gr_t[...] = gr_ref[...].T

    width = w_qk.shape[1] // 2
    gr = gr_ref[...]
    gc = dot(gr, w_vo[:, width:], NN).astype(BF)
    mask = mask_ref[:, :1]
    sums = []
    for head in range(width // HD):
        q = qkv_ref[0, :, head * HD : (head + 1) * HD]
        k = qkv_ref[0, :, width + head * HD : width + (head + 1) * HD]
        v = qkv_ref[0, :, 2 * width + head * HD : 2 * width + (head + 1) * HD]
        g = gc[:, head * HD : (head + 1) * HD]
        p = jnp.exp(dot(k, q, NT) + mask - lse_ref[0, head : head + 1])
        dp = dot(v, g, NT)
        gv = dot(p.astype(BF), g, NN)
        delta = jnp.sum(p * dp, 0, keepdims=True)
        gs = (p * (dp - delta)).astype(BF)
        gk = dot(gs, q, NN)
        gq = dot(gs.T, (k.astype(F32) * HD ** (-0.5)).astype(BF), NN)
        g_qkv[:, head * HD : (head + 1) * HD] = gq.astype(BF)
        g_qkv[:, width + head * HD : width + (head + 1) * HD] = gk.astype(BF)
        g_qkv[:, 2 * width + head * HD : 2 * width + (head + 1) * HD] = gv.astype(BF)
        sums.append((jnp.sum(gq, 0, keepdims=True), jnp.sum(gv, 0, keepdims=True)))
    bias_ref[0, 0:1, :] = jnp.concatenate([s[0] for s in sums], 1)
    bias_ref[0, 1:2, :] = jnp.concatenate([s[1] for s in sums], 1)
    g_qk = g_qkv[:, : 2 * width]
    g_v = g_qkv[:, 2 * width :]
    gin = dot(g_qk, w_qk[...], NT) + dot(g_v, w_vo[:, :width], NT)

    @pl.when(step == 0)
    def _():
        gin_ref[...] = gin

    @pl.when(step > 0)
    def _():
        gin_ref[...] += gin

    w_qk[...] = dot(x_t[...], g_qk, NN).astype(BF)
    w_vo[:, :width] = dot(x_t[...], g_v, NN).astype(BF)
    w_vo[:, width:] = dot(gr_t[...], context_ref[0], NN).astype(BF)
    across, deep = gqk_ref.shape[1], gqk_ref.shape[3]
    for i in range(across):
        for j in range(deep):
            start = place_ref[i * deep + j] * rows
            if rows % 32 == 0:
                start = pl.multiple_of(start, 32)
            gqk_ref[0, i, 0, j, :rows] = w_qk[pl.ds(start, rows), :]
            gvo_ref[0, i, 0, j] = w_vo[pl.ds(start, rows), :]


def whole(shape):
    return pl.BlockSpec(shape, lambda g: (0,) * len(shape))


def per_group(array):
    rest = array[1:]
    return pl.BlockSpec((1, *rest), lambda g: (g, *(0 for _ in rest)))


def per_corner(shape, rows):
    return pl.BlockSpec(
        (1, shape[1], 1, shape[3], rows, shape[5]), lambda g: (g // 2, 0, g % 2, 0, 0, 0)
    )


def attention_forward(place, x, w_qk, w_vo, biases, mask_row, rows):
    length = x.shape[0]
    pair = w_qk.shape[5]
    width = pair // 2
    outs = [
        jax.ShapeDtypeStruct((4, length, 3 * width), BF),
        jax.ShapeDtypeStruct((4, 8, length), F32),
        jax.ShapeDtypeStruct((4, length, width), BF),
        jax.ShapeDtypeStruct((length, D), F32),
    ]
    return pl.pallas_call(
        functools.partial(forward_kernel, rows),
        grid=(4,),
        in_specs=[
            pl.BlockSpec(memory_space=pltpu.SMEM),
            whole(x.shape),
            per_corner(w_qk.shape, rows),
            per_corner(w_vo.shape, rows),
            per_group(biases.shape),
            whole(mask_row.shape),
        ],
        out_specs=[per_group(o.shape) for o in outs[:3]] + [whole(outs[3].shape)],
        out_shape=outs,
        scratch_shapes=[pltpu.VMEM((D, pair), BF), pltpu.VMEM((D, pair), BF)],
        compiler_params=pltpu.CompilerParams(vmem_limit_bytes=32 << 20),
        cost_estimate=pl.CostEstimate(
            flops=9_000_000_000, bytes_accessed=12_000_000, transcendentals=6_300_000
        ),
        name="attention_forward",
    )(place, x, w_qk, w_vo, biases, mask_row)


def attention_backward(place, x, gr, w_qk, w_vo, qkv, lse, context, mask_col, rows, extra):
    length = x.shape[0]
    pair = w_qk.shape[5]
    width = pair // 2
    lead = w_qk.shape[:4]
    outs = [
        jax.ShapeDtypeStruct((*lead, rows + extra, pair), BF),
        jax.ShapeDtypeStruct((*lead, rows, pair), BF),
        jax.ShapeDtypeStruct((4, 8, width), F32),
        jax.ShapeDtypeStruct((length, D), F32),
    ]
    return pl.pallas_call(
        functools.partial(backward_kernel, rows),
        grid=(4,),
        in_specs=[
            pl.BlockSpec(memory_space=pltpu.SMEM),
            whole(x.shape),
            whole(gr.shape),
            per_corner(w_qk.shape, rows),
            per_corner(w_vo.shape, rows),
            per_group(qkv.shape),
            per_group(lse.shape),
            per_group(context.shape),
            whole(mask_col.shape),
        ],
        out_specs=[
            per_corner(outs[0].shape, rows + extra),
            per_corner(outs[1].shape, rows),
            per_group(outs[2].shape),
            whole(outs[3].shape),
        ],
        out_shape=outs,
        scratch_shapes=[
            pltpu.VMEM((D, pair), BF),
            pltpu.VMEM((D, pair), BF),
            pltpu.VMEM((D, length), BF),
            pltpu.VMEM((D, length), BF),
            pltpu.VMEM((length, 3 * width), BF),
        ],
        compiler_params=pltpu.CompilerParams(vmem_limit_bytes=40 << 20),
        cost_estimate=pl.CostEstimate(
            flops=18_000_000_000, bytes_accessed=16_000_000, transcendentals=3_200_000
        ),
        name="attention_backward",
    )(place, x, gr, w_qk, w_vo, qkv, lse, context, mask_col)


def norm_forward(values, gain, shift):
    center = values - jnp.mean(values, -1, keepdims=True)
    inverse = lax.rsqrt(jnp.mean(center * center, -1, keepdims=True) + EPSILON)
    normed = center * inverse
    return (normed * gain + shift, normed, inverse)


def norm_backward(d_result, normed, inverse, gain):
    d_normed = d_result * gain
    return inverse * (
        d_normed
        - jnp.mean(d_normed, -1, keepdims=True)
        - normed * jnp.mean(d_normed * normed, -1, keepdims=True)
    )


def gelu_slope(values):
    return (
        0.5 * (1.0 + lax.erf(values * 0.7071067811865476))
        + values * jnp.exp(-0.5 * values * values) * 0.3989422804014327
    )


def advance(weight, grad, moment, average, decay, rate):
    step_grad = grad + decay * weight
    moment_new = MOMENTUM * moment + step_grad
    weight_new = weight - rate * (step_grad + MOMENTUM * moment_new)
    average_new = AVERAGE * average + (1.0 - AVERAGE) * weight_new
    return (weight_new, moment_new, average_new)


def body(
    layer_input,
    lengths,
    cotangent,
    w_qkv,
    w_out,
    w_up,
    w_down,
    vectors,
    mom_qkv,
    mom_out,
    mom_up,
    mom_down,
    mom_vec,
    avg_qkv,
    avg_out,
    avg_up,
    avg_down,
    avg_vec,
):
    z, x, y, c = (lax.axis_index(a) for a in ("z", "x", "y", "c"))
    deep = lax.axis_size("z")
    blocks = deep * 8
    rows, head_cols = w_qkv.shape[1], w_qkv.shape[2]
    pair = 2 * head_cols
    vec_len = vectors.shape[0]
    ff_rows = w_up.shape[1]
    local = layer_input.shape[0]
    length = 4 * local

    kc, kx, ky, kz = jnp.meshgrid(
        jnp.arange(2), jnp.arange(2), jnp.arange(2), jnp.arange(deep), indexing="ij"
    )
    owner = ((((z - kz) % deep) * 2 + (x ^ kx)) * 4 + (y ^ ky) * 2 + (c ^ kc)).reshape(blocks)
    tz, tx, ty, tc = jnp.meshgrid(
        jnp.arange(deep), jnp.arange(2), jnp.arange(2), jnp.arange(2), indexing="ij"
    )
    seat = ((((c ^ tc) * 2 + (x ^ tx)) * 2 + (y ^ ty)) * deep + (z - tz) % deep).reshape(blocks)
    group_c, group_y = jnp.meshgrid(jnp.arange(2), jnp.arange(2), indexing="ij")
    group_head = ((y ^ group_y) * 2 + (c ^ group_c)).reshape(4)
    head_group = ((c ^ group_y) * 2 + (y ^ group_c)).reshape(4)

    vec_row = jnp.pad(vectors.astype(BF), (0, pair - vec_len))[None]
    pack_qk = jnp.concatenate(
        [jnp.concatenate([w_qkv[0], w_qkv[1]], 1).astype(BF), vec_row], 0
    )
    pack_vo = jnp.concatenate([w_qkv[2], w_out.T], 1).astype(BF)
    doc_x = to_documents(layer_input).reshape(length, D)
    full_qk = gather(pack_qk, ("z", "y", "x", "c"))
    full_vo = gather(pack_vo, ("z", "x", "y", "c"))
    full_up = gather(w_up.T.astype(BF), ("z", "y", "x", "c")).reshape(FF, D)
    full_down = gather(w_down.astype(BF), ("z", "x", "y", "c")).reshape(FF, D)
    doc_cot = to_documents(cotangent).reshape(length, D)

    vec_all = full_qk[..., rows, :vec_len].reshape(blocks, vec_len).astype(F32)
    vec_rows = jnp.take(vec_all, seat, axis=0).reshape(12, D)
    bias_up = jnp.take(vec_rows[5:9].reshape(blocks, ff_rows), owner, axis=0).reshape(FF)
    bias_q = jnp.take(vec_rows[0].reshape(4, head_cols), group_head, axis=0)
    bias_v = jnp.take(vec_rows[1].reshape(4, head_cols), group_head, axis=0)
    biases = jnp.pad(jnp.stack([bias_q, bias_v], 1), ((0, 0), (0, 6), (0, 0)))

    row = jnp.arange(length)
    part = row // local
    position = ((y ^ (part % 2)) * 2 + (c ^ (part // 2))) * local + row % local
    doc_len = lax.dynamic_index_in_dim(lengths, y * 2 + c, 0, keepdims=False)
    alive = position < doc_len
    mask = jnp.where(alive, 0.0, -1e30).astype(F32)

    in_kernel = rows % 32 == 0 and deep <= 4
    if in_kernel:
        place = (((z - jnp.arange(deep)[None, :]) % deep) * 2 + (x ^ jnp.arange(2)[:, None])).reshape(
            2 * deep
        )
        attn_qk, attn_vo, kernel_rows = full_qk, full_vo, rows
    else:
        xs = x ^ jnp.arange(2)
        zs = flip_order("z")

        def true_order(values):
            values = jnp.take(jnp.take(values[..., :rows, :], xs, axis=1), zs, axis=3)
            return values.transpose(0, 2, 3, 1, 4, 5).reshape(2, 1, 2, 1, D, pair)

        place = jnp.zeros((1,), jnp.int32)
        attn_qk, attn_vo, kernel_rows = true_order(full_qk), true_order(full_vo), D
    place = place.astype(jnp.int32)

    qkv, lse, context, mix = attention_forward(
        place, doc_x, attn_qk, attn_vo, biases, mask[None, :], kernel_rows
    )
    first_res = doc_x.astype(F32) + mix + vec_rows[2]
    hidden_one, normed_one, inverse_one = norm_forward(first_res, vec_rows[3], vec_rows[4])
    hidden_b = hidden_one.astype(BF)
    up_pre = lax.dot_general(hidden_b, full_up, NT, preferred_element_type=F32) + bias_up
    act_b = jax.nn.gelu(up_pre, approximate=False).astype(BF)
    second_res = hidden_one + (
        lax.dot_general(act_b, full_down, NN, preferred_element_type=F32) + vec_rows[9]
    )
    result, normed_two, inverse_two = norm_forward(second_res, vec_rows[10], vec_rows[11])
    layer_output = from_documents(result.astype(BF).reshape(2, 2, local, D))

    d_result = jnp.where(alive[:, None], doc_cot.astype(F32), 0.0)
    d_gain_two = jnp.sum(d_result * normed_two, 0)
    d_shift_two = jnp.sum(d_result, 0)
    d_second = norm_backward(d_result, normed_two, inverse_two, vec_rows[10])
    d_bias_down = jnp.sum(d_second, 0)
    d_second_b = d_second.astype(BF)
    lead = (2, 2, 2, deep, ff_rows, D)
    grad_down = lax.dot_general(
        act_b, d_second_b, (((0,), (0,)), ((), ())), preferred_element_type=F32
    )
    grad_down = scatter(grad_down.astype(BF).reshape(lead), ("c", "y", "x", "z"))
    d_act = lax.dot_general(d_second_b, full_down, NT, preferred_element_type=F32)
    d_up = d_act * gelu_slope(up_pre)
    d_bias_up = jnp.sum(d_up, 0)
    d_up_b = d_up.astype(BF)
    grad_up = lax.dot_general(
        d_up_b, hidden_b, (((0,), (0,)), ((), ())), preferred_element_type=F32
    )
    grad_up = scatter(grad_up.astype(BF).reshape(lead), ("c", "x", "y", "z")).T
    d_hidden = d_second + lax.dot_general(d_up_b, full_up, NN, preferred_element_type=F32)
    d_gain_one = jnp.sum(d_hidden * normed_one, 0)
    d_shift_one = jnp.sum(d_hidden, 0)
    d_first = norm_backward(d_hidden, normed_one, inverse_one, vec_rows[3])
    d_bias_out = jnp.sum(d_first, 0)
    d_first_b = d_first.astype(BF)

    mask_col = jnp.broadcast_to(mask[:, None], (length, 128))
    grad_qk, grad_vo, d_bias, d_attn = attention_backward(
        place, doc_x, d_first_b, attn_qk, attn_vo, qkv, lse, context, mask_col, kernel_rows, 8
    )
    grad_input = from_documents((d_first + d_attn).astype(BF).reshape(2, 2, local, D)).astype(F32)

    if not in_kernel:

        def relative_order(values):
            values = values[..., :D, :].reshape(2, 2, deep, 2, rows, pair)
            values = values.transpose(0, 3, 1, 2, 4, 5)
            return jnp.take(jnp.take(values, xs, axis=1), zs, axis=3)

        grad_qk, grad_vo = relative_order(grad_qk), relative_order(grad_vo)
        grad_qk = jnp.pad(grad_qk, ((0, 0),) * 4 + ((0, 8), (0, 0)))

    d_bias_q = jnp.take(d_bias[:, 0], head_group, axis=0).reshape(D)
    d_bias_v = jnp.take(d_bias[:, 1], head_group, axis=0).reshape(D)
    d_bias_up = jnp.take(d_bias_up.reshape(blocks, ff_rows), seat, axis=0).reshape(FF)
    grad_vec = jnp.concatenate(
        [
            d_bias_q,
            d_bias_v,
            d_bias_out,
            d_gain_one,
            d_shift_one,
            d_bias_up,
            d_bias_down,
            d_gain_two,
            d_shift_two,
        ]
    )
    vec_part = jnp.take(grad_vec.reshape(blocks, vec_len), owner, axis=0).astype(BF)
    vec_part = jnp.pad(vec_part, ((0, 0), (0, pair - vec_len))).reshape(2, 2, 2, deep, 1, pair)
    vec_part = jnp.pad(vec_part, ((0, 0),) * 4 + ((0, 7), (0, 0)))
    grad_qk = lax.dynamic_update_slice(grad_qk, vec_part, (0, 0, 0, 0, rows, 0))
    sum_vo = scatter(grad_vo, ("c", "y", "x", "z"))
    sum_qk = scatter(grad_qk, ("c", "x", "y", "z"))
    grad_qkv = jnp.stack(
        [sum_qk[:rows, :head_cols], sum_qk[:rows, head_cols:], sum_vo[:, :head_cols]]
    )
    grad_out = sum_vo[:, head_cols:].T
    grad_vec = sum_qk[rows, :vec_len]

    slots = local * 4 * layer_input.shape[1] * deep * 2
    rate = RATE_BASE / math.sqrt(slots)
    rate_out = rate * math.sqrt(LEN / 8.0)
    new_qkv, new_mom_qkv, new_avg_qkv = advance(w_qkv, grad_qkv, mom_qkv, avg_qkv, DECAY, rate)
    new_out, new_mom_out, new_avg_out = advance(w_out, grad_out, mom_out, avg_out, DECAY, rate_out)
    new_up, new_mom_up, new_avg_up = advance(w_up, grad_up, mom_up, avg_up, DECAY, rate)
    new_down, new_mom_down, new_avg_down = advance(
        w_down, grad_down, mom_down, avg_down, DECAY, rate
    )
    new_vec, new_mom_vec, new_avg_vec = advance(vectors, grad_vec, mom_vec, avg_vec, 0.0, rate)
    return (
        layer_output,
        grad_input,
        grad_qkv,
        grad_out,
        grad_up,
        grad_down,
        grad_vec,
        new_qkv,
        new_out,
        new_up,
        new_down,
        new_vec,
        new_mom_qkv,
        new_mom_out,
        new_mom_up,
        new_mom_down,
        new_mom_vec,
        new_avg_qkv,
        new_avg_out,
        new_avg_up,
        new_avg_down,
        new_avg_vec,
    )


def solution(mesh):
    dp, head = mesh.shape["dp"], mesh.shape["head"]
    fine = Mesh(mesh.devices.reshape(dp // 2, 2, head // 2, 2), ("z", "x", "y", "c"))
    dps, heads, every = ("z", "x"), ("y", "c"), ("z", "x", "y", "c")
    acts = P(heads, dps, None)
    params = (P(None, dps, heads), P(heads, dps), P(None, every), P(every, None), P(every))
    return jax.shard_map(
        body,
        mesh=fine,
        in_specs=(acts, P(dps), acts) + params * 3,
        out_specs=(acts, acts) + params * 4,
        check_vma=False,
    )
```

```python
import functools
import math

import jax
import jax.numpy as jnp
from jax import lax
from jax.experimental import pallas as pl
from jax.experimental.pallas import tpu as pltpu
from jax.sharding import Mesh
from jax.sharding import PartitionSpec as P

D = 768
HD = 64
FF = 3072
LEN = 512

EPSILON = 1e-05
MOMENTUM = 0.9
AVERAGE = 0.9
DECAY = 0.01
RATE_BASE = 0.05

BF = jnp.bfloat16
F32 = jnp.float32
NT = (((1,), (1,)), ((), ()))
NN = (((1,), (0,)), ((), ()))


def send(values, axis, shift=1):
    size = lax.axis_size(axis)
    return lax.ppermute(values, axis, [(i, (i + shift) % size) for i in range(size)])


def corner(array):
    rows, columns = min(8, array.shape[-2]), min(128, array.shape[-1])
    return array.reshape(-1, *array.shape[-2:])[0, :rows, :columns]


def after(values, *others):
    zero = sum(corner(v)[0, 0].astype(F32) * 0.0 for v in jax.tree.leaves(others))
    return jax.tree.map(lambda v: v + zero.astype(v.dtype), values)


def flip_order(axis):
    size = lax.axis_size(axis)
    return (lax.axis_index(axis) - jnp.arange(size)) % size


def gather_z(shard):
    size = lax.axis_size("z")
    if size > 4:
        return jnp.take(lax.all_gather(shard, "z"), flip_order("z"), axis=0)
    return jnp.stack([shard] + [send(shard, "z", k) for k in range(1, size)], 0)


def total(terms):
    result = terms[0].astype(F32)
    for term in terms[1:]:
        result = result + term.astype(F32)
    return result


def swap(terms, axis, others=()):
    part = total([t[1] for t in terms])
    got = send((after(part, others) if others else part).astype(BF), axis)
    return [t[0] for t in terms] + [got]


def scatter_z(values):
    size = lax.axis_size("z")
    if size > 4:
        everything = jnp.stack([values(k).astype(BF) for k in range(size)], 0)
        everything = jnp.take(everything, flip_order("z"), axis=0)
        return list(lax.all_to_all(everything, "z", 0, 0, tiled=True))
    return [values(0)] + [send(values(k).astype(BF), "z", -k) for k in range(1, size)]


def to_documents(values):
    y, c = lax.axis_index("y"), lax.axis_index("c")
    arrays, local, _, width = values.shape
    docs = values.transpose(0, 2, 1, 3).reshape(arrays, 2, 2, local, width)
    mine = lax.dynamic_index_in_dim(docs, y, 1, keepdims=False)
    got_y = send(lax.dynamic_index_in_dim(docs, 1 - y, 1, keepdims=False), "y")
    of = lambda v, core: lax.dynamic_index_in_dim(v, core, 1, keepdims=False)
    got = send(jnp.stack([of(mine, 1 - c), of(got_y, 1 - c)], 1), "c")
    document = jnp.stack([of(mine, c), of(got_y, c), got[:, 0], got[:, 1]], 1)
    return document.reshape(arrays, 4 * local, width), got_y


def from_documents_c(values, local):
    values = values.reshape(2, 2, local, values.shape[1])
    return values[0], send(values[1], "c")


def from_documents_y(own, got_c):
    return send(jnp.stack([own[1], got_c[1]], 0), "y")


def from_documents(own, got_c, got_y):
    y, c = lax.axis_index("y"), lax.axis_index("c")
    docs = jnp.stack([own[0], got_c[0], got_y[0], got_y[1]], 0)
    seats = [(y ^ (doc // 2)) * 2 + (c ^ (doc % 2)) for doc in range(4)]
    return jnp.stack([lax.dynamic_index_in_dim(docs, s, 0, keepdims=False) for s in seats], 1)


def dot(a, b, dims):
    return lax.dot_general(a, b, dims, preferred_element_type=F32)


def normalized(values):
    center = values - jnp.mean(values, -1, keepdims=True)
    inverse = lax.rsqrt(jnp.mean(center * center, -1, keepdims=True) + EPSILON)
    return center * inverse, inverse


def norm_backward(d_result, normed, inverse, gain):
    d_normed = d_result * gain
    return inverse * (
        d_normed
        - jnp.mean(d_normed, -1, keepdims=True)
        - normed * jnp.mean(d_normed * normed, -1, keepdims=True)
    )


def block_start(place_ref, index, rows):
    start = place_ref[index] * rows
    return pl.multiple_of(start, 32) if rows % 32 == 0 else start


def place_weights(place_ref, qk_refs, vo_refs, w_qk, w_vo, rows):
    across, deep = len(qk_refs), qk_refs[0].shape[1]

    def place(group):
        for i in range(across):
            for k in range(deep):
                start = block_start(place_ref, i * deep + k, rows)
                w_qk[pl.ds(start, rows), :] = qk_refs[i][0, k]
                w_vo[pl.ds(start, rows), :] = vo_refs[group][i, k]

    for group in range(2):
        pl.when(pl.program_id(0) == group)(functools.partial(place, group))


def accumulate(step, target, start_ref, value):
    @pl.when(step == 0)
    def _():
        target[...] = value if start_ref is None else start_ref[...] + value

    @pl.when(step > 0)
    def _():
        target[...] += value


def attention_forward_kernel(rows, last, parts, *refs):
    qk_refs, vo_refs, refs = refs[:parts], refs[parts : parts + 2], refs[parts + 2 :]
    place_ref, x_ref, bias_ref, mask_ref, vec_ref = refs[:5]
    if last:
        mix_in, qkv_ref, lse_ref, context_ref = refs[5:9]
        h_ref, hb_ref, n_ref, inv_ref, xt_ref, w_qk, w_vo, mix_ref = refs[9:]
    else:
        mix_in = None
        qkv_ref, lse_ref, context_ref, mix_ref, w_qk, w_vo = refs[5:]
    step = pl.program_id(0)
    place_weights(place_ref, qk_refs, vo_refs, w_qk, w_vo, rows)
    x = x_ref[...]
    width = w_qk.shape[1] // 2
    bias = bias_ref[0]
    qk = dot(x, w_qk[...], NN)
    v = (dot(x, w_vo[:, :width], NN) + bias[1:2, :width]).astype(BF)
    q = ((qk[:, :width] + bias[0:1, :width]).astype(BF).astype(F32) * HD ** (-0.5)).astype(BF)
    k = qk[:, width:].astype(BF)
    qkv_ref[0, :, :width] = q
    qkv_ref[0, :, width : 2 * width] = k
    qkv_ref[0, :, 2 * width :] = v
    mask = mask_ref[0:1]
    length = x.shape[0]
    contexts, logs = [], []
    for head in range(width // HD):
        cols = slice(head * HD, (head + 1) * HD)
        s = dot(q[:, cols], k[:, cols], NT) + mask
        peak = jnp.max(s, -1, keepdims=True)
        total = jnp.sum(jnp.exp(s - peak), -1, keepdims=True)
        log_total = peak + jnp.log(total)
        p = jnp.exp(s - log_total).astype(BF)
        contexts.append(dot(p, v[:, cols], NN).astype(BF))
        logs.append(log_total)
    context = jnp.concatenate(contexts, 1)
    context_ref[0] = context
    lanes = lax.broadcasted_iota(jnp.int32, (length, 128), 1)
    packed = jnp.zeros((length, 128), F32)
    for head, log_total in enumerate(logs):
        packed = jnp.where(lanes == head, log_total, packed)
    lse_ref[0] = packed.T[:8]
    accumulate(step, mix_ref, mix_in, dot(context, w_vo[:, width:], NT))
    if last:

        @pl.when(step == pl.num_programs(0) - 1)
        def _():
            first_res = x_ref[...].astype(F32) + mix_ref[...] + vec_ref[2:3]
            normed, inverse = normalized(first_res)
            hidden = normed * vec_ref[3:4] + vec_ref[4:5]
            n_ref[...] = normed
            inv_ref[...] = jnp.broadcast_to(inverse, inv_ref.shape)
            h_ref[...] = hidden
            hb_ref[...] = hidden.astype(BF)
            xt_ref[...] = x_ref[...].T


def attention_backward_kernel(rows, last, parts, *refs):
    qk_refs, vo_refs, refs = refs[:parts], refs[parts : parts + 2], refs[parts + 2 :]
    place_ref, xt_ref, gr_ref, grt_ref, qkv_ref, lse_ref, context_ref = refs[:7]
    mask_ref, start_ref = refs[7:9]
    if last:
        gqk_ref, gvo_ref, bias_ref, out_ref, w_qk, w_vo, g_qkv, gin_ref = refs[9:]
    else:
        gqk_ref, gvo_ref, bias_ref, gin_ref, w_qk, w_vo, g_qkv = refs[9:]
    step = pl.program_id(0)
    place_weights(place_ref, qk_refs, vo_refs, w_qk, w_vo, rows)
    width = w_qk.shape[1] // 2
    gc = dot(gr_ref[...], w_vo[:, width:], NN).astype(BF)
    mask = mask_ref[:, :1]
    sums = []
    for head in range(width // HD):
        q = qkv_ref[0, :, head * HD : (head + 1) * HD]
        k = qkv_ref[0, :, width + head * HD : width + (head + 1) * HD]
        v = qkv_ref[0, :, 2 * width + head * HD : 2 * width + (head + 1) * HD]
        g = gc[:, head * HD : (head + 1) * HD]
        p = jnp.exp(dot(k, q, NT) + mask - lse_ref[0, head : head + 1])
        dp = dot(v, g, NT)
        gv = dot(p.astype(BF), g, NN)
        delta = jnp.sum(p * dp, 0, keepdims=True)
        gs = (p * (dp - delta)).astype(BF)
        gk = dot(gs, q, NN)
        gq = dot(gs.T, (k.astype(F32) * HD ** (-0.5)).astype(BF), NN)
        g_qkv[:, head * HD : (head + 1) * HD] = gq.astype(BF)
        g_qkv[:, width + head * HD : width + (head + 1) * HD] = gk.astype(BF)
        g_qkv[:, 2 * width + head * HD : 2 * width + (head + 1) * HD] = gv.astype(BF)
        sums.append((jnp.sum(gq, 0, keepdims=True), jnp.sum(gv, 0, keepdims=True)))
    bias_ref[0, 0:1, :] = jnp.concatenate([s[0] for s in sums], 1)
    bias_ref[0, 1:2, :] = jnp.concatenate([s[1] for s in sums], 1)
    g_qk = g_qkv[:, : 2 * width]
    g_v = g_qkv[:, 2 * width :]
    gin = dot(g_qk, w_qk[...], NT) + dot(g_v, w_vo[:, :width], NT)
    accumulate(step, gin_ref, start_ref, gin)

    w_qk[...] = dot(xt_ref[...], g_qk, NN).astype(BF)
    w_vo[:, :width] = dot(xt_ref[...], g_v, NN).astype(BF)
    w_vo[:, width:] = dot(grt_ref[...], context_ref[0], NN).astype(BF)
    across, deep = gqk_ref.shape[0], gqk_ref.shape[2]
    for i in range(across):
        for j in range(deep):
            start = block_start(place_ref, i * deep + j, rows)
            gqk_ref[i, 0, j] = w_qk[pl.ds(start, rows), :]
            gvo_ref[0, i, j] = w_vo[pl.ds(start, rows), :]
    if last:

        @pl.when(step == pl.num_programs(0) - 1)
        def _():
            out_ref[...] = gin_ref[...].astype(BF)


def ffn_weights(refs):
    step = pl.program_id(0)
    up = jnp.where(step < 2, refs[0][...], refs[1][...])
    down = jnp.where(step % 2 == 0, refs[2][...], refs[3][...])
    return up, down


def ffn_forward_kernel(last, *refs):
    up, down = ffn_weights(refs[:4])
    h_ref, hb_ref, bias_ref, vec_ref = refs[4:8]
    if last:
        sum_in, cot_ref, mask_ref = refs[8:11]
        act_ref, slope_ref, out_ref, gr_ref, grb_ref, vec_out, sum_ref = refs[11:]
    else:
        sum_in = None
        act_ref, slope_ref, sum_ref = refs[8:]
    step = pl.program_id(0)
    u = dot(hb_ref[...], up, NT) + bias_ref[0:1]
    phi = 0.5 + 0.5 * lax.erf(u * 0.7071067811865476)
    act = (u * phi).astype(BF)
    act_ref[...] = act
    slope_ref[...] = phi + u * jnp.exp(-0.5 * u * u) * 0.3989422804014327
    accumulate(step, sum_ref, sum_in, dot(act, down, NN))
    if last:

        @pl.when(step == pl.num_programs(0) - 1)
        def _():
            second_res = h_ref[...] + (sum_ref[...] + vec_ref[9:10])
            normed, inverse = normalized(second_res)
            out_ref[...] = (normed * vec_ref[10:11] + vec_ref[11:12]).astype(BF)
            d_result = jnp.where(mask_ref[:, :1] == 0.0, cot_ref[...].astype(F32), 0.0)
            vec_out[0:1] = jnp.sum(d_result * normed, 0, keepdims=True)
            vec_out[1:2] = jnp.sum(d_result, 0, keepdims=True)
            d_second = norm_backward(d_result, normed, inverse, vec_ref[10:11])
            vec_out[2:3] = jnp.sum(d_second, 0, keepdims=True)
            gr_ref[...] = d_second
            grb_ref[...] = d_second.astype(BF)


def ffn_backward_kernel(last, *refs):
    up, down = ffn_weights(refs[:4])
    grb_ref, hb_ref, act_ref, slope_ref, sum_in = refs[4:9]
    if last:
        n_ref, inv_ref, vec_ref = refs[9:12]
        gu_ref, gd_ref, bias_ref, gr_ref, gr1b_ref, grt_ref, vec_out, sum_ref = refs[12:]
    else:
        gu_ref, gd_ref, bias_ref, sum_ref = refs[9:]
    step = pl.program_id(0)
    grb = grb_ref[...]
    d_up = dot(grb, down, NT) * slope_ref[...]
    bias_ref[0:1] = jnp.sum(d_up, 0, keepdims=True)
    d_up_b = d_up.astype(BF)
    gd_ref[...] = dot(act_ref[...].T, grb, NN).astype(BF)
    gu_ref[...] = dot(d_up_b.T, hb_ref[...], NN).astype(BF)
    accumulate(step, sum_ref, sum_in, dot(d_up_b, up, NN))
    if last:

        @pl.when(step == pl.num_programs(0) - 1)
        def _():
            d_hidden = sum_ref[...]
            normed = n_ref[...]
            vec_out[0:1] = jnp.sum(d_hidden * normed, 0, keepdims=True)
            vec_out[1:2] = jnp.sum(d_hidden, 0, keepdims=True)
            d_first = norm_backward(d_hidden, normed, inv_ref[:, :1], vec_ref[3:4])
            vec_out[2:3] = jnp.sum(d_first, 0, keepdims=True)
            gr_ref[...] = d_first
            gr1b_ref[...] = d_first.astype(BF)
            grt_ref[...] = d_first.astype(BF).T


def whole(array):
    shape = array.shape
    return pl.BlockSpec(shape, lambda g: (0,) * len(shape))


def per_group(array):
    rest = array.shape[1:]
    return pl.BlockSpec((1, *rest), lambda g: (g, *(0 for _ in rest)))


def per_corner(array, rows, dim):
    block = [*array.shape[:3], rows, array.shape[4]]
    block[dim] = 1
    return pl.BlockSpec(tuple(block), lambda g: (0, g, 0, 0, 0) if dim else (g, 0, 0, 0, 0))


def per_rows(array, size, crossed):
    if crossed:
        return pl.BlockSpec((size, array.shape[1]), lambda g: (g % 2 * 2 + g // 2, 0))
    return pl.BlockSpec((size, array.shape[1]), lambda g: (g, 0))


def per_columns(array, size):
    return pl.BlockSpec((array.shape[0], size), lambda g: (0, g))


def waiting(kernel, others):
    corners = [corner(v) for v in jax.tree.leaves(others)]
    count = len(corners)
    return lambda *refs: kernel(*refs[count:]), corners, [whole(v) for v in corners]


SMEM_SPEC = pl.BlockSpec(memory_space=pltpu.SMEM)
like = jax.ShapeDtypeStruct


def per_part(array, size, by_x):
    return pl.BlockSpec((size, array.shape[1]), lambda g: (g // 2 if by_x else g % 2, 0))


def attention_weights(weights, rows):
    parts_qk, parts_vo = weights
    specs = []
    for part in parts_qk:
        block = (1, part.shape[1], rows, part.shape[3])
        specs.append(pl.BlockSpec(block, lambda g: (g, 0, 0, 0)))
    for part in parts_vo:
        block = (*part.shape[:2], rows, part.shape[3])
        specs.append(pl.BlockSpec(block, lambda g: (0, 0, 0, 0)))
    return [*parts_qk, *parts_vo], specs


def params(mib):
    return pltpu.CompilerParams(vmem_limit_bytes=mib << 20)


def cost(giga_flops, mega_bytes, mega_exps):
    return pl.CostEstimate(
        flops=int(giga_flops * 1e9),
        bytes_accessed=int(mega_bytes * 1e6),
        transcendentals=int(mega_exps * 1e6),
    )


def attention_forward(place, x, weights, biases, mask, vec_rows, mix, rows):
    length = x.shape[0]
    pair = weights[0][0].shape[3]
    width = pair // 2
    last = mix is not None
    row = like((length, D), F32)
    outs = [
        like((2, length, 3 * width), BF),
        like((2, 8, length), F32),
        like((2, length, width), BF),
    ]
    tail = [row]
    scratch = [pltpu.VMEM((D, pair), BF), pltpu.VMEM((D, pair), BF)]
    operands, specs = attention_weights(weights, rows)
    operands += [place, x, biases, mask, vec_rows]
    specs += [SMEM_SPEC, whole(x), per_group(biases), whole(mask), whole(vec_rows)]
    if last:
        low = like((length, D), BF)
        tail = [row, low, row, like((length, 128), F32), like((D, length), BF)]
        operands.append(mix)
        specs.append(whole(mix))
        scratch.append(pltpu.VMEM((length, D), F32))
    return pl.pallas_call(
        functools.partial(attention_forward_kernel, rows, last, len(weights[0])),
        grid=(2,),
        in_specs=specs,
        out_specs=[per_group(o) for o in outs] + [whole(o) for o in tail],
        out_shape=outs + tail,
        scratch_shapes=scratch,
        compiler_params=params(18),
        cost_estimate=cost(4.5, 6.0, 3.1),
        name="attention_forward_last" if last else "attention_forward",
    )(*operands)


def attention_backward(place, x_t, gr, gr_t, weights, saved, mask, start, rows, last, others):
    length = gr.shape[0]
    pair = weights[0][0].shape[3]
    width = pair // 2
    across = len(weights[0])
    deep = weights[0][0].shape[1]
    qkv, lse, context = saved
    grad_qk = like((across, 2, deep, rows, pair), BF)
    grad_vo = like((2, across, deep, rows, pair), BF)
    outs = [
        grad_qk,
        grad_vo,
        like((2, 8, width), F32),
        like((length, D), BF if last else F32),
    ]
    scratch = [
        pltpu.VMEM((D, pair), BF),
        pltpu.VMEM((D, pair), BF),
        pltpu.VMEM((length, 3 * width), BF),
    ]
    if last:
        scratch.append(pltpu.VMEM((length, D), F32))
    operands, specs = attention_weights(weights, rows)
    kernel = functools.partial(attention_backward_kernel, rows, last, across)
    kernel, corners, corner_specs = waiting(kernel, others)
    return pl.pallas_call(
        kernel,
        grid=(2,),
        in_specs=corner_specs
        + specs
        + [
            SMEM_SPEC,
            whole(x_t),
            whole(gr),
            whole(gr_t),
            per_group(qkv),
            per_group(lse),
            per_group(context),
            whole(mask),
            whole(start),
        ],
        out_specs=[
            per_corner(grad_qk, rows, 1),
            per_corner(grad_vo, rows, 0),
            per_group(outs[2]),
            whole(outs[3]),
        ],
        out_shape=outs,
        scratch_shapes=scratch,
        compiler_params=params(18),
        cost_estimate=cost(0.5, 1.0, 0.1),
        name="attention_backward_last" if last else "attention_backward",
    )(*corners, *operands, place, x_t, gr, gr_t, qkv, lse, context, mask, start)


def ffn_operands(up, down):
    chunk = up[0].shape[0] // 2
    specs = [per_part(u, chunk, False) for u in up] + [per_part(d, chunk, True) for d in down]
    return [*up, *down], specs, chunk


def ffn_forward(h, hb, up, down, bias, vec_rows, tail_operands):
    length = h.shape[0]
    operands, specs, chunk = ffn_operands(up, down)
    hidden = 4 * chunk
    last = len(tail_operands) > 0
    row = like((length, D), F32)
    outs = [like((length, hidden), BF), like((length, hidden), F32)]
    tail = [row]
    scratch = []
    if last:
        low = like((length, D), BF)
        tail = [low, row, low, like((8, D), F32)]
        scratch = [pltpu.VMEM((length, D), F32)]
    return pl.pallas_call(
        functools.partial(ffn_forward_kernel, last),
        grid=(4,),
        in_specs=specs
        + [whole(h), whole(hb), per_columns(bias, chunk), whole(vec_rows)]
        + [whole(t) for t in tail_operands],
        out_specs=[per_columns(o, chunk) for o in outs] + [whole(o) for o in tail],
        out_shape=outs + tail,
        scratch_shapes=scratch,
        compiler_params=params(18),
        cost_estimate=cost(4.9, 12.0, 1.6),
        name="ffn_forward_last" if last else "ffn_forward",
    )(*operands, h, hb, bias, vec_rows, *tail_operands)


def ffn_backward(grb, hb, act, slope, up, down, total, tail_operands, others):
    length = grb.shape[0]
    operands, specs, chunk = ffn_operands(up, down)
    hidden = 4 * chunk
    last = len(tail_operands) > 0
    row = like((length, D), F32)
    grad = like((hidden, D), BF)
    outs = [grad, grad, like((8, hidden), F32)]
    tail = [row]
    scratch = []
    if last:
        tail = [row, like((length, D), BF), like((D, length), BF), like((8, D), F32)]
        scratch = [pltpu.VMEM((length, D), F32)]
    kernel, corners, corner_specs = waiting(functools.partial(ffn_backward_kernel, last), others)
    return pl.pallas_call(
        kernel,
        grid=(4,),
        in_specs=corner_specs
        + specs
        + [whole(grb), whole(hb), per_columns(act, chunk), per_columns(slope, chunk)]
        + [whole(total)]
        + [whole(t) for t in tail_operands],
        out_specs=[
            per_rows(grad, chunk, False),
            per_rows(grad, chunk, True),
            per_columns(outs[2], chunk),
        ]
        + [whole(o) for o in tail],
        out_shape=outs + tail,
        scratch_shapes=scratch,
        compiler_params=params(18),
        cost_estimate=cost(9.7, 16.0, 0.0),
        name="ffn_backward_last" if last else "ffn_backward",
    )(*corners, *operands, grb, hb, act, slope, total, *tail_operands)


def advance(weight, grad, moment, average, decay, rate):
    step_grad = grad + decay * weight
    moment_new = MOMENTUM * moment + step_grad
    weight_new = weight - rate * (step_grad + MOMENTUM * moment_new)
    average_new = AVERAGE * average + (1.0 - AVERAGE) * weight_new
    return (weight_new, moment_new, average_new)


def body(
    layer_input,
    lengths,
    cotangent,
    w_qkv,
    w_out,
    w_up,
    w_down,
    vectors,
    mom_qkv,
    mom_out,
    mom_up,
    mom_down,
    mom_vec,
    avg_qkv,
    avg_out,
    avg_up,
    avg_down,
    avg_vec,
):
    z, x, y, c = (lax.axis_index(a) for a in ("z", "x", "y", "c"))
    deep = lax.axis_size("z")
    blocks = deep * 8
    rows, head_cols = w_qkv.shape[1], w_qkv.shape[2]
    pair = 2 * head_cols
    vec_len = vectors.shape[0]
    ff_rows = w_up.shape[1]
    local = layer_input.shape[0]
    length = 4 * local

    kc, kx, ky, kz = jnp.meshgrid(
        jnp.arange(2), jnp.arange(2), jnp.arange(2), jnp.arange(deep), indexing="ij"
    )
    owner = ((((z - kz) % deep) * 2 + (x ^ kx)) * 4 + (y ^ ky) * 2 + (c ^ kc)).reshape(blocks)
    tz, tx, ty, tc = jnp.meshgrid(
        jnp.arange(deep), jnp.arange(2), jnp.arange(2), jnp.arange(2), indexing="ij"
    )
    seat = ((((c ^ tc) * 2 + (x ^ tx)) * 2 + (y ^ ty)) * deep + (z - tz) % deep).reshape(blocks)
    first, second = jnp.meshgrid(jnp.arange(2), jnp.arange(2), indexing="ij")
    group_head = ((y ^ second) * 2 + (c ^ first)).reshape(4)
    head_group = ((c ^ second) * 2 + (y ^ first)).reshape(4)

    vec_row = jnp.pad(vectors.astype(BF), (0, pair - vec_len))[None]
    pack_qk = jnp.concatenate([w_qkv[0], w_qkv[1]], 1).astype(BF)
    pack_vo = jnp.concatenate([w_qkv[2], w_out.T], 1).astype(BF)
    pack = jnp.concatenate([pack_qk, pack_vo, jnp.pad(vec_row, ((0, 7), (0, 0)))], 0)
    (doc_x, doc_cot), got_y = to_documents(jnp.stack([layer_input, cotangent], 0))
    attn_z = after(gather_z(pack), got_y)
    qk, vo = attn_z[:, :rows], attn_z[:, rows : 2 * rows]
    qk_got, vo_got = send(qk, "y"), send(vo, "x")
    vec = after(attn_z[:, 2 * rows, :vec_len], qk_got)
    qk = after(jnp.stack([qk, qk_got], 0), vo_got)
    vo = after(jnp.stack([vo, vo_got], 0), qk_got)
    qk_got, vo_got = send(qk, "x"), send(vo, "y")
    vec = jnp.stack([vec, send(vec, "y")], 0)
    vec = jnp.stack([vec, send(vec, "x")], 0)
    vec = jnp.stack([vec, send(vec, "c")], 0)
    attn_own = ((qk, qk_got), (vo, vo_got))
    attn_other = jax.tree.map(lambda v: send(v, "c"), attn_own)

    pack = jnp.concatenate([w_up.T.astype(BF), w_down.astype(BF)], 0)
    ffn_z = after(gather_z(after(pack, attn_z)), qk_got, vo_got)
    up, down = ffn_z[:, :ff_rows], ffn_z[:, ff_rows:]
    up_got, down_got = send(up, "y"), send(down, "x")
    up, down = (
        after(jnp.stack([up, up_got], 0), down_got),
        after(jnp.stack([down, down_got], 0), up_got),
    )
    up_got, down_got = send(up, "x"), send(down, "y")

    vec_all = vec.reshape(blocks, vec_len).astype(F32)
    vec_rows = jnp.take(vec_all, seat, axis=0).reshape(12, D)
    bias_up = jnp.take(vec_rows[5:9].reshape(blocks, ff_rows), owner, axis=0).reshape(2, FF // 2)
    bias_q = jnp.take(vec_rows[0].reshape(4, head_cols), group_head, axis=0)
    bias_v = jnp.take(vec_rows[1].reshape(4, head_cols), group_head, axis=0)
    biases = jnp.pad(jnp.stack([bias_q, bias_v], 1), ((0, 0), (0, 6), (0, 0)))

    row = jnp.arange(length)
    part = row // local
    position = ((y ^ (part % 2)) * 2 + (c ^ (part // 2))) * local + row % local
    doc_len = lax.dynamic_index_in_dim(lengths, y * 2 + c, 0, keepdims=False)
    alive = position < doc_len
    mask = jnp.where(alive, 0.0, -1e30).astype(F32)
    mask_row = jnp.broadcast_to(mask[None, :], (8, length))
    mask_col = jnp.broadcast_to(mask[:, None], (length, 128))

    in_kernel = rows % 32 == 0 and deep <= 4
    if in_kernel:
        zs = (z - jnp.arange(deep)[None, :]) % deep
        place = (zs * 2 + (x ^ jnp.arange(2)[:, None])).reshape(2 * deep)
        kernel_rows = rows
    else:
        xs = x ^ jnp.arange(2)
        zs = flip_order("z")

        def true_order(weights):
            qk, vo = (jnp.stack(parts, 0) for parts in weights)
            qk = jnp.take(jnp.take(qk, xs, axis=0), zs, axis=2).transpose(1, 2, 0, 3, 4)
            vo = jnp.take(jnp.take(vo, xs, axis=1), zs, axis=2).transpose(0, 2, 1, 3, 4)
            qk, vo = qk.reshape(2, 1, D, pair), vo.reshape(2, 1, 1, D, pair)
            return ((qk,), (vo[0], vo[1]))

        def relative_order(qk, vo):
            qk = qk.reshape(2, deep, 2, rows, pair).transpose(2, 0, 1, 3, 4)
            vo = vo.reshape(2, deep, 2, rows, pair).transpose(0, 2, 1, 3, 4)
            qk = jnp.take(jnp.take(qk, xs, axis=0), zs, axis=2)
            return qk, jnp.take(jnp.take(vo, xs, axis=1), zs, axis=2)

        place = jnp.zeros((1,), jnp.int32)
        attn_own, attn_other = true_order(attn_own), true_order(attn_other)
        kernel_rows = D
    place = place.astype(jnp.int32)

    *saved_0, mix = attention_forward(
        place, doc_x, attn_own, biases[:2], mask_row, vec_rows, None, kernel_rows
    )
    *saved_1, hidden, hidden_b, normed, inverse, x_t = attention_forward(
        place, doc_x, attn_other, biases[2:], mask_row, vec_rows, mix, kernel_rows
    )
    flat = lambda v: v.reshape(FF // 4, D)
    up_own, down_own = (flat(up), flat(up_got)), (flat(down), flat(down_got))
    up_other = (send(up_own[0], "c"), send(after(up_own[1], hidden_b), "c"))
    down_other = (send(down_own[0], "c"), send(after(down_own[1], hidden_b), "c"))
    act_0, slope_0, mix = ffn_forward(
        hidden, hidden_b, up_own, down_own, bias_up[:1], vec_rows, ()
    )
    act_1, slope_1, result, d_second, d_second_b, vec_two = ffn_forward(
        hidden, hidden_b, up_other, down_other, bias_up[1:], vec_rows, (mix, doc_cot, mask_col)
    )
    out_own, out_c = from_documents_c(result, local)

    lead = (2, 2, deep, ff_rows, D)
    up_1, down_1, d_bias_1, d_hidden = ffn_backward(
        d_second_b, hidden_b, act_1, slope_1, up_other, down_other, d_second, (), ()
    )
    up_1, down_1 = send(up_1, "c"), send(down_1, "c")
    out_y = from_documents_y(out_own, out_c)
    up_0, down_0, d_bias_0, d_first, d_first_b, d_first_t, vec_one = ffn_backward(
        d_second_b,
        hidden_b,
        act_0,
        slope_0,
        up_own,
        down_own,
        d_hidden,
        (normed, inverse, vec_rows),
        (out_c,),
    )
    grad_up = swap([up_0.reshape(lead), up_1.reshape(lead)], "x")
    grad_down = swap([down_0.reshape(lead), down_1.reshape(lead)], "y")
    ffn_c = (up_1, down_1)
    ffn_big = (grad_up[-1], grad_down[-1])
    grad_up, grad_down = swap(grad_up, "y"), swap(grad_down, "x")
    grad_ffn = scatter_z(
        lambda k: jnp.concatenate(
            [total([t[k] for t in grad_up]), total([t[k] for t in grad_down])], 0
        )
    )
    layer_output = from_documents(out_own, out_c, out_y)
    qk_1, vo_1, bias_1, d_attn = attention_backward(
        place, x_t, d_first_b, d_first_t, attn_other, saved_1, mask_col, d_first, kernel_rows, False, (ffn_c, out_y)
    )
    qk_0, vo_0, bias_0, d_input = attention_backward(
        place, x_t, d_first_b, d_first_t, attn_own, saved_0, mask_col, d_attn, kernel_rows, True, ()
    )
    if not in_kernel:
        qk_1, vo_1 = relative_order(qk_1, vo_1)
        qk_0, vo_0 = relative_order(qk_0, vo_0)
    qk_1, vo_1 = send(qk_1, "c"), send(vo_1, "c")
    bias_1 = after(bias_1, ffn_big)

    d_bias = jnp.concatenate([bias_0, bias_1], 0)
    d_bias_q = jnp.take(d_bias[:, 0], head_group, axis=0).reshape(D)
    d_bias_v = jnp.take(d_bias[:, 1], head_group, axis=0).reshape(D)
    d_bias_up = jnp.concatenate([d_bias_0[0], d_bias_1[0]]).reshape(blocks, ff_rows)
    d_bias_up = jnp.take(d_bias_up, seat, axis=0).reshape(FF)
    grad_vec = jnp.concatenate(
        [
            d_bias_q,
            d_bias_v,
            vec_one[2],
            vec_one[0],
            vec_one[1],
            d_bias_up,
            vec_two[2],
            vec_two[0],
            vec_two[1],
        ]
    )
    vec_part = jnp.take(grad_vec.reshape(blocks, vec_len), owner, axis=0)
    vec_part = jnp.pad(vec_part, ((0, 0), (0, pair - vec_len))).reshape(2, 2, 2, deep, 1, pair)
    for axis in ("c", "x", "y"):
        vec_part = vec_part[0] + send(vec_part[1], axis)

    sum_qk, sum_vo = swap([qk_0, qk_1], "x", ffn_big), swap([vo_0, vo_1], "y", ffn_big)
    sum_qk, sum_vo = swap(sum_qk, "y"), swap(sum_vo, "x")
    d_input = after(d_input, sum_qk[-1], sum_vo[-1])
    grad_ffn = after(total(grad_ffn), sum_qk[-1], sum_vo[-1])
    grad_up, grad_down = grad_ffn[:ff_rows].T, grad_ffn[ff_rows:]
    grad_attn = scatter_z(
        lambda k: jnp.concatenate(
            [
                total([t[k] for t in sum_qk]),
                total([t[k] for t in sum_vo]),
                jnp.pad(vec_part[k], ((0, 7), (0, 0))),
            ],
            0,
        )
    )
    grad_attn = total(grad_attn)
    sum_qk, sum_vo = grad_attn[:rows], grad_attn[rows : 2 * rows]
    d_own, d_c = from_documents_c(d_input, local)
    grad_input = from_documents(d_own, d_c, from_documents_y(d_own, d_c)).astype(F32)
    grad_qkv = jnp.stack([sum_qk[:, :head_cols], sum_qk[:, head_cols:], sum_vo[:, :head_cols]])
    grad_out = sum_vo[:, head_cols:].T
    grad_vec = grad_attn[2 * rows, :vec_len]

    slots = length * layer_input.shape[1] * deep * 2
    rate = RATE_BASE / math.sqrt(slots)
    rate_out = rate * math.sqrt(LEN / 8.0)
    new_qkv, new_mom_qkv, new_avg_qkv = advance(w_qkv, grad_qkv, mom_qkv, avg_qkv, DECAY, rate)
    new_out, new_mom_out, new_avg_out = advance(w_out, grad_out, mom_out, avg_out, DECAY, rate_out)
    new_up, new_mom_up, new_avg_up = advance(w_up, grad_up, mom_up, avg_up, DECAY, rate)
    new_down, new_mom_down, new_avg_down = advance(
        w_down, grad_down, mom_down, avg_down, DECAY, rate
    )
    new_vec, new_mom_vec, new_avg_vec = advance(vectors, grad_vec, mom_vec, avg_vec, 0.0, rate)
    return (
        layer_output,
        grad_input,
        grad_qkv,
        grad_out,
        grad_up,
        grad_down,
        grad_vec,
        new_qkv,
        new_out,
        new_up,
        new_down,
        new_vec,
        new_mom_qkv,
        new_mom_out,
        new_mom_up,
        new_mom_down,
        new_mom_vec,
        new_avg_qkv,
        new_avg_out,
        new_avg_up,
        new_avg_down,
        new_avg_vec,
    )


def solution(mesh):
    dp, head = mesh.shape["dp"], mesh.shape["head"]
    fine = Mesh(mesh.devices.reshape(dp // 2, 2, head // 2, 2), ("z", "x", "y", "c"))
    dps, heads, every = ("z", "x"), ("y", "c"), ("z", "x", "y", "c")
    acts = P(heads, dps, None)
    weights = (P(None, dps, heads), P(heads, dps), P(None, every), P(every, None), P(every))
    return jax.shard_map(
        body,
        mesh=fine,
        in_specs=(acts, P(dps), acts) + weights * 3,
        out_specs=(acts, acts) + weights * 4,
        check_vma=False,
    )
```

```python
import functools
import math

import jax
import jax.numpy as jnp
from jax import lax
from jax.experimental import pallas as pl
from jax.experimental.pallas import tpu as pltpu
from jax.sharding import Mesh
from jax.sharding import PartitionSpec as P

D = 768
HD = 64
FF = 3072
LEN = 512

EPSILON = 1e-05
MOMENTUM = 0.9
AVERAGE = 0.9
DECAY = 0.01
RATE_BASE = 0.05

BF = jnp.bfloat16
F32 = jnp.float32
NT = (((1,), (1,)), ((), ()))
NN = (((1,), (0,)), ((), ()))


def send(values, axis, bit=1):
    return lax.ppermute(values, axis, [(i, i ^ bit) for i in range(lax.axis_size(axis))])


def corner(array):
    rows, columns = min(8, array.shape[-2]), min(128, array.shape[-1])
    return array.reshape(-1, *array.shape[-2:])[0, :rows, :columns]


def after(values, *others):
    zero = sum(corner(v)[0, 0].astype(F32) * 0.0 for v in jax.tree.leaves(others))
    return jax.tree.map(lambda v: v + zero.astype(v.dtype), values)


def z_order(size):
    return jnp.array([0, 2, 1, 3]) if size == 4 else jnp.arange(size)


def flip_order(axis):
    size = lax.axis_size(axis)
    return lax.axis_index(axis) ^ z_order(size)


def gather_z(shard):
    size = lax.axis_size("z")
    if size != 4:
        whole = jnp.take(lax.all_gather(shard, "z"), flip_order("z"), axis=0)
        return whole, whole[0]
    got = send(shard, "z", 2)
    pair = jnp.stack([shard, got], 0)
    return jnp.concatenate([pair, send(pair, "z", 1)], 0), got


def total(terms):
    result = terms[0].astype(F32)
    for term in terms[1:]:
        result = result + term.astype(F32)
    return result


def swap(terms, axis, others=()):
    part = total([t[1] for t in terms])
    got = send((after(part, others) if others else part).astype(BF), axis)
    return [t[0] for t in terms] + [got]


def scatter_z(sums):
    joined = lambda index: jnp.concatenate([total([t[index] for t in terms]) for terms in sums], -2)
    if lax.axis_size("z") != 4:
        everything = jnp.take(joined(slice(None)).astype(BF), flip_order("z"), axis=0)
        parts = lax.all_to_all(everything, "z", 0, 0, tiled=True)
        return [total(list(parts[1:])), parts[0]]
    got = send(joined(slice(2, 4)).astype(BF), "z", 1)
    left, start = [], 0
    for terms in sums:
        end = start + terms[0].shape[-2]
        left.append([t[:2] for t in terms] + [got[:, start:end]])
        start = end
    sums = left
    return [joined(0), send(joined(1).astype(BF), "z", 2)]


def to_documents(values):
    y, c = lax.axis_index("y"), lax.axis_index("c")
    local, _, width = values.shape
    docs = values.transpose(1, 0, 2).reshape(2, 2, local, width)
    mine = lax.dynamic_index_in_dim(docs, y, 0, keepdims=False)
    got_y = send(lax.dynamic_index_in_dim(docs, 1 - y, 0, keepdims=False), "y")
    of = lambda v, core: lax.dynamic_index_in_dim(v, core, 0, keepdims=False)
    got = send(jnp.stack([of(mine, 1 - c), of(got_y, 1 - c)], 0), "c")
    document = jnp.stack([of(mine, c), of(got_y, c), got[0], got[1]], 0)
    return document.reshape(4 * local, width), got_y


def from_documents_y(values, local):
    values = values.reshape(2, 2, local, values.shape[1])
    return values[:, 0], send(values[:, 1], "y")


def assemble_kernel(seats_ref, own_ref, got_y_ref, got_c_ref, out_ref):
    for place, ref, part in ((0, own_ref, 0), (1, got_y_ref, 0), (2, got_c_ref, 0), (3, got_c_ref, 1)):
        out_ref[seats_ref[place]] = ref[part].astype(out_ref.dtype)


def from_documents(seats, own, got_y, dtype):
    got_c = send(jnp.stack([own[1], got_y[1]], 0), "c")
    vmem = pl.BlockSpec(memory_space=pltpu.VMEM)
    docs = pl.pallas_call(
        assemble_kernel,
        in_specs=[SMEM_SPEC, vmem, vmem, vmem],
        out_specs=vmem,
        out_shape=jax.ShapeDtypeStruct((4, *own.shape[1:]), dtype),
        compiler_params=params(12),
        cost_estimate=cost(0.0, 2.0, 0.0),
        name="assemble",
    )(seats, own, got_y, got_c)
    return docs.transpose(1, 0, 2)


def dot(a, b, dims):
    return lax.dot_general(a, b, dims, preferred_element_type=F32)


def normalized(values):
    center = values - jnp.mean(values, -1, keepdims=True)
    inverse = lax.rsqrt(jnp.mean(center * center, -1, keepdims=True) + EPSILON)
    return center * inverse, inverse


def norm_backward(d_result, normed, inverse, gain):
    d_normed = d_result * gain
    return inverse * (
        d_normed
        - jnp.mean(d_normed, -1, keepdims=True)
        - normed * jnp.mean(d_normed * normed, -1, keepdims=True)
    )


def block_start(place_ref, index, rows):
    start = place_ref[index] * rows
    return pl.multiple_of(start, 32) if rows % 32 == 0 else start


def place_weights(place_ref, qk_refs, vo_refs, w_qk, w_vo, rows):
    across, deep = len(qk_refs), qk_refs[0].shape[1]

    def place(group):
        for i in range(across):
            for k in range(deep):
                start = block_start(place_ref, i * deep + k, rows)
                w_qk[pl.ds(start, rows), :] = qk_refs[i][0, k]
                w_vo[pl.ds(start, rows), :] = vo_refs[group][i, k]

    for group in range(2):
        pl.when(pl.program_id(0) == group)(functools.partial(place, group))


def accumulate(step, target, start_ref, value):
    @pl.when(step == 0)
    def _():
        target[...] = value if start_ref is None else start_ref[...] + value

    @pl.when(step > 0)
    def _():
        target[...] += value


def attention_forward_kernel(rows, last, parts, *refs):
    qk_refs, vo_refs, refs = refs[:parts], refs[parts : parts + 2], refs[parts + 2 :]
    place_ref, x_ref, bias_ref, mask_ref, vec_ref = refs[:5]
    if last:
        mix_in, qkv_ref, lse_ref, context_ref = refs[5:9]
        h_ref, hb_ref, n_ref, inv_ref, xt_ref, w_qk, w_vo, mix_ref = refs[9:]
    else:
        mix_in = None
        qkv_ref, lse_ref, context_ref, mix_ref, w_qk, w_vo = refs[5:]
    step = pl.program_id(0)
    place_weights(place_ref, qk_refs, vo_refs, w_qk, w_vo, rows)
    x = x_ref[...]
    width = w_qk.shape[1] // 2
    bias = bias_ref[0]
    qk = dot(x, w_qk[...], NN)
    v = (dot(x, w_vo[:, :width], NN) + bias[1:2, :width]).astype(BF)
    q = ((qk[:, :width] + bias[0:1, :width]).astype(BF).astype(F32) * HD ** (-0.5)).astype(BF)
    k = qk[:, width:].astype(BF)
    qkv_ref[0, :, :width] = q
    qkv_ref[0, :, width : 2 * width] = k
    qkv_ref[0, :, 2 * width :] = v
    mask = mask_ref[0:1]
    length = x.shape[0]
    contexts, logs = [], []
    for head in range(width // HD):
        cols = slice(head * HD, (head + 1) * HD)
        s = dot(q[:, cols], k[:, cols], NT) + mask
        peak = jnp.max(s, -1, keepdims=True)
        total = jnp.sum(jnp.exp(s - peak), -1, keepdims=True)
        log_total = peak + jnp.log(total)
        p = jnp.exp(s - log_total).astype(BF)
        contexts.append(dot(p, v[:, cols], NN).astype(BF))
        logs.append(log_total)
    context = jnp.concatenate(contexts, 1)
    context_ref[0] = context
    lanes = lax.broadcasted_iota(jnp.int32, (length, 128), 1)
    packed = jnp.zeros((length, 128), F32)
    for head, log_total in enumerate(logs):
        packed = jnp.where(lanes == head, log_total, packed)
    lse_ref[0] = packed.T[:8]
    accumulate(step, mix_ref, mix_in, dot(context, w_vo[:, width:], NT))
    if last:

        @pl.when(step == pl.num_programs(0) - 1)
        def _():
            first_res = x_ref[...].astype(F32) + mix_ref[...] + vec_ref[2:3]
            normed, inverse = normalized(first_res)
            hidden = normed * vec_ref[3:4] + vec_ref[4:5]
            n_ref[...] = normed
            inv_ref[...] = jnp.broadcast_to(inverse, inv_ref.shape)
            h_ref[...] = hidden
            hb_ref[...] = hidden.astype(BF)
            xt_ref[...] = x_ref[...].T


def attention_backward_kernel(rows, last, parts, *refs):
    qk_refs, vo_refs, refs = refs[:parts], refs[parts : parts + 2], refs[parts + 2 :]
    place_ref, xt_ref, gr_ref, grt_ref, qkv_ref, lse_ref, context_ref = refs[:7]
    mask_ref, start_ref = refs[7:9]
    if last:
        gqk_ref, gvo_ref, bias_ref, out_ref, w_qk, w_vo, g_qkv, gin_ref = refs[9:]
    else:
        gqk_ref, gvo_ref, bias_ref, gin_ref, w_qk, w_vo, g_qkv = refs[9:]
    step = pl.program_id(0)
    place_weights(place_ref, qk_refs, vo_refs, w_qk, w_vo, rows)
    width = w_qk.shape[1] // 2
    gc = dot(gr_ref[...], w_vo[:, width:], NN).astype(BF)
    mask = mask_ref[:, :1]
    sums = []
    for head in range(width // HD):
        q = qkv_ref[0, :, head * HD : (head + 1) * HD]
        k = qkv_ref[0, :, width + head * HD : width + (head + 1) * HD]
        v = qkv_ref[0, :, 2 * width + head * HD : 2 * width + (head + 1) * HD]
        g = gc[:, head * HD : (head + 1) * HD]
        p = jnp.exp(dot(k, q, NT) + mask - lse_ref[0, head : head + 1])
        dp = dot(v, g, NT)
        gv = dot(p.astype(BF), g, NN)
        delta = jnp.sum(p * dp, 0, keepdims=True)
        gs = (p * (dp - delta)).astype(BF)
        gk = dot(gs, q, NN)
        gq = dot(gs.T, (k.astype(F32) * HD ** (-0.5)).astype(BF), NN)
        g_qkv[:, head * HD : (head + 1) * HD] = gq.astype(BF)
        g_qkv[:, width + head * HD : width + (head + 1) * HD] = gk.astype(BF)
        g_qkv[:, 2 * width + head * HD : 2 * width + (head + 1) * HD] = gv.astype(BF)
        sums.append((jnp.sum(gq, 0, keepdims=True), jnp.sum(gv, 0, keepdims=True)))
    bias_ref[0, 0:1, :] = jnp.concatenate([s[0] for s in sums], 1)
    bias_ref[0, 1:2, :] = jnp.concatenate([s[1] for s in sums], 1)
    g_qk = g_qkv[:, : 2 * width]
    g_v = g_qkv[:, 2 * width :]
    gin = dot(g_qk, w_qk[...], NT) + dot(g_v, w_vo[:, :width], NT)
    accumulate(step, gin_ref, start_ref, gin)

    w_qk[...] = dot(xt_ref[...], g_qk, NN).astype(BF)
    w_vo[:, :width] = dot(xt_ref[...], g_v, NN).astype(BF)
    w_vo[:, width:] = dot(grt_ref[...], context_ref[0], NN).astype(BF)
    across, deep = gqk_ref.shape[0], gqk_ref.shape[2]
    for i in range(across):
        for j in range(deep):
            start = block_start(place_ref, i * deep + j, rows)
            gqk_ref[i, 0, j] = w_qk[pl.ds(start, rows), :]
            gvo_ref[0, i, j] = w_vo[pl.ds(start, rows), :]
    if last:

        @pl.when(step == pl.num_programs(0) - 1)
        def _():
            out_ref[...] = gin_ref[...].astype(BF)


def ffn_weights(refs):
    step = pl.program_id(0)
    up = jnp.where(step < 2, refs[0][...], refs[1][...])
    down = jnp.where(step % 2 == 0, refs[2][...], refs[3][...])
    return up, down


def ffn_forward_kernel(last, *refs):
    up, down = ffn_weights(refs[:4])
    h_ref, hb_ref, bias_ref, vec_ref = refs[4:8]
    if last:
        sum_in, cot_ref, mask_ref = refs[8:11]
        act_ref, slope_ref, out_ref, gr_ref, grb_ref, vec_out, sum_ref = refs[11:]
    else:
        sum_in = None
        act_ref, slope_ref, sum_ref = refs[8:]
    step = pl.program_id(0)
    u = dot(hb_ref[...], up, NT) + bias_ref[0:1]
    phi = 0.5 + 0.5 * lax.erf(u * 0.7071067811865476)
    act = (u * phi).astype(BF)
    act_ref[...] = act
    slope_ref[...] = phi + u * jnp.exp(-0.5 * u * u) * 0.3989422804014327
    accumulate(step, sum_ref, sum_in, dot(act, down, NN))
    if last:

        @pl.when(step == pl.num_programs(0) - 1)
        def _():
            second_res = h_ref[...] + (sum_ref[...] + vec_ref[9:10])
            normed, inverse = normalized(second_res)
            out_ref[...] = (normed * vec_ref[10:11] + vec_ref[11:12]).astype(BF)
            d_result = jnp.where(mask_ref[:, :1] == 0.0, cot_ref[...].astype(F32), 0.0)
            vec_out[0:1] = jnp.sum(d_result * normed, 0, keepdims=True)
            vec_out[1:2] = jnp.sum(d_result, 0, keepdims=True)
            d_second = norm_backward(d_result, normed, inverse, vec_ref[10:11])
            vec_out[2:3] = jnp.sum(d_second, 0, keepdims=True)
            gr_ref[...] = d_second
            grb_ref[...] = d_second.astype(BF)


def ffn_backward_kernel(last, *refs):
    up, down = ffn_weights(refs[:4])
    grb_ref, hb_ref, act_ref, slope_ref, sum_in = refs[4:9]
    if last:
        n_ref, inv_ref, vec_ref = refs[9:12]
        gu_ref, gd_ref, bias_ref, gr_ref, gr1b_ref, grt_ref, vec_out, sum_ref = refs[12:]
    else:
        gu_ref, gd_ref, bias_ref, sum_ref = refs[9:]
    step = pl.program_id(0)
    grb = grb_ref[...]
    d_up = dot(grb, down, NT) * slope_ref[...]
    bias_ref[0:1] = jnp.sum(d_up, 0, keepdims=True)
    d_up_b = d_up.astype(BF)
    gd_ref[...] = dot(act_ref[...].T, grb, NN).astype(BF)
    gu_ref[...] = dot(d_up_b.T, hb_ref[...], NN).astype(BF)
    accumulate(step, sum_ref, sum_in, dot(d_up_b, up, NN))
    if last:

        @pl.when(step == pl.num_programs(0) - 1)
        def _():
            d_hidden = sum_ref[...]
            normed = n_ref[...]
            vec_out[0:1] = jnp.sum(d_hidden * normed, 0, keepdims=True)
            vec_out[1:2] = jnp.sum(d_hidden, 0, keepdims=True)
            d_first = norm_backward(d_hidden, normed, inv_ref[:, :1], vec_ref[3:4])
            vec_out[2:3] = jnp.sum(d_first, 0, keepdims=True)
            gr_ref[...] = d_first
            gr1b_ref[...] = d_first.astype(BF)
            grt_ref[...] = d_first.astype(BF).T


def whole(array):
    shape = array.shape
    return pl.BlockSpec(shape, lambda g: (0,) * len(shape))


def per_group(array):
    rest = array.shape[1:]
    return pl.BlockSpec((1, *rest), lambda g: (g, *(0 for _ in rest)))


def per_corner(array, rows, dim):
    block = [*array.shape[:3], rows, array.shape[4]]
    block[dim] = 1
    return pl.BlockSpec(tuple(block), lambda g: (0, g, 0, 0, 0) if dim else (g, 0, 0, 0, 0))


def per_rows(array, size, crossed):
    if crossed:
        return pl.BlockSpec((size, array.shape[1]), lambda g: (g % 2 * 2 + g // 2, 0))
    return pl.BlockSpec((size, array.shape[1]), lambda g: (g, 0))


def per_columns(array, size):
    return pl.BlockSpec((array.shape[0], size), lambda g: (0, g))


def spread_vectors_kernel(owner_ref, heads_ref, pieces_ref, rows_ref, up_ref, bias_ref, units):
    _, across, _, deep = COUNTS
    unit = units.shape[1]
    for x in range(2):
        for y in range(2):
            for z in range(deep):
                for c in range(2):
                    index = ((c * across + x) * 2 + y) * deep + z
                    start = owner_ref[index] * 3
                    for i in range(3):
                        units[pl.ds(start + i, 1), :] = pieces_ref[
                            x, y, z, c : c + 1, i * unit : (i + 1) * unit
                        ]
    per_row = D // unit
    for row in range(12):
        for i in range(per_row):
            rows_ref[row : row + 1, i * unit : (i + 1) * unit] = units[
                row * per_row + i : row * per_row + i + 1, :
            ]
    half = FF // 2
    for index in range(FF // unit):
        start = index * unit
        up_ref[start // half, 0:1, start % half : start % half + unit] = units[
            pl.ds(5 * per_row + owner_ref[index], 1), :
        ]
    width = bias_ref.shape[2]
    for group in range(4):
        for kind in range(2):
            for i in range(width // unit):
                start = kind * per_row + heads_ref[group] * (width // unit) + i
                bias_ref[group, kind : kind + 1, i * unit : (i + 1) * unit] = units[
                    pl.ds(start, 1), :
                ]


def collect_vectors_kernel(
    owner_ref, heads_ref, bias_0, bias_1, up_0, up_1, one_ref, two_ref, out_ref, units
):
    out_ref[...] = jnp.zeros(out_ref.shape, F32)
    unit = units.shape[1]
    per_row = D // unit
    width = bias_0.shape[2]
    for group in range(4):
        source = (bias_0, bias_1)[group // 2]
        for kind in range(2):
            for i in range(width // unit):
                start = kind * per_row + heads_ref[group] * (width // unit) + i
                units[pl.ds(start, 1), :] = source[
                    group % 2, kind : kind + 1, i * unit : (i + 1) * unit
                ]
    half = FF // 2
    for index in range(FF // unit):
        source = (up_0, up_1)[index * unit // half]
        start = index * unit % half
        units[pl.ds(5 * per_row + owner_ref[index], 1), :] = source[0:1, start : start + unit]
    for row, source, line in (
        (2, one_ref, 2),
        (3, one_ref, 0),
        (4, one_ref, 1),
        (9, two_ref, 2),
        (10, two_ref, 0),
        (11, two_ref, 1),
    ):
        for i in range(per_row):
            units[row * per_row + i : row * per_row + i + 1, :] = source[
                line : line + 1, i * unit : (i + 1) * unit
            ]
    for index in range(FF // unit):
        for i in range(3):
            out_ref[index, 0:1, i * unit : (i + 1) * unit] = units[
                pl.ds(owner_ref[index] * 3 + i, 1), :
            ]


COUNTS = (2, 2, 2, 4)


def spread_vectors(owner, heads, pieces, unit, width):
    outs = [like((12, D), F32), like((2, 8, FF // 2), F32), like((4, 8, width), F32)]
    return pl.pallas_call(
        spread_vectors_kernel,
        in_specs=[SMEM_SPEC, SMEM_SPEC, pl.BlockSpec(memory_space=pltpu.VMEM)],
        out_specs=[pl.BlockSpec(memory_space=pltpu.VMEM)] * 3,
        out_shape=outs,
        scratch_shapes=[pltpu.VMEM((12 * D // unit, unit), F32)],
        compiler_params=params(8),
        cost_estimate=cost(0.0, 0.5, 0.0),
        name="spread_vectors",
    )(owner, heads, pieces)


def collect_vectors(owner, heads, unit, pair, *sources):
    return pl.pallas_call(
        collect_vectors_kernel,
        in_specs=[SMEM_SPEC, SMEM_SPEC] + [pl.BlockSpec(memory_space=pltpu.VMEM)] * len(sources),
        out_specs=pl.BlockSpec(memory_space=pltpu.VMEM),
        out_shape=like((FF // unit, 8, pair), F32),
        scratch_shapes=[pltpu.VMEM((12 * D // unit, unit), F32)],
        compiler_params=params(8),
        cost_estimate=cost(0.0, 0.5, 0.0),
        name="collect_vectors",
    )(owner, heads, *sources)


def advance_attention_kernel(rates, *refs):
    terms, olds, outs = refs[:2], refs[2:8], refs[8:]
    whole_sum = terms[0][...]
    for term in terms[1:]:
        whole_sum = whole_sum + term[...].astype(F32)
    rows, width = olds[0].shape[1], olds[0].shape[2]
    parts = [
        whole_sum[:rows, :width],
        whole_sum[:rows, width:],
        whole_sum[rows + 8 :, :width],
    ]
    for i, grad in enumerate(parts):
        new = advance(olds[0][i], grad, olds[1][i], olds[2][i], DECAY, rates[0])
        for ref, value in zip(outs[:4], (grad, *new)):
            ref[i] = value
    grad = whole_sum[rows + 8 :, width:].T
    new = advance(olds[3][...], grad, olds[4][...], olds[5][...], DECAY, rates[1])
    for ref, value in zip(outs[4:8], (grad, *new)):
        ref[...] = value
    outs[8][...] = whole_sum[rows : rows + 8]


def advance_attention(terms, qkv, out, rates):
    outs = [like(qkv[0].shape, F32)] * 4 + [like(out[0].shape, F32)] * 4
    outs.append(like((8, terms[0].shape[1]), F32))
    vmem = pl.BlockSpec(memory_space=pltpu.VMEM)
    return pl.pallas_call(
        functools.partial(advance_attention_kernel, rates),
        in_specs=[vmem] * 8,
        out_specs=[vmem] * 9,
        out_shape=outs,
        compiler_params=params(16),
        cost_estimate=cost(0.0, 3.0, 0.0),
        name="advance_attention",
    )(*terms, *qkv, *out)


def waiting(kernel, others):
    corners = [corner(v) for v in jax.tree.leaves(others)]
    count = len(corners)
    return lambda *refs: kernel(*refs[count:]), corners, [whole(v) for v in corners]


SMEM_SPEC = pl.BlockSpec(memory_space=pltpu.SMEM)
like = jax.ShapeDtypeStruct


def per_part(array, size, by_x):
    return pl.BlockSpec((size, array.shape[1]), lambda g: (g // 2 if by_x else g % 2, 0))


def attention_weights(weights, rows):
    parts_qk, parts_vo = weights
    specs = []
    for part in parts_qk:
        block = (1, part.shape[1], rows, part.shape[3])
        specs.append(pl.BlockSpec(block, lambda g: (g, 0, 0, 0)))
    for part in parts_vo:
        block = (*part.shape[:2], rows, part.shape[3])
        specs.append(pl.BlockSpec(block, lambda g: (0, 0, 0, 0)))
    return [*parts_qk, *parts_vo], specs


def params(mib):
    return pltpu.CompilerParams(vmem_limit_bytes=mib << 20)


def cost(giga_flops, mega_bytes, mega_exps):
    return pl.CostEstimate(
        flops=int(giga_flops * 1e9),
        bytes_accessed=int(mega_bytes * 1e6),
        transcendentals=int(mega_exps * 1e6),
    )


def attention_forward(place, x, weights, biases, half, mask, vec_rows, mix, rows):
    length = x.shape[0]
    pair = weights[0][0].shape[3]
    width = pair // 2
    last = mix is not None
    row = like((length, D), F32)
    outs = [
        like((2, length, 3 * width), BF),
        like((2, 8, length), F32),
        like((2, length, width), BF),
    ]
    tail = [row]
    scratch = [pltpu.VMEM((D, pair), BF), pltpu.VMEM((D, pair), BF)]
    operands, specs = attention_weights(weights, rows)
    operands += [place, x, biases, mask, vec_rows]
    specs += [
        SMEM_SPEC,
        whole(x),
        pl.BlockSpec((1, *biases.shape[1:]), lambda g: (half * 2 + g, 0, 0)),
        whole(mask),
        whole(vec_rows),
    ]
    if last:
        low = like((length, D), BF)
        tail = [row, low, row, like((length, 128), F32), like((D, length), BF)]
        operands.append(mix)
        specs.append(whole(mix))
        scratch.append(pltpu.VMEM((length, D), F32))
    return pl.pallas_call(
        functools.partial(attention_forward_kernel, rows, last, len(weights[0])),
        grid=(2,),
        in_specs=specs,
        out_specs=[per_group(o) for o in outs] + [whole(o) for o in tail],
        out_shape=outs + tail,
        scratch_shapes=scratch,
        compiler_params=params(18),
        cost_estimate=cost(4.5, 6.0, 3.1),
        name="attention_forward_last" if last else "attention_forward",
    )(*operands)


def attention_backward(place, x_t, gr, gr_t, weights, saved, mask, start, rows, last, others):
    length = gr.shape[0]
    pair = weights[0][0].shape[3]
    width = pair // 2
    across = len(weights[0])
    deep = weights[0][0].shape[1]
    qkv, lse, context = saved
    grad_qk = like((across, 2, deep, rows, pair), BF)
    grad_vo = like((2, across, deep, rows, pair), BF)
    outs = [
        grad_qk,
        grad_vo,
        like((2, 8, width), F32),
        like((length, D), BF if last else F32),
    ]
    scratch = [
        pltpu.VMEM((D, pair), BF),
        pltpu.VMEM((D, pair), BF),
        pltpu.VMEM((length, 3 * width), BF),
    ]
    if last:
        scratch.append(pltpu.VMEM((length, D), F32))
    operands, specs = attention_weights(weights, rows)
    kernel = functools.partial(attention_backward_kernel, rows, last, across)
    kernel, corners, corner_specs = waiting(kernel, others)
    return pl.pallas_call(
        kernel,
        grid=(2,),
        in_specs=corner_specs
        + specs
        + [
            SMEM_SPEC,
            whole(x_t),
            whole(gr),
            whole(gr_t),
            per_group(qkv),
            per_group(lse),
            per_group(context),
            whole(mask),
            whole(start),
        ],
        out_specs=[
            per_corner(grad_qk, rows, 1),
            per_corner(grad_vo, rows, 0),
            per_group(outs[2]),
            whole(outs[3]),
        ],
        out_shape=outs,
        scratch_shapes=scratch,
        compiler_params=params(18),
        cost_estimate=cost(0.5, 1.0, 0.1),
        name="attention_backward_last" if last else "attention_backward",
    )(*corners, *operands, place, x_t, gr, gr_t, qkv, lse, context, mask, start)


def ffn_operands(up, down):
    chunk = up[0].shape[0] // 2
    specs = [per_part(u, chunk, False) for u in up] + [per_part(d, chunk, True) for d in down]
    return [*up, *down], specs, chunk


def ffn_forward(h, hb, up, down, bias, vec_rows, tail_operands):
    length = h.shape[0]
    operands, specs, chunk = ffn_operands(up, down)
    hidden = 4 * chunk
    last = len(tail_operands) > 0
    row = like((length, D), F32)
    outs = [like((length, hidden), BF), like((length, hidden), F32)]
    tail = [row]
    scratch = []
    if last:
        low = like((length, D), BF)
        tail = [low, row, low, like((8, D), F32)]
        scratch = [pltpu.VMEM((length, D), F32)]
    return pl.pallas_call(
        functools.partial(ffn_forward_kernel, last),
        grid=(4,),
        in_specs=specs
        + [whole(h), whole(hb), per_columns(bias, chunk), whole(vec_rows)]
        + [whole(t) for t in tail_operands],
        out_specs=[per_columns(o, chunk) for o in outs] + [whole(o) for o in tail],
        out_shape=outs + tail,
        scratch_shapes=scratch,
        compiler_params=params(18),
        cost_estimate=cost(4.9, 12.0, 1.6),
        name="ffn_forward_last" if last else "ffn_forward",
    )(*operands, h, hb, bias, vec_rows, *tail_operands)


def ffn_backward(grb, hb, act, slope, up, down, total, tail_operands, others):
    length = grb.shape[0]
    operands, specs, chunk = ffn_operands(up, down)
    hidden = 4 * chunk
    last = len(tail_operands) > 0
    row = like((length, D), F32)
    grad = like((hidden, D), BF)
    outs = [grad, grad, like((8, hidden), F32)]
    tail = [row]
    scratch = []
    if last:
        tail = [row, like((length, D), BF), like((D, length), BF), like((8, D), F32)]
        scratch = [pltpu.VMEM((length, D), F32)]
    kernel, corners, corner_specs = waiting(functools.partial(ffn_backward_kernel, last), others)
    return pl.pallas_call(
        kernel,
        grid=(4,),
        in_specs=corner_specs
        + specs
        + [whole(grb), whole(hb), per_columns(act, chunk), per_columns(slope, chunk)]
        + [whole(total)]
        + [whole(t) for t in tail_operands],
        out_specs=[
            per_rows(grad, chunk, False),
            per_rows(grad, chunk, True),
            per_columns(outs[2], chunk),
        ]
        + [whole(o) for o in tail],
        out_shape=outs + tail,
        scratch_shapes=scratch,
        compiler_params=params(18),
        cost_estimate=cost(9.7, 16.0, 0.0),
        name="ffn_backward_last" if last else "ffn_backward",
    )(*corners, *operands, grb, hb, act, slope, total, *tail_operands)


def advance(weight, grad, moment, average, decay, rate):
    step_grad = grad + decay * weight
    moment_new = MOMENTUM * moment + step_grad
    weight_new = weight - rate * (step_grad + MOMENTUM * moment_new)
    average_new = AVERAGE * average + (1.0 - AVERAGE) * weight_new
    return (weight_new, moment_new, average_new)


def body(
    layer_input,
    lengths,
    cotangent,
    w_qkv,
    w_out,
    w_up,
    w_down,
    vectors,
    mom_qkv,
    mom_out,
    mom_up,
    mom_down,
    mom_vec,
    avg_qkv,
    avg_out,
    avg_up,
    avg_down,
    avg_vec,
):
    z, x, y, c = (lax.axis_index(a) for a in ("z", "x", "y", "c"))
    deep = lax.axis_size("z")
    blocks = deep * 8
    rows, head_cols = w_qkv.shape[1], w_qkv.shape[2]
    pair = 2 * head_cols
    vec_len = vectors.shape[0]
    ff_rows = w_up.shape[1]
    local = layer_input.shape[0]
    length = 4 * local

    kc, kx, ky, kz = jnp.meshgrid(
        jnp.arange(2), jnp.arange(2), jnp.arange(2), z_order(deep), indexing="ij"
    )
    owner = (((z ^ kz) * 2 + (x ^ kx)) * 4 + (y ^ ky) * 2 + (c ^ kc)).reshape(blocks)
    tz, tx, ty, tc = jnp.meshgrid(
        jnp.arange(deep), jnp.arange(2), jnp.arange(2), jnp.arange(2), indexing="ij"
    )
    seat = ((((c ^ tc) * 2 + (x ^ tx)) * 2 + (y ^ ty)) * deep + z_order(deep)[z ^ tz]).reshape(blocks)
    first, second = jnp.meshgrid(jnp.arange(2), jnp.arange(2), indexing="ij")
    group_head = ((y ^ second) * 2 + (c ^ first)).reshape(4)
    head_group = ((c ^ second) * 2 + (y ^ first)).reshape(4)

    in_kernel = rows % 32 == 0 and deep == COUNTS[3]
    owner, group_head = owner.astype(jnp.int32), group_head.astype(jnp.int32)

    vec_row = jnp.pad(vectors.astype(BF), (0, pair - vec_len))[None]
    vec_rows = jnp.pad(jnp.concatenate([vec_row, send(vec_row, "c")], 0), ((0, 6), (0, 0)))
    pack_qk = jnp.concatenate([w_qkv[0], w_qkv[1]], 1).astype(BF)
    pack_vo = jnp.concatenate([w_qkv[2], w_out.T], 1).astype(BF)
    pack = jnp.concatenate([pack_qk, vec_rows, pack_vo], 0)
    doc_x, x_y = to_documents(after(layer_input, vec_rows))
    doc_cot, cot_y = to_documents(after(cotangent, vec_rows))
    attn_z, z_first = gather_z(pack)
    qk, vo = attn_z[:, : rows + 8], attn_z[:, rows + 8 :]
    qk_first, vo_first = send(qk, "y"), send(vo, "x")
    qk = after(jnp.stack([qk, qk_first], 0), vo_first, x_y, cot_y)
    vo = after(jnp.stack([vo, vo_first], 0), qk_first)
    qk_got, vo_got = send(qk, "x"), send(vo, "y")
    attn_own = ((qk, qk_got), (vo, vo_got))
    attn_other = jax.tree.map(lambda v: send(v, "c"), attn_own)

    pack = jnp.concatenate([w_up.T.astype(BF), w_down.astype(BF)], 0)
    ffn_z, _ = gather_z(after(pack, z_first))
    first_got = (qk_first, vo_first)
    up, down = after((ffn_z[:, :ff_rows], ffn_z[:, ff_rows:]), first_got)
    up_got, down_got = send(up, "y"), send(down, "x")
    up, down = (
        after(jnp.stack([up, up_got], 0), down_got, qk_got, vo_got),
        after(jnp.stack([down, down_got], 0), up_got, qk_got, vo_got),
    )
    up_got, down_got = send(up, "x"), send(down, "y")

    pieces = jnp.stack([qk[..., rows:, :], qk_got[..., rows:, :]], 0).astype(F32)
    if in_kernel:
        vec_rows, bias_up, biases = spread_vectors(owner, group_head, pieces, ff_rows, head_cols)
    else:
        vec_all = jnp.moveaxis(pieces[..., :2, :vec_len], -2, 0).reshape(blocks, vec_len)
        vec_rows = jnp.take(vec_all, seat, axis=0).reshape(12, D)
        bias_up = jnp.take(vec_rows[5:9].reshape(blocks, ff_rows), owner, axis=0)
        bias_up = jnp.pad(bias_up.reshape(2, 1, FF // 2), ((0, 0), (0, 7), (0, 0)))
        bias_q = jnp.take(vec_rows[0].reshape(4, head_cols), group_head, axis=0)
        bias_v = jnp.take(vec_rows[1].reshape(4, head_cols), group_head, axis=0)
        biases = jnp.pad(jnp.stack([bias_q, bias_v], 1), ((0, 0), (0, 6), (0, 0)))

    row = jnp.arange(length)
    part = row // local
    position = ((y ^ (part % 2)) * 2 + (c ^ (part // 2))) * local + row % local
    doc_len = lax.dynamic_index_in_dim(lengths, y * 2 + c, 0, keepdims=False)
    alive = position < doc_len
    mask = jnp.where(alive, 0.0, -1e30).astype(F32)
    mask_row = jnp.broadcast_to(mask[None, :], (8, length))
    mask_col = jnp.broadcast_to(mask[:, None], (length, 128))

    if in_kernel:
        zs = flip_order("z")[None, :]
        place = (zs * 2 + (x ^ jnp.arange(2)[:, None])).reshape(2 * deep)
        kernel_rows = rows
    else:
        xs = x ^ jnp.arange(2)
        zs = flip_order("z")

        def true_order(weights):
            qk, vo = (jnp.stack(parts, 0)[..., :rows, :] for parts in weights)
            qk = jnp.take(jnp.take(qk, xs, axis=0), zs, axis=2).transpose(1, 2, 0, 3, 4)
            vo = jnp.take(jnp.take(vo, xs, axis=1), zs, axis=2).transpose(0, 2, 1, 3, 4)
            qk, vo = qk.reshape(2, 1, D, pair), vo.reshape(2, 1, 1, D, pair)
            return ((qk,), (vo[0], vo[1]))

        def relative_order(qk, vo):
            qk = qk.reshape(2, deep, 2, rows, pair).transpose(2, 0, 1, 3, 4)
            vo = vo.reshape(2, deep, 2, rows, pair).transpose(0, 2, 1, 3, 4)
            qk = jnp.take(jnp.take(qk, xs, axis=0), zs, axis=2)
            return qk, jnp.take(jnp.take(vo, xs, axis=1), zs, axis=2)

        place = jnp.zeros((1,), jnp.int32)
        attn_own, attn_other = true_order(attn_own), true_order(attn_other)
        kernel_rows = D
    place = place.astype(jnp.int32)

    *saved_0, mix = attention_forward(
        place, doc_x, attn_own, biases, 0, mask_row, vec_rows, None, kernel_rows
    )
    *saved_1, hidden, hidden_b, normed, inverse, x_t = attention_forward(
        place, doc_x, attn_other, biases, 1, mask_row, vec_rows, mix, kernel_rows
    )
    flat = lambda v: v.reshape(FF // 4, D)
    up_own, down_own = (flat(up), flat(up_got)), (flat(down), flat(down_got))
    up_other = (send(up_own[0], "c"), send(after(up_own[1], hidden_b), "c"))
    down_other = (send(down_own[0], "c"), send(after(down_own[1], hidden_b), "c"))
    act_0, slope_0, mix = ffn_forward(
        hidden, hidden_b, up_own, down_own, bias_up[0], vec_rows, ()
    )
    act_1, slope_1, result, d_second, d_second_b, vec_two = ffn_forward(
        hidden, hidden_b, up_other, down_other, bias_up[1], vec_rows, (mix, doc_cot, mask_col)
    )
    out_own, out_y = from_documents_y(result, local)

    lead = (2, 2, deep, ff_rows, D)
    up_1, down_1, d_bias_1, d_hidden = ffn_backward(
        d_second_b, hidden_b, act_1, slope_1, up_other, down_other, d_second, (), ()
    )
    up_1, down_1 = send(up_1, "c"), send(down_1, "c")
    up_0, down_0, d_bias_0, d_first, d_first_b, d_first_t, vec_one = ffn_backward(
        d_second_b,
        hidden_b,
        act_0,
        slope_0,
        up_own,
        down_own,
        d_hidden,
        (normed, inverse, vec_rows),
        (out_y,),
    )
    grad_up = swap([up_0.reshape(lead), up_1.reshape(lead)], "x")
    grad_down = swap([down_0.reshape(lead), down_1.reshape(lead)], "y")
    ffn_c = (up_1, down_1)
    ffn_big = (grad_up[-1], grad_down[-1])
    grad_up, grad_down = swap(grad_up, "y"), swap(grad_down, "x")
    ffn_second = (grad_up[-1], grad_down[-1])
    grad_ffn = scatter_z([grad_up, grad_down])

    qk_1, vo_1, bias_1, d_attn = attention_backward(
        place, x_t, d_first_b, d_first_t, attn_other, saved_1, mask_col, d_first, kernel_rows, False, ffn_c
    )
    qk_0, vo_0, bias_0, d_input = attention_backward(
        place, x_t, d_first_b, d_first_t, attn_own, saved_0, mask_col, d_attn, kernel_rows, True, ()
    )
    if not in_kernel:
        qk_1, vo_1 = relative_order(qk_1, vo_1)
        qk_0, vo_0 = relative_order(qk_0, vo_0)
    qk_1, vo_1 = send(qk_1, "c"), send(vo_1, "c")

    bias_0 = after(bias_0, ffn_big)
    if in_kernel:
        vec_part = collect_vectors(
            owner, group_head, ff_rows, pair, bias_0, bias_1, d_bias_0, d_bias_1, vec_one, vec_two
        ).reshape(2, 2, 2, deep, 8, pair)
    else:
        d_bias = jnp.concatenate([bias_0, bias_1], 0)
        d_bias_q = jnp.take(d_bias[:, 0], head_group, axis=0).reshape(D)
        d_bias_v = jnp.take(d_bias[:, 1], head_group, axis=0).reshape(D)
        d_bias_up = jnp.concatenate([d_bias_0[0], d_bias_1[0]]).reshape(blocks, ff_rows)
        d_bias_up = jnp.take(d_bias_up, seat, axis=0).reshape(FF)
        grad_vec = jnp.concatenate(
            [
                d_bias_q,
                d_bias_v,
                vec_one[2],
                vec_one[0],
                vec_one[1],
                d_bias_up,
                vec_two[2],
                vec_two[0],
                vec_two[1],
            ]
        )
        vec_part = jnp.take(grad_vec.reshape(blocks, vec_len), owner, axis=0)
        vec_part = jnp.pad(vec_part, ((0, 0), (0, pair - vec_len))).reshape(2, 2, 2, deep, 1, pair)
        vec_part = jnp.pad(vec_part, ((0, 0),) * 4 + ((0, 7), (0, 0)))
    vec_part = vec_part[0] + send(vec_part[1], "c")
    sum_qk, vec_terms, sum_vo = [qk_0, qk_1], [vec_part], [vo_0, vo_1]
    for axis_qk, axis_vo in (("x", "y"), ("y", "x")):
        part = jnp.concatenate(
            [total([t[1] for t in sum_qk]), total([t[1] for t in vec_terms])], -2
        )
        got = send(after(part, ffn_second).astype(BF), axis_qk)
        sum_qk = [t[0] for t in sum_qk] + [got[..., :rows, :]]
        vec_terms = [t[0] for t in vec_terms] + [got[..., rows:, :]]
        sum_vo = swap(sum_vo, axis_vo, ffn_second)
    d_input = after(d_input, got, sum_vo[-1])
    grad_ffn = after(total(grad_ffn), got, sum_vo[-1])
    grad_up, grad_down = grad_ffn[:ff_rows].T, grad_ffn[ff_rows:]
    grad_attn = scatter_z([sum_qk, vec_terms, sum_vo])
    layer_output = from_documents(group_head, after(out_own, grad_ffn), out_y, BF)
    grad_input = from_documents(group_head, *from_documents_y(d_input, local), F32)

    slots = length * layer_input.shape[1] * deep * 2
    rate = RATE_BASE / math.sqrt(slots)
    rate_out = rate * math.sqrt(LEN / 8.0)
    olds_qkv, olds_out = (w_qkv, mom_qkv, avg_qkv), (w_out, mom_out, avg_out)
    if in_kernel:
        (
            grad_qkv,
            new_qkv,
            new_mom_qkv,
            new_avg_qkv,
            grad_out,
            new_out,
            new_mom_out,
            new_avg_out,
            grad_vec,
        ) = advance_attention(grad_attn, olds_qkv, olds_out, (rate, rate_out))
        grad_vec = grad_vec[0, :vec_len]
    else:
        grad_attn = total(grad_attn)
        sum_qk, sum_vo = grad_attn[:rows], grad_attn[rows + 8 :]
        grad_qkv = jnp.stack([sum_qk[:, :head_cols], sum_qk[:, head_cols:], sum_vo[:, :head_cols]])
        grad_out = sum_vo[:, head_cols:].T
        grad_vec = grad_attn[rows, :vec_len]
        new_qkv, new_mom_qkv, new_avg_qkv = advance(
            w_qkv, grad_qkv, mom_qkv, avg_qkv, DECAY, rate
        )
        new_out, new_mom_out, new_avg_out = advance(
            w_out, grad_out, mom_out, avg_out, DECAY, rate_out
        )
    new_up, new_mom_up, new_avg_up = advance(w_up, grad_up, mom_up, avg_up, DECAY, rate)
    new_down, new_mom_down, new_avg_down = advance(
        w_down, grad_down, mom_down, avg_down, DECAY, rate
    )
    new_vec, new_mom_vec, new_avg_vec = advance(vectors, grad_vec, mom_vec, avg_vec, 0.0, rate)
    return (
        layer_output,
        grad_input,
        grad_qkv,
        grad_out,
        grad_up,
        grad_down,
        grad_vec,
        new_qkv,
        new_out,
        new_up,
        new_down,
        new_vec,
        new_mom_qkv,
        new_mom_out,
        new_mom_up,
        new_mom_down,
        new_mom_vec,
        new_avg_qkv,
        new_avg_out,
        new_avg_up,
        new_avg_down,
        new_avg_vec,
    )


def solution(mesh):
    dp, head = mesh.shape["dp"], mesh.shape["head"]
    fine = Mesh(mesh.devices.reshape(dp // 2, 2, head // 2, 2), ("z", "x", "y", "c"))
    dps, heads, every = ("z", "x"), ("y", "c"), ("z", "x", "y", "c")
    acts = P(heads, dps, None)
    weights = (P(None, dps, heads), P(heads, dps), P(None, every), P(every, None), P(every))
    return jax.shard_map(
        body,
        mesh=fine,
        in_specs=(acts, P(dps), acts) + weights * 3,
        out_specs=(acts, acts) + weights * 4,
        check_vma=False,
    )
```

```python
import functools
import math

import jax
import jax.numpy as jnp
from jax import lax
from jax.experimental import pallas as pl
from jax.experimental.pallas import tpu as pltpu
from jax.sharding import Mesh
from jax.sharding import PartitionSpec as P

D = 768
HD = 64
FF = 3072
LEN = 512

EPSILON = 1e-05
MOMENTUM = 0.9
AVERAGE = 0.9
DECAY = 0.01
RATE_BASE = 0.05

BF = jnp.bfloat16
F32 = jnp.float32
NT = (((1,), (1,)), ((), ()))
NN = (((1,), (0,)), ((), ()))


def send(values, axis, bit=1):
    return lax.ppermute(values, axis, [(i, i ^ bit) for i in range(lax.axis_size(axis))])


def corner(array):
    rows, columns = min(8, array.shape[-2]), min(128, array.shape[-1])
    return array.reshape(-1, *array.shape[-2:])[0, :rows, :columns]


def after(values, *others):
    zero = sum(corner(v)[0, 0].astype(F32) * 0.0 for v in jax.tree.leaves(others))
    return jax.tree.map(lambda v: v + zero.astype(v.dtype), values)


def z_order(size):
    return jnp.array([0, 2, 1, 3]) if size == 4 else jnp.arange(size)


def flip_order(axis):
    size = lax.axis_size(axis)
    return lax.axis_index(axis) ^ z_order(size)


def gather_z(shard):
    size = lax.axis_size("z")
    if size != 4:
        whole = jnp.take(lax.all_gather(shard, "z"), flip_order("z"), axis=0)
        return whole, whole[0]
    got = send(shard, "z", 2)
    pair = jnp.stack([shard, got], 0)
    return jnp.concatenate([pair, send(pair, "z", 1)], 0), got


def total(terms):
    result = terms[0].astype(F32)
    for term in terms[1:]:
        result = result + term.astype(F32)
    return result


def swap(terms, axis, others=()):
    part = total([t[1] for t in terms])
    got = send((after(part, others) if others else part).astype(BF), axis)
    return [t[0] for t in terms] + [got]


def scatter_z(sums, direct):
    joined = lambda index: jnp.concatenate([total([t[index] for t in terms]) for terms in sums], -2)
    if lax.axis_size("z") != 4:
        everything = jnp.take(joined(slice(None)).astype(BF), flip_order("z"), axis=0)
        parts = lax.all_to_all(everything, "z", 0, 0, tiled=True)
        return [total(list(parts[1:])), parts[0]], parts[0]
    if direct:
        parts = [joined(place).astype(BF) for place in (1, 2, 3)]
        return [joined(0)] + [send(part, "z", bit) for part, bit in zip(parts, (2, 1, 3))], parts[2]
    got = send(joined(slice(2, 4)).astype(BF), "z", 1)
    left, start = [], 0
    for terms in sums:
        end = start + terms[0].shape[-2]
        left.append([t[:2] for t in terms] + [got[:, start:end]])
        start = end
    sums = left
    part = joined(1).astype(BF)
    return [joined(0), send(part, "z", 2)], part


def to_documents(values):
    y, c = lax.axis_index("y"), lax.axis_index("c")
    local, _, width = values.shape
    docs = values.transpose(1, 0, 2).reshape(2, 2, local, width)
    mine = lax.dynamic_index_in_dim(docs, y, 0, keepdims=False)
    got_y = send(lax.dynamic_index_in_dim(docs, 1 - y, 0, keepdims=False), "y")
    of = lambda v, core: lax.dynamic_index_in_dim(v, core, 0, keepdims=False)
    got = send(jnp.stack([of(mine, 1 - c), of(got_y, 1 - c)], 0), "c")
    document = jnp.stack([of(mine, c), of(got_y, c), got[0], got[1]], 0)
    return document.reshape(4 * local, width), got_y


def from_documents_y(values, local):
    values = values.reshape(2, 2, local, values.shape[1])
    return values[:, 0], send(values[:, 1], "y")


def assemble_kernel(seats_ref, own_ref, got_y_ref, got_c_ref, out_ref):
    for place, ref, part in ((0, own_ref, 0), (1, got_y_ref, 0), (2, got_c_ref, 0), (3, got_c_ref, 1)):
        out_ref[seats_ref[place]] = ref[part].astype(out_ref.dtype)


def from_documents(seats, own, got_y, dtype):
    got_c = send(jnp.stack([own[1], got_y[1]], 0), "c")
    vmem = pl.BlockSpec(memory_space=pltpu.VMEM)
    docs = pl.pallas_call(
        assemble_kernel,
        in_specs=[SMEM_SPEC, vmem, vmem, vmem],
        out_specs=vmem,
        out_shape=jax.ShapeDtypeStruct((4, *own.shape[1:]), dtype),
        compiler_params=params(12),
        cost_estimate=cost(0.0, 2.0, 0.0),
        name="assemble",
    )(seats, own, got_y, got_c)
    return docs.transpose(1, 0, 2)


def dot(a, b, dims):
    return lax.dot_general(a, b, dims, preferred_element_type=F32)


def normalized(values):
    center = values - jnp.mean(values, -1, keepdims=True)
    inverse = lax.rsqrt(jnp.mean(center * center, -1, keepdims=True) + EPSILON)
    return center * inverse, inverse


def norm_backward(d_result, normed, inverse, gain):
    d_normed = d_result * gain
    return inverse * (
        d_normed
        - jnp.mean(d_normed, -1, keepdims=True)
        - normed * jnp.mean(d_normed * normed, -1, keepdims=True)
    )


def block_start(place_ref, index, rows):
    start = place_ref[index] * rows
    return pl.multiple_of(start, 32) if rows % 32 == 0 else start


def place_weights(place_ref, qk_ref, vo_ref, w_qk, w_vo, rows):
    across, _, deep = qk_ref.shape[:3]
    for i in range(across):
        for k in range(deep):
            start = block_start(place_ref, i * deep + k, rows)
            w_qk[pl.ds(start, rows), :] = qk_ref[i, 0, k]
            w_vo[pl.ds(start, rows), :] = vo_ref[0, i, k]


def accumulate(step, target, start_ref, value):
    @pl.when(step == 0)
    def _():
        target[...] = value if start_ref is None else start_ref[...] + value

    @pl.when(step > 0)
    def _():
        target[...] += value


def attention_forward_kernel(rows, last, *refs):
    qk_ref, vo_ref, *refs = refs
    place_ref, x_ref, bias_ref, mask_ref, vec_ref = refs[:5]
    if last:
        mix_in, qkv_ref, lse_ref, context_ref = refs[5:9]
        h_ref, hb_ref, n_ref, inv_ref, xt_ref, w_qk, w_vo, mix_ref = refs[9:]
    else:
        mix_in = None
        qkv_ref, lse_ref, context_ref, mix_ref, w_qk, w_vo = refs[5:]
    step = pl.program_id(0)
    place_weights(place_ref, qk_ref, vo_ref, w_qk, w_vo, rows)
    x = x_ref[...]
    width = w_qk.shape[1] // 2
    bias = bias_ref[0]
    qk = dot(x, w_qk[...], NN)
    v = (dot(x, w_vo[:, :width], NN) + bias[1:2, :width]).astype(BF)
    q = ((qk[:, :width] + bias[0:1, :width]).astype(BF).astype(F32) * HD ** (-0.5)).astype(BF)
    k = qk[:, width:].astype(BF)
    qkv_ref[0, :, :width] = q
    qkv_ref[0, :, width : 2 * width] = k
    qkv_ref[0, :, 2 * width :] = v
    mask = mask_ref[0:1]
    length = x.shape[0]
    contexts, logs = [], []
    for head in range(width // HD):
        cols = slice(head * HD, (head + 1) * HD)
        s = dot(q[:, cols], k[:, cols], NT) + mask
        peak = jnp.max(s, -1, keepdims=True)
        total = jnp.sum(jnp.exp(s - peak), -1, keepdims=True)
        log_total = peak + jnp.log(total)
        p = jnp.exp(s - log_total).astype(BF)
        contexts.append(dot(p, v[:, cols], NN).astype(BF))
        logs.append(log_total)
    context = jnp.concatenate(contexts, 1)
    context_ref[0] = context
    lanes = lax.broadcasted_iota(jnp.int32, (length, 128), 1)
    packed = jnp.zeros((length, 128), F32)
    for head, log_total in enumerate(logs):
        packed = jnp.where(lanes == head, log_total, packed)
    lse_ref[0] = packed.T[:8]
    accumulate(step, mix_ref, mix_in, dot(context, w_vo[:, width:], NT))
    if last:

        @pl.when(step == pl.num_programs(0) - 1)
        def _():
            first_res = x_ref[...].astype(F32) + mix_ref[...] + vec_ref[2:3]
            normed, inverse = normalized(first_res)
            hidden = normed * vec_ref[3:4] + vec_ref[4:5]
            n_ref[...] = normed
            inv_ref[...] = jnp.broadcast_to(inverse, inv_ref.shape)
            h_ref[...] = hidden
            hb_ref[...] = hidden.astype(BF)
            xt_ref[...] = x_ref[...].T


def attention_backward_kernel(rows, last, *refs):
    qk_ref, vo_ref, *refs = refs
    place_ref, xt_ref, gr_ref, grt_ref, qkv_ref, lse_ref, context_ref = refs[:7]
    mask_ref, start_ref = refs[7:9]
    if last:
        gqk_ref, gvo_ref, bias_ref, out_ref, w_qk, w_vo, g_qkv, gin_ref = refs[9:]
    else:
        gqk_ref, gvo_ref, bias_ref, gin_ref, w_qk, w_vo, g_qkv = refs[9:]
    step = pl.program_id(0)
    place_weights(place_ref, qk_ref, vo_ref, w_qk, w_vo, rows)
    width = w_qk.shape[1] // 2
    gc = dot(gr_ref[...], w_vo[:, width:], NN).astype(BF)
    mask = mask_ref[:, :1]
    sums = []
    for head in range(width // HD):
        q = qkv_ref[0, :, head * HD : (head + 1) * HD]
        k = qkv_ref[0, :, width + head * HD : width + (head + 1) * HD]
        v = qkv_ref[0, :, 2 * width + head * HD : 2 * width + (head + 1) * HD]
        g = gc[:, head * HD : (head + 1) * HD]
        p = jnp.exp(dot(k, q, NT) + mask - lse_ref[0, head : head + 1])
        dp = dot(v, g, NT)
        gv = dot(p.astype(BF), g, NN)
        delta = jnp.sum(p * dp, 0, keepdims=True)
        gs = (p * (dp - delta)).astype(BF)
        gk = dot(gs, q, NN)
        gq = dot(gs.T, (k.astype(F32) * HD ** (-0.5)).astype(BF), NN)
        g_qkv[:, head * HD : (head + 1) * HD] = gq.astype(BF)
        g_qkv[:, width + head * HD : width + (head + 1) * HD] = gk.astype(BF)
        g_qkv[:, 2 * width + head * HD : 2 * width + (head + 1) * HD] = gv.astype(BF)
        sums.append((jnp.sum(gq, 0, keepdims=True), jnp.sum(gv, 0, keepdims=True)))
    bias_ref[0, 0:1, :] = jnp.concatenate([s[0] for s in sums], 1)
    bias_ref[0, 1:2, :] = jnp.concatenate([s[1] for s in sums], 1)
    g_qk = g_qkv[:, : 2 * width]
    g_v = g_qkv[:, 2 * width :]
    gin = dot(g_qk, w_qk[...], NT) + dot(g_v, w_vo[:, :width], NT)
    accumulate(step, gin_ref, start_ref, gin)

    w_qk[...] = dot(xt_ref[...], g_qk, NN).astype(BF)
    w_vo[:, :width] = dot(xt_ref[...], g_v, NN).astype(BF)
    w_vo[:, width:] = dot(grt_ref[...], context_ref[0], NN).astype(BF)
    across, deep = gqk_ref.shape[0], gqk_ref.shape[2]
    for i in range(across):
        for j in range(deep):
            start = block_start(place_ref, i * deep + j, rows)
            gqk_ref[i, 0, j] = w_qk[pl.ds(start, rows), :]
            gvo_ref[0, i, j] = w_vo[pl.ds(start, rows), :]
    if last:

        @pl.when(step == pl.num_programs(0) - 1)
        def _():
            out_ref[...] = gin_ref[...].astype(BF)


def ffn_weights(refs):
    step = pl.program_id(0)
    up = jnp.where(step < 2, refs[0][...], refs[1][...])
    down = jnp.where(step % 2 == 0, refs[2][...], refs[3][...])
    return up, down


def ffn_forward_kernel(last, *refs):
    up, down = ffn_weights(refs[:4])
    h_ref, hb_ref, bias_ref, vec_ref = refs[4:8]
    if last:
        sum_in, cot_ref, mask_ref = refs[8:11]
        act_ref, slope_ref, out_ref, gr_ref, grb_ref, vec_out, sum_ref = refs[11:]
    else:
        sum_in = None
        act_ref, slope_ref, sum_ref = refs[8:]
    step = pl.program_id(0)
    u = dot(hb_ref[...], up, NT) + bias_ref[0:1]
    phi = 0.5 + 0.5 * lax.erf(u * 0.7071067811865476)
    act = (u * phi).astype(BF)
    act_ref[...] = act
    slope = phi + u * jnp.exp(-0.5 * u * u) * 0.3989422804014327
    slope_ref[...] = slope.astype(slope_ref.dtype)
    accumulate(step, sum_ref, sum_in, dot(act, down, NN))
    if last:

        @pl.when(step == pl.num_programs(0) - 1)
        def _():
            second_res = h_ref[...] + (sum_ref[...] + vec_ref[9:10])
            normed, inverse = normalized(second_res)
            out_ref[...] = (normed * vec_ref[10:11] + vec_ref[11:12]).astype(BF)
            d_result = jnp.where(mask_ref[:, :1] == 0.0, cot_ref[...].astype(F32), 0.0)
            vec_out[0:1] = jnp.sum(d_result * normed, 0, keepdims=True)
            vec_out[1:2] = jnp.sum(d_result, 0, keepdims=True)
            d_second = norm_backward(d_result, normed, inverse, vec_ref[10:11])
            vec_out[2:3] = jnp.sum(d_second, 0, keepdims=True)
            gr_ref[...] = d_second
            grb_ref[...] = d_second.astype(BF)


def ffn_backward_kernel(last, *refs):
    up, down = ffn_weights(refs[:4])
    grb_ref, hb_ref, act_ref, slope_ref, sum_in = refs[4:9]
    if last:
        n_ref, inv_ref, vec_ref = refs[9:12]
        gu_ref, gd_ref, bias_ref, gr_ref, gr1b_ref, grt_ref, vec_out, sum_ref = refs[12:]
    else:
        gu_ref, gd_ref, bias_ref, sum_ref = refs[9:]
    step = pl.program_id(0)
    grb = grb_ref[...]
    d_up = dot(grb, down, NT) * slope_ref[...].astype(F32)
    bias_ref[0:1] = jnp.sum(d_up, 0, keepdims=True)
    d_up_b = d_up.astype(BF)
    gd_ref[...] = dot(act_ref[...].T, grb, NN).astype(BF)
    gu_ref[...] = dot(d_up_b.T, hb_ref[...], NN).astype(BF)
    accumulate(step, sum_ref, sum_in, dot(d_up_b, up, NN))
    if last:

        @pl.when(step == pl.num_programs(0) - 1)
        def _():
            d_hidden = sum_ref[...]
            normed = n_ref[...]
            vec_out[0:1] = jnp.sum(d_hidden * normed, 0, keepdims=True)
            vec_out[1:2] = jnp.sum(d_hidden, 0, keepdims=True)
            d_first = norm_backward(d_hidden, normed, inv_ref[:, :1], vec_ref[3:4])
            vec_out[2:3] = jnp.sum(d_first, 0, keepdims=True)
            gr_ref[...] = d_first
            gr1b_ref[...] = d_first.astype(BF)
            grt_ref[...] = d_first.astype(BF).T


def whole(array):
    shape = array.shape
    return pl.BlockSpec(shape, lambda g: (0,) * len(shape))


def per_group(array):
    rest = array.shape[1:]
    return pl.BlockSpec((1, *rest), lambda g: (g, *(0 for _ in rest)))


def per_corner(array, rows, dim):
    block = [*array.shape[:3], rows, array.shape[4]]
    block[dim] = 1
    return pl.BlockSpec(tuple(block), lambda g: (0, g, 0, 0, 0) if dim else (g, 0, 0, 0, 0))


def per_rows(array, size, crossed):
    if crossed:
        return pl.BlockSpec((size, array.shape[1]), lambda g: (g % 2 * 2 + g // 2, 0))
    return pl.BlockSpec((size, array.shape[1]), lambda g: (g, 0))


def per_columns(array, size):
    return pl.BlockSpec((array.shape[0], size), lambda g: (0, g))


def spread_vectors_kernel(
    owner_ref, heads_ref, own_ref, other_ref, rows_ref, up_ref, bias_ref, units
):
    _, across, _, deep = COUNTS
    unit = units.shape[1]
    for x in range(2):
        for y in range(2):
            for z in range(deep):
                for c in range(2):
                    index = ((c * across + x) * 2 + y) * deep + z
                    start = owner_ref[index] * 3
                    for i in range(3):
                        units[pl.ds(start + i, 1), :] = (own_ref, other_ref)[c][
                            x, y, z, 0:1, i * unit : (i + 1) * unit
                        ]
    per_row = D // unit
    for row in range(12):
        for i in range(per_row):
            rows_ref[row : row + 1, i * unit : (i + 1) * unit] = units[
                row * per_row + i : row * per_row + i + 1, :
            ]
    half = FF // 2
    for index in range(FF // unit):
        start = index * unit
        up_ref[start // half, 0:1, start % half : start % half + unit] = units[
            pl.ds(5 * per_row + owner_ref[index], 1), :
        ]
    width = bias_ref.shape[2]
    for group in range(4):
        for kind in range(2):
            for i in range(width // unit):
                start = kind * per_row + heads_ref[group] * (width // unit) + i
                bias_ref[group, kind : kind + 1, i * unit : (i + 1) * unit] = units[
                    pl.ds(start, 1), :
                ]


def collect_vectors_kernel(
    owner_ref, heads_ref, bias_0, bias_1, up_0, up_1, one_ref, two_ref, out_ref, units
):
    out_ref[...] = jnp.zeros(out_ref.shape, F32)
    unit = units.shape[1]
    per_row = D // unit
    width = bias_0.shape[2]
    for group in range(4):
        source = (bias_0, bias_1)[group // 2]
        for kind in range(2):
            for i in range(width // unit):
                start = kind * per_row + heads_ref[group] * (width // unit) + i
                units[pl.ds(start, 1), :] = source[
                    group % 2, kind : kind + 1, i * unit : (i + 1) * unit
                ]
    half = FF // 2
    for index in range(FF // unit):
        source = (up_0, up_1)[index * unit // half]
        start = index * unit % half
        units[pl.ds(5 * per_row + owner_ref[index], 1), :] = source[0:1, start : start + unit]
    for row, source, line in (
        (2, one_ref, 2),
        (3, one_ref, 0),
        (4, one_ref, 1),
        (9, two_ref, 2),
        (10, two_ref, 0),
        (11, two_ref, 1),
    ):
        for i in range(per_row):
            units[row * per_row + i : row * per_row + i + 1, :] = source[
                line : line + 1, i * unit : (i + 1) * unit
            ]
    for index in range(FF // unit):
        for i in range(3):
            out_ref[index, 0:1, i * unit : (i + 1) * unit] = units[
                pl.ds(owner_ref[index] * 3 + i, 1), :
            ]


COUNTS = (2, 2, 2, 4)


def spread_vectors(owner, heads, own, other, unit, width):
    outs = [like((12, D), F32), like((2, 8, FF // 2), F32), like((4, 8, width), F32)]
    return pl.pallas_call(
        spread_vectors_kernel,
        in_specs=[SMEM_SPEC, SMEM_SPEC] + [pl.BlockSpec(memory_space=pltpu.VMEM)] * 2,
        out_specs=[pl.BlockSpec(memory_space=pltpu.VMEM)] * 3,
        out_shape=outs,
        scratch_shapes=[pltpu.VMEM((12 * D // unit, unit), F32)],
        compiler_params=params(8),
        cost_estimate=cost(0.0, 0.5, 0.0),
        name="spread_vectors",
    )(owner, heads, own, other)


def collect_vectors(owner, heads, unit, pair, *sources):
    return pl.pallas_call(
        collect_vectors_kernel,
        in_specs=[SMEM_SPEC, SMEM_SPEC] + [pl.BlockSpec(memory_space=pltpu.VMEM)] * len(sources),
        out_specs=pl.BlockSpec(memory_space=pltpu.VMEM),
        out_shape=like((FF // unit, 8, pair), F32),
        scratch_shapes=[pltpu.VMEM((12 * D // unit, unit), F32)],
        compiler_params=params(8),
        cost_estimate=cost(0.0, 0.5, 0.0),
        name="collect_vectors",
    )(owner, heads, *sources)


def advance_attention_kernel(rates, count, *refs):
    terms, olds, outs = refs[:count], refs[count : count + 6], refs[count + 6 :]
    whole_sum = terms[0][...]
    for term in terms[1:]:
        whole_sum = whole_sum + term[...].astype(F32)
    rows, width = olds[0].shape[1], olds[0].shape[2]
    parts = [
        whole_sum[:rows, :width],
        whole_sum[:rows, width:],
        whole_sum[rows + 8 :, :width],
    ]
    for i, grad in enumerate(parts):
        new = advance(olds[0][i], grad, olds[1][i], olds[2][i], DECAY, rates[0])
        for ref, value in zip(outs[:4], (grad, *new)):
            ref[i] = value
    grad = whole_sum[rows + 8 :, width:].T
    new = advance(olds[3][...], grad, olds[4][...], olds[5][...], DECAY, rates[1])
    for ref, value in zip(outs[4:8], (grad, *new)):
        ref[...] = value
    outs[8][...] = whole_sum[rows : rows + 8]


def advance_attention(terms, qkv, out, rates, others):
    outs = [like(qkv[0].shape, F32)] * 4 + [like(out[0].shape, F32)] * 4
    outs.append(like((8, terms[0].shape[1]), F32))
    vmem = pl.BlockSpec(memory_space=pltpu.VMEM)
    kernel = functools.partial(advance_attention_kernel, rates, len(terms))
    kernel, corners, _ = waiting(kernel, others)
    return pl.pallas_call(
        kernel,
        in_specs=[vmem] * (len(corners) + len(terms) + 6),
        out_specs=[vmem] * 9,
        out_shape=outs,
        compiler_params=params(16),
        cost_estimate=cost(0.0, 3.0, 0.0),
        name="advance_attention",
    )(*corners, *terms, *qkv, *out)


def waiting(kernel, others):
    corners = [corner(v) for v in jax.tree.leaves(others)]
    count = len(corners)
    return lambda *refs: kernel(*refs[count:]), corners, [whole(v) for v in corners]


SMEM_SPEC = pl.BlockSpec(memory_space=pltpu.SMEM)
like = jax.ShapeDtypeStruct


def per_part(array, size, by_x):
    return pl.BlockSpec((size, array.shape[1]), lambda g: (g // 2 if by_x else g % 2, 0))


def params(mib):
    return pltpu.CompilerParams(vmem_limit_bytes=mib << 20)


def cost(giga_flops, mega_bytes, mega_exps):
    return pl.CostEstimate(
        flops=int(giga_flops * 1e9),
        bytes_accessed=int(mega_bytes * 1e6),
        transcendentals=int(mega_exps * 1e6),
    )


def attention_forward(place, x, weights, biases, half, mask, vec_rows, mix, rows):
    length = x.shape[0]
    pair = weights[0].shape[4]
    width = pair // 2
    last = mix is not None
    row = like((length, D), F32)
    outs = [
        like((2, length, 3 * width), BF),
        like((2, 8, length), F32),
        like((2, length, width), BF),
    ]
    tail = [row]
    scratch = [pltpu.VMEM((D, pair), BF), pltpu.VMEM((D, pair), BF)]
    operands = [*weights, place, x, biases, mask, vec_rows]
    specs = [
        per_corner(weights[0], rows, 1),
        per_corner(weights[1], rows, 0),
        SMEM_SPEC,
        whole(x),
        pl.BlockSpec((1, *biases.shape[1:]), lambda g: (half * 2 + g, 0, 0)),
        whole(mask),
        whole(vec_rows),
    ]
    if last:
        low = like((length, D), BF)
        tail = [row, low, row, like((length, 128), F32), like((D, length), BF)]
        operands.append(mix)
        specs.append(whole(mix))
        scratch.append(pltpu.VMEM((length, D), F32))
    return pl.pallas_call(
        functools.partial(attention_forward_kernel, rows, last),
        grid=(2,),
        in_specs=specs,
        out_specs=[per_group(o) for o in outs] + [whole(o) for o in tail],
        out_shape=outs + tail,
        scratch_shapes=scratch,
        compiler_params=params(18),
        cost_estimate=cost(4.5, 6.0, 3.1),
        name="attention_forward_last" if last else "attention_forward",
    )(*operands)


def attention_backward(place, x_t, gr, gr_t, weights, saved, mask, start, rows, last, others):
    length = gr.shape[0]
    pair = weights[0].shape[4]
    width = pair // 2
    across, _, deep = weights[0].shape[:3]
    qkv, lse, context = saved
    grad_qk = like((across, 2, deep, rows, pair), BF)
    grad_vo = like((2, across, deep, rows, pair), BF)
    outs = [
        grad_qk,
        grad_vo,
        like((2, 8, width), F32),
        like((length, D), BF if last else F32),
    ]
    scratch = [
        pltpu.VMEM((D, pair), BF),
        pltpu.VMEM((D, pair), BF),
        pltpu.VMEM((length, 3 * width), BF),
    ]
    if last:
        scratch.append(pltpu.VMEM((length, D), F32))
    kernel = functools.partial(attention_backward_kernel, rows, last)
    kernel, corners, corner_specs = waiting(kernel, others)
    return pl.pallas_call(
        kernel,
        grid=(2,),
        in_specs=corner_specs
        + [
            per_corner(weights[0], rows, 1),
            per_corner(weights[1], rows, 0),
            SMEM_SPEC,
            whole(x_t),
            whole(gr),
            whole(gr_t),
            per_group(qkv),
            per_group(lse),
            per_group(context),
            whole(mask),
            whole(start),
        ],
        out_specs=[
            per_corner(grad_qk, rows, 1),
            per_corner(grad_vo, rows, 0),
            per_group(outs[2]),
            whole(outs[3]),
        ],
        out_shape=outs,
        scratch_shapes=scratch,
        compiler_params=params(18),
        cost_estimate=cost(0.5, 1.0, 0.1),
        name="attention_backward_last" if last else "attention_backward",
    )(*corners, *weights, place, x_t, gr, gr_t, qkv, lse, context, mask, start)


def ffn_operands(up, down):
    chunk = up[0].shape[0] // 2
    specs = [per_part(u, chunk, False) for u in up] + [per_part(d, chunk, True) for d in down]
    return [*up, *down], specs, chunk


def ffn_forward(h, hb, up, down, bias, vec_rows, tail_operands):
    length = h.shape[0]
    operands, specs, chunk = ffn_operands(up, down)
    hidden = 4 * chunk
    last = len(tail_operands) > 0
    row = like((length, D), F32)
    outs = [like((length, hidden), BF), like((length, hidden), BF)]
    tail = [row]
    scratch = []
    if last:
        low = like((length, D), BF)
        tail = [low, row, low, like((8, D), F32)]
        scratch = [pltpu.VMEM((length, D), F32)]
    return pl.pallas_call(
        functools.partial(ffn_forward_kernel, last),
        grid=(4,),
        in_specs=specs
        + [whole(h), whole(hb), per_columns(bias, chunk), whole(vec_rows)]
        + [whole(t) for t in tail_operands],
        out_specs=[per_columns(o, chunk) for o in outs] + [whole(o) for o in tail],
        out_shape=outs + tail,
        scratch_shapes=scratch,
        compiler_params=params(18),
        cost_estimate=cost(4.9, 12.0, 1.6),
        name="ffn_forward_last" if last else "ffn_forward",
    )(*operands, h, hb, bias, vec_rows, *tail_operands)


def ffn_backward(grb, hb, act, slope, up, down, total, tail_operands, others):
    length = grb.shape[0]
    operands, specs, chunk = ffn_operands(up, down)
    hidden = 4 * chunk
    last = len(tail_operands) > 0
    row = like((length, D), F32)
    grad = like((hidden, D), BF)
    outs = [grad, grad, like((8, hidden), F32)]
    tail = [row]
    scratch = []
    if last:
        tail = [row, like((length, D), BF), like((D, length), BF), like((8, D), F32)]
        scratch = [pltpu.VMEM((length, D), F32)]
    kernel, corners, corner_specs = waiting(functools.partial(ffn_backward_kernel, last), others)
    return pl.pallas_call(
        kernel,
        grid=(4,),
        in_specs=corner_specs
        + specs
        + [whole(grb), whole(hb), per_columns(act, chunk), per_columns(slope, chunk)]
        + [whole(total)]
        + [whole(t) for t in tail_operands],
        out_specs=[
            per_rows(grad, chunk, False),
            per_rows(grad, chunk, True),
            per_columns(outs[2], chunk),
        ]
        + [whole(o) for o in tail],
        out_shape=outs + tail,
        scratch_shapes=scratch,
        compiler_params=params(18),
        cost_estimate=cost(9.7, 16.0, 0.0),
        name="ffn_backward_last" if last else "ffn_backward",
    )(*corners, *operands, grb, hb, act, slope, total, *tail_operands)


def advance(weight, grad, moment, average, decay, rate):
    step_grad = grad + decay * weight
    moment_new = MOMENTUM * moment + step_grad
    weight_new = weight - rate * (step_grad + MOMENTUM * moment_new)
    average_new = AVERAGE * average + (1.0 - AVERAGE) * weight_new
    return (weight_new, moment_new, average_new)


def body(
    layer_input,
    lengths,
    cotangent,
    w_qkv,
    w_out,
    w_up,
    w_down,
    vectors,
    mom_qkv,
    mom_out,
    mom_up,
    mom_down,
    mom_vec,
    avg_qkv,
    avg_out,
    avg_up,
    avg_down,
    avg_vec,
):
    z, x, y, c = (lax.axis_index(a) for a in ("z", "x", "y", "c"))
    deep = lax.axis_size("z")
    blocks = deep * 8
    rows, head_cols = w_qkv.shape[1], w_qkv.shape[2]
    pair = 2 * head_cols
    vec_len = vectors.shape[0]
    ff_rows = w_up.shape[1]
    local = layer_input.shape[0]
    length = 4 * local

    kc, kx, ky, kz = jnp.meshgrid(
        jnp.arange(2), jnp.arange(2), jnp.arange(2), z_order(deep), indexing="ij"
    )
    owner = (((z ^ kz) * 2 + (x ^ kx)) * 4 + (y ^ ky) * 2 + (c ^ kc)).reshape(blocks)
    tz, tx, ty, tc = jnp.meshgrid(
        jnp.arange(deep), jnp.arange(2), jnp.arange(2), jnp.arange(2), indexing="ij"
    )
    seat = ((((c ^ tc) * 2 + (x ^ tx)) * 2 + (y ^ ty)) * deep + z_order(deep)[z ^ tz]).reshape(blocks)
    first, second = jnp.meshgrid(jnp.arange(2), jnp.arange(2), indexing="ij")
    group_head = ((y ^ second) * 2 + (c ^ first)).reshape(4)
    head_group = ((c ^ second) * 2 + (y ^ first)).reshape(4)

    in_kernel = rows % 32 == 0 and deep == COUNTS[3]
    owner, group_head = owner.astype(jnp.int32), group_head.astype(jnp.int32)

    vec_row = jnp.pad(vectors.astype(BF), (0, pair - vec_len))[None]
    vec_rows = jnp.pad(vec_row, ((0, 7), (0, 0)))
    pack_qk = jnp.concatenate([w_qkv[0], w_qkv[1]], 1).astype(BF)
    pack_vo = jnp.concatenate([w_qkv[2], w_out.T], 1).astype(BF)
    pack = jnp.concatenate([pack_qk, vec_rows, pack_vo], 0)
    doc_x, x_y = to_documents(layer_input)
    doc_cot, cot_y = to_documents(cotangent)
    attn_z, z_first = gather_z(pack)
    qk, vo = attn_z[:, : rows + 8], attn_z[:, rows + 8 :]
    qk_first, vo_first = send(qk, "y"), send(vo, "x")
    qk = after(jnp.stack([qk, qk_first], 0), vo_first, x_y)
    vo = after(jnp.stack([vo, vo_first], 0), qk_first)
    qk_got, vo_got = send(qk, "x"), send(vo, "y")
    qk, vo = jnp.stack([qk, qk_got], 0), jnp.stack([vo, vo_got], 0)
    qk_other, vo_other = send(qk, "c"), send(vo, "c")

    pack = jnp.concatenate([w_up.T.astype(BF), w_down.astype(BF)], 0)
    ffn_z, _ = gather_z(after(pack, z_first))
    first_got = (qk_first, vo_first)
    up, down = after((ffn_z[:, :ff_rows], ffn_z[:, ff_rows:]), first_got)
    up_got, down_got = send(up, "y"), send(down, "x")
    up, down = (
        after(jnp.stack([up, up_got], 0), down_got, qk_got, vo_got),
        after(jnp.stack([down, down_got], 0), up_got, qk_got, vo_got),
    )
    up_got, down_got = send(up, "x"), send(down, "y")

    vec_own, vec_other = (v[..., rows:, :].astype(F32) for v in (qk, qk_other))
    if in_kernel:
        vec_rows, bias_up, biases = spread_vectors(
            owner, group_head, vec_own, vec_other, ff_rows, head_cols
        )
    else:
        vec_all = jnp.stack([v[..., 0, :vec_len] for v in (vec_own, vec_other)], 0)
        vec_all = vec_all.reshape(blocks, vec_len)
        vec_rows = jnp.take(vec_all, seat, axis=0).reshape(12, D)
        bias_up = jnp.take(vec_rows[5:9].reshape(blocks, ff_rows), owner, axis=0)
        bias_up = jnp.pad(bias_up.reshape(2, 1, FF // 2), ((0, 0), (0, 7), (0, 0)))
        bias_q = jnp.take(vec_rows[0].reshape(4, head_cols), group_head, axis=0)
        bias_v = jnp.take(vec_rows[1].reshape(4, head_cols), group_head, axis=0)
        biases = jnp.pad(jnp.stack([bias_q, bias_v], 1), ((0, 0), (0, 6), (0, 0)))

    row = jnp.arange(length)
    part = row // local
    position = ((y ^ (part % 2)) * 2 + (c ^ (part // 2))) * local + row % local
    doc_len = lax.dynamic_index_in_dim(lengths, y * 2 + c, 0, keepdims=False)
    alive = position < doc_len
    mask = jnp.where(alive, 0.0, -1e30).astype(F32)
    mask_row = jnp.broadcast_to(mask[None, :], (8, length))
    mask_col = jnp.broadcast_to(mask[:, None], (length, 128))

    if in_kernel:
        zs = flip_order("z")[None, :]
        place = (zs * 2 + (x ^ jnp.arange(2)[:, None])).reshape(2 * deep)
        kernel_rows = rows
    else:
        xs = x ^ jnp.arange(2)
        zs = flip_order("z")

        def true_order(qk, vo):
            qk = jnp.take(jnp.take(qk[..., :rows, :], xs, axis=0), zs, axis=2)
            vo = jnp.take(jnp.take(vo, xs, axis=1), zs, axis=2)
            qk, vo = qk.transpose(1, 2, 0, 3, 4), vo.transpose(0, 2, 1, 3, 4)
            return qk.reshape(1, 2, 1, D, pair), vo.reshape(2, 1, 1, D, pair)

        def relative_order(qk, vo):
            qk = qk.reshape(2, deep, 2, rows, pair).transpose(2, 0, 1, 3, 4)
            vo = vo.reshape(2, deep, 2, rows, pair).transpose(0, 2, 1, 3, 4)
            qk = jnp.take(jnp.take(qk, xs, axis=0), zs, axis=2)
            return qk, jnp.take(jnp.take(vo, xs, axis=1), zs, axis=2)

        place = jnp.zeros((1,), jnp.int32)
        qk, vo = true_order(qk, vo)
        qk_other, vo_other = true_order(qk_other, vo_other)
        kernel_rows = D
    place = place.astype(jnp.int32)

    *saved_0, mix = attention_forward(
        place, doc_x, (qk, vo), biases, 0, mask_row, vec_rows, None, kernel_rows
    )
    *saved_1, hidden, hidden_b, normed, inverse, x_t = attention_forward(
        place, doc_x, (qk_other, vo_other), biases, 1, mask_row, vec_rows, mix, kernel_rows
    )
    flat = lambda v: v.reshape(FF // 4, D)
    up_own, down_own = (flat(up), flat(up_got)), (flat(down), flat(down_got))
    up_other = (send(up_own[0], "c"), send(after(up_own[1], hidden_b), "c"))
    down_other = (send(down_own[0], "c"), send(after(down_own[1], hidden_b), "c"))
    act_0, slope_0, mix = ffn_forward(
        hidden, hidden_b, up_own, down_own, bias_up[0], vec_rows, ()
    )
    act_1, slope_1, result, d_second, d_second_b, vec_two = ffn_forward(
        hidden, hidden_b, up_other, down_other, bias_up[1], vec_rows, (mix, doc_cot, mask_col)
    )
    out_own, out_y = from_documents_y(result, local)

    lead = (2, 2, deep, ff_rows, D)
    up_1, down_1, d_bias_1, d_hidden = ffn_backward(
        d_second_b, hidden_b, act_1, slope_1, up_other, down_other, d_second, (), ()
    )
    up_1, down_1 = send(up_1, "c"), send(down_1, "c")
    up_0, down_0, d_bias_0, d_first, d_first_b, d_first_t, vec_one = ffn_backward(
        d_second_b,
        hidden_b,
        act_0,
        slope_0,
        up_own,
        down_own,
        d_hidden,
        (normed, inverse, vec_rows),
        (),
    )
    grad_up = swap([up_0.reshape(lead), up_1.reshape(lead)], "x")
    grad_down = swap([down_0.reshape(lead), down_1.reshape(lead)], "y")
    ffn_c = (up_1, down_1)
    ffn_big = (grad_up[-1], grad_down[-1])
    grad_up, grad_down = swap(grad_up, "y"), swap(grad_down, "x")
    ffn_second = (grad_up[-1], grad_down[-1])
    grad_ffn, _ = scatter_z([grad_up, grad_down], False)

    qk_1, vo_1, bias_1, d_attn = attention_backward(
        place, x_t, d_first_b, d_first_t, (qk_other, vo_other), saved_1, mask_col, d_first, kernel_rows, False, (ffn_c, out_y)
    )
    qk_0, vo_0, bias_0, d_input = attention_backward(
        place, x_t, d_first_b, d_first_t, (qk, vo), saved_0, mask_col, d_attn, kernel_rows, True, ()
    )
    if not in_kernel:
        qk_1, vo_1 = relative_order(qk_1, vo_1)
        qk_0, vo_0 = relative_order(qk_0, vo_0)
    qk_1, vo_1 = send(qk_1, "c"), send(vo_1, "c")

    bias_0 = after(bias_0, ffn_big)
    if in_kernel:
        vec_part = collect_vectors(
            owner, group_head, ff_rows, pair, bias_0, bias_1, d_bias_0, d_bias_1, vec_one, vec_two
        ).reshape(2, 2, 2, deep, 8, pair)
    else:
        d_bias = jnp.concatenate([bias_0, bias_1], 0)
        d_bias_q = jnp.take(d_bias[:, 0], head_group, axis=0).reshape(D)
        d_bias_v = jnp.take(d_bias[:, 1], head_group, axis=0).reshape(D)
        d_bias_up = jnp.concatenate([d_bias_0[0], d_bias_1[0]]).reshape(blocks, ff_rows)
        d_bias_up = jnp.take(d_bias_up, seat, axis=0).reshape(FF)
        grad_vec = jnp.concatenate(
            [
                d_bias_q,
                d_bias_v,
                vec_one[2],
                vec_one[0],
                vec_one[1],
                d_bias_up,
                vec_two[2],
                vec_two[0],
                vec_two[1],
            ]
        )
        vec_part = jnp.take(grad_vec.reshape(blocks, vec_len), owner, axis=0)
        vec_part = jnp.pad(vec_part, ((0, 0), (0, pair - vec_len))).reshape(2, 2, 2, deep, 1, pair)
        vec_part = jnp.pad(vec_part, ((0, 0),) * 4 + ((0, 7), (0, 0)))
    vec_part = vec_part[0] + send(vec_part[1], "c")
    sum_qk, vec_terms, sum_vo = [qk_0, qk_1], [vec_part], [vo_0, vo_1]
    for axis_qk, axis_vo in (("x", "y"), ("y", "x")):
        part = jnp.concatenate(
            [total([t[1] for t in sum_qk]), total([t[1] for t in vec_terms])], -2
        )
        got = send(after(part, ffn_second).astype(BF), axis_qk)
        sum_qk = [t[0] for t in sum_qk] + [got[..., :rows, :]]
        vec_terms = [t[0] for t in vec_terms] + [got[..., rows:, :]]
        sum_vo = swap(sum_vo, axis_vo, ffn_second)
    d_input = after(d_input, got, sum_vo[-1])
    grad_attn, sent = scatter_z([sum_qk, vec_terms, sum_vo], True)
    grad_ffn = after(total(grad_ffn), sent)
    grad_up, grad_down = grad_ffn[:ff_rows].T, grad_ffn[ff_rows:]
    layer_output = from_documents(group_head, after(out_own, grad_ffn), out_y, BF)
    grad_input = from_documents(group_head, *from_documents_y(d_input, local), F32)

    slots = length * layer_input.shape[1] * deep * 2
    rate = RATE_BASE / math.sqrt(slots)
    rate_out = rate * math.sqrt(LEN / 8.0)
    olds_qkv, olds_out = (w_qkv, mom_qkv, avg_qkv), (w_out, mom_out, avg_out)
    if in_kernel:
        (
            grad_qkv,
            new_qkv,
            new_mom_qkv,
            new_avg_qkv,
            grad_out,
            new_out,
            new_mom_out,
            new_avg_out,
            grad_vec,
        ) = advance_attention(
            grad_attn, olds_qkv, olds_out, (rate, rate_out), (layer_output, grad_input)
        )
        grad_vec = grad_vec[0, :vec_len]
    else:
        grad_attn = total(grad_attn)
        sum_qk, sum_vo = grad_attn[:rows], grad_attn[rows + 8 :]
        grad_qkv = jnp.stack([sum_qk[:, :head_cols], sum_qk[:, head_cols:], sum_vo[:, :head_cols]])
        grad_out = sum_vo[:, head_cols:].T
        grad_vec = grad_attn[rows, :vec_len]
        new_qkv, new_mom_qkv, new_avg_qkv = advance(
            w_qkv, grad_qkv, mom_qkv, avg_qkv, DECAY, rate
        )
        new_out, new_mom_out, new_avg_out = advance(
            w_out, grad_out, mom_out, avg_out, DECAY, rate_out
        )
    new_up, new_mom_up, new_avg_up = advance(w_up, grad_up, mom_up, avg_up, DECAY, rate)
    new_down, new_mom_down, new_avg_down = advance(
        w_down, grad_down, mom_down, avg_down, DECAY, rate
    )
    new_vec, new_mom_vec, new_avg_vec = advance(vectors, grad_vec, mom_vec, avg_vec, 0.0, rate)
    return (
        layer_output,
        grad_input,
        grad_qkv,
        grad_out,
        grad_up,
        grad_down,
        grad_vec,
        new_qkv,
        new_out,
        new_up,
        new_down,
        new_vec,
        new_mom_qkv,
        new_mom_out,
        new_mom_up,
        new_mom_down,
        new_mom_vec,
        new_avg_qkv,
        new_avg_out,
        new_avg_up,
        new_avg_down,
        new_avg_vec,
    )


def solution(mesh):
    dp, head = mesh.shape["dp"], mesh.shape["head"]
    fine = Mesh(mesh.devices.reshape(dp // 2, 2, head // 2, 2), ("z", "x", "y", "c"))
    dps, heads, every = ("z", "x"), ("y", "c"), ("z", "x", "y", "c")
    acts = P(heads, dps, None)
    weights = (P(None, dps, heads), P(heads, dps), P(None, every), P(every, None), P(every))
    return jax.shard_map(
        body,
        mesh=fine,
        in_specs=(acts, P(dps), acts) + weights * 3,
        out_specs=(acts, acts) + weights * 4,
        check_vma=False,
    )
```

```python
import functools
import math

import jax
import jax.numpy as jnp
from jax import lax
from jax.experimental import pallas as pl
from jax.experimental.pallas import tpu as pltpu
from jax.sharding import Mesh
from jax.sharding import PartitionSpec as P

D = 768
HD = 64
FF = 3072
LEN = 512

EPSILON = 1e-05
MOMENTUM = 0.9
AVERAGE = 0.9
DECAY = 0.01
RATE_BASE = 0.05

BF = jnp.bfloat16
F32 = jnp.float32
NT = (((1,), (1,)), ((), ()))
NN = (((1,), (0,)), ((), ()))


def send(values, axis, bit=1):
    return lax.ppermute(values, axis, [(i, i ^ bit) for i in range(lax.axis_size(axis))])


def corner(array):
    rows, columns = min(8, array.shape[-2]), min(128, array.shape[-1])
    return array.reshape(-1, *array.shape[-2:])[0, :rows, :columns]


def after(values, *others):
    if not jax.tree.leaves(others):
        return values
    zero = sum(corner(v)[0, 0].astype(F32) * 0.0 for v in jax.tree.leaves(others))
    return jax.tree.map(lambda v: v + zero.astype(v.dtype), values)


def z_order(size):
    return jnp.array([0, 2, 1, 3]) if size == 4 else jnp.arange(size)


def flip_order(axis):
    size = lax.axis_size(axis)
    return lax.axis_index(axis) ^ z_order(size)


def gather_z(shard, before=()):
    size = lax.axis_size("z")
    if size != 4:
        whole = jnp.take(lax.all_gather(shard, "z"), flip_order("z"), axis=0)
        return whole, whole[0], whole[0]
    first = send(shard, "z", 2)
    pair = after(jnp.stack([shard, first], 0), before)
    second = send(pair, "z", 1)
    return jnp.concatenate([pair, second], 0), first, second


def total(terms):
    result = terms[0].astype(F32)
    for term in terms[1:]:
        result = result + term.astype(F32)
    return result


def swap(terms, axis, others=()):
    part = total([t[1] for t in terms])
    got = send(after(part, others).astype(BF), axis)
    return [t[0] for t in terms] + [got]


def scatter_z(sums, direct):
    joined = lambda index: jnp.concatenate([total([t[index] for t in terms]) for terms in sums], -2)
    if lax.axis_size("z") != 4:
        everything = jnp.take(joined(slice(None)).astype(BF), flip_order("z"), axis=0)
        parts = lax.all_to_all(everything, "z", 0, 0, tiled=True)
        return [total(list(parts[1:])), parts[0]], parts[0]
    if direct:
        parts = [joined(place).astype(BF) for place in (1, 2, 3)]
        return [joined(0)] + [send(part, "z", bit) for part, bit in zip(parts, (2, 1, 3))], parts[2]
    got = send(joined(slice(2, 4)).astype(BF), "z", 1)
    left, start = [], 0
    for terms in sums:
        end = start + terms[0].shape[-2]
        left.append([t[:2] for t in terms] + [got[:, start:end]])
        start = end
    sums = left
    part = joined(1).astype(BF)
    return [joined(0), send(part, "z", 2)], part


def to_documents(values, before_y=(), before_c=()):
    y, c = lax.axis_index("y"), lax.axis_index("c")
    local, _, width = values.shape
    docs = values.transpose(1, 0, 2).reshape(2, 2, local, width)
    mine = lax.dynamic_index_in_dim(docs, y, 0, keepdims=False)
    theirs = lax.dynamic_index_in_dim(docs, 1 - y, 0, keepdims=False)
    got_y = send(after(theirs, before_y), "y")
    of = lambda v, core: lax.dynamic_index_in_dim(v, core, 0, keepdims=False)
    got = send(after(jnp.stack([of(mine, 1 - c), of(got_y, 1 - c)], 0), before_c), "c")
    document = jnp.stack([of(mine, c), of(got_y, c), got[0], got[1]], 0)
    return document.reshape(4 * local, width), got_y


def from_documents_y(values, local):
    values = values.reshape(2, 2, local, values.shape[1])
    return values[:, 0], send(values[:, 1], "y")


def assemble_kernel(seats_ref, own_ref, got_y_ref, got_c_ref, out_ref):
    for place, ref, part in ((0, own_ref, 0), (1, got_y_ref, 0), (2, got_c_ref, 0), (3, got_c_ref, 1)):
        out_ref[seats_ref[place]] = ref[part].astype(out_ref.dtype)


def from_documents(seats, own, got_y, dtype):
    got_c = send(jnp.stack([own[1], got_y[1]], 0), "c")
    vmem = pl.BlockSpec(memory_space=pltpu.VMEM)
    docs = pl.pallas_call(
        assemble_kernel,
        in_specs=[SMEM_SPEC, vmem, vmem, vmem],
        out_specs=vmem,
        out_shape=jax.ShapeDtypeStruct((4, *own.shape[1:]), dtype),
        compiler_params=params(12),
        cost_estimate=cost(0.0, 2.0, 0.0),
        name="assemble",
    )(seats, own, got_y, got_c)
    return docs.transpose(1, 0, 2)


def dot(a, b, dims):
    return lax.dot_general(a, b, dims, preferred_element_type=F32)


def normalized(values):
    center = values - jnp.mean(values, -1, keepdims=True)
    inverse = lax.rsqrt(jnp.mean(center * center, -1, keepdims=True) + EPSILON)
    return center * inverse, inverse


def norm_backward(d_result, normed, inverse, gain):
    d_normed = d_result * gain
    return inverse * (
        d_normed
        - jnp.mean(d_normed, -1, keepdims=True)
        - normed * jnp.mean(d_normed * normed, -1, keepdims=True)
    )


def block_start(place_ref, index, rows):
    start = place_ref[index] * rows
    return pl.multiple_of(start, 32) if rows % 32 == 0 else start


def place_weights(place_ref, group, qk_ref, vo_ref, w_qk, w_vo, rows):
    across, _, deep = qk_ref.shape[:3]
    for i in range(across):
        for k in range(deep):
            start = block_start(place_ref, i * deep + k, rows)
            w_qk[pl.ds(start, rows), :] = qk_ref[i, group, k, :rows]
            w_vo[pl.ds(start, rows), :] = vo_ref[group, i, k]


def attention_forward_kernel(rows, half, last, *refs):
    qk_ref, vo_ref, *refs = refs
    place_ref, x_ref, bias_ref, mask_ref, vec_ref = refs[:5]
    if last:
        mix_in, qkv_ref, lse_ref, context_ref = refs[5:9]
        h_ref, hb_ref, n_ref, inv_ref, xt_ref, w_qk, w_vo, mix_ref = refs[9:]
    else:
        mix_in = None
        qkv_ref, lse_ref, context_ref, mix_ref, w_qk, w_vo = refs[5:]
    x = x_ref[...]
    length = x.shape[0]
    width = w_qk.shape[1] // 2
    mix_ref[...] = jnp.zeros(mix_ref.shape, F32) if mix_in is None else mix_in[...]

    @pl.loop(0, 2)
    def _(group):
        place_weights(place_ref, group, qk_ref, vo_ref, w_qk, w_vo, rows)
        bias = bias_ref[half * 2 + group]
        qk = dot(x, w_qk[...], NN)
        v = (dot(x, w_vo[:, :width], NN) + bias[1:2, :width]).astype(BF)
        q = ((qk[:, :width] + bias[0:1, :width]).astype(BF).astype(F32) * HD ** (-0.5)).astype(BF)
        k = qk[:, width:].astype(BF)
        qkv_ref[group, :, :width] = q
        qkv_ref[group, :, width : 2 * width] = k
        qkv_ref[group, :, 2 * width :] = v
        mask = mask_ref[0:1]
        contexts, logs = [], []
        for head in range(width // HD):
            cols = slice(head * HD, (head + 1) * HD)
            s = dot(q[:, cols], k[:, cols], NT) + mask
            peak = jnp.max(s, -1, keepdims=True)
            total_exp = jnp.sum(jnp.exp(s - peak), -1, keepdims=True)
            log_total = peak + jnp.log(total_exp)
            p = jnp.exp(s - log_total).astype(BF)
            contexts.append(dot(p, v[:, cols], NN).astype(BF))
            logs.append(log_total)
        context = jnp.concatenate(contexts, 1)
        context_ref[group] = context
        lanes = lax.broadcasted_iota(jnp.int32, (length, 128), 1)
        packed = jnp.zeros((length, 128), F32)
        for head, log_total in enumerate(logs):
            packed = jnp.where(lanes == head, log_total, packed)
        lse_ref[group] = packed.T[:8]
        mix_ref[...] += dot(context, w_vo[:, width:], NT)

    if last:
        first_res = x_ref[...].astype(F32) + mix_ref[...] + vec_ref[2:3]
        normed, inverse = normalized(first_res)
        hidden = normed * vec_ref[3:4] + vec_ref[4:5]
        n_ref[...] = normed
        inv_ref[...] = jnp.broadcast_to(inverse, inv_ref.shape)
        h_ref[...] = hidden
        hb_ref[...] = hidden.astype(BF)
        xt_ref[...] = x_ref[...].T


def attention_backward_kernel(rows, last, *refs):
    qk_ref, vo_ref, *refs = refs
    place_ref, xt_ref, gr_ref, grt_ref, qkv_ref, lse_ref, context_ref = refs[:7]
    mask_ref, start_ref = refs[7:9]
    if last:
        gqk_ref, gvo_ref, bias_ref, out_ref, w_qk, w_vo, g_qkv, gin_ref = refs[9:]
    else:
        gqk_ref, gvo_ref, bias_ref, gin_ref, w_qk, w_vo, g_qkv = refs[9:]
    width = w_qk.shape[1] // 2
    gin_ref[...] = start_ref[...]

    @pl.loop(0, 2)
    def _(group):
        place_weights(place_ref, group, qk_ref, vo_ref, w_qk, w_vo, rows)
        gc = dot(gr_ref[...], w_vo[:, width:], NN).astype(BF)
        mask = mask_ref[:, :1]
        sums = []
        for head in range(width // HD):
            q = qkv_ref[group, :, head * HD : (head + 1) * HD]
            k = qkv_ref[group, :, width + head * HD : width + (head + 1) * HD]
            v = qkv_ref[group, :, 2 * width + head * HD : 2 * width + (head + 1) * HD]
            g = gc[:, head * HD : (head + 1) * HD]
            p = jnp.exp(dot(k, q, NT) + mask - lse_ref[group, head : head + 1])
            dp = dot(v, g, NT)
            gv = dot(p.astype(BF), g, NN)
            delta = jnp.sum(p * dp, 0, keepdims=True)
            gs = (p * (dp - delta)).astype(BF)
            gk = dot(gs, q, NN)
            gq = dot(gs.T, (k.astype(F32) * HD ** (-0.5)).astype(BF), NN)
            g_qkv[:, head * HD : (head + 1) * HD] = gq.astype(BF)
            g_qkv[:, width + head * HD : width + (head + 1) * HD] = gk.astype(BF)
            g_qkv[:, 2 * width + head * HD : 2 * width + (head + 1) * HD] = gv.astype(BF)
            sums.append((jnp.sum(gq, 0, keepdims=True), jnp.sum(gv, 0, keepdims=True)))
        bias_ref[group, 0:1, :] = jnp.concatenate([s[0] for s in sums], 1)
        bias_ref[group, 1:2, :] = jnp.concatenate([s[1] for s in sums], 1)
        g_qk = g_qkv[:, : 2 * width]
        g_v = g_qkv[:, 2 * width :]
        gin = dot(g_qk, w_qk[...], NT) + dot(g_v, w_vo[:, :width], NT)
        gin_ref[...] += gin

        w_qk[...] = dot(xt_ref[...], g_qk, NN).astype(BF)
        w_vo[:, :width] = dot(xt_ref[...], g_v, NN).astype(BF)
        w_vo[:, width:] = dot(grt_ref[...], context_ref[group], NN).astype(BF)
        across, deep = gqk_ref.shape[0], gqk_ref.shape[2]
        for i in range(across):
            for j in range(deep):
                start = block_start(place_ref, i * deep + j, rows)
                gqk_ref[i, group, j] = w_qk[pl.ds(start, rows), :]
                gvo_ref[group, i, j] = w_vo[pl.ds(start, rows), :]

    if last:
        out_ref[...] = gin_ref[...].astype(BF)


def ffn_weights(refs, chunk, step):
    x, y = step // 2, step % 2
    up = refs[x][y * chunk : (y + 1) * chunk]
    down = refs[2 + y][x * chunk : (x + 1) * chunk]
    return up, down


def ffn_forward_kernel(last, *refs):
    weights, refs = refs[:4], refs[4:]
    h_ref, hb_ref, bias_ref, vec_ref = refs[:4]
    if last:
        sum_in, act_ref, slope_ref, out_ref, n_ref, inv_ref, sum_ref = refs[4:]
    else:
        sum_in = None
        act_ref, slope_ref, sum_ref = refs[4:]
    chunk = weights[0].shape[0] // 2
    for step in range(4):
        up, down = ffn_weights(weights, chunk, step)
        columns = slice(step * chunk, (step + 1) * chunk)
        u = dot(hb_ref[...], up, NT) + bias_ref[0:1, columns]
        phi = 0.5 + 0.5 * lax.erf(u * 0.7071067811865476)
        act = (u * phi).astype(BF)
        act_ref[:, columns] = act
        slope = phi + u * jnp.exp(-0.5 * u * u) * 0.3989422804014327
        slope_ref[:, columns] = slope.astype(slope_ref.dtype)
        part = dot(act, down, NN)
        if step > 0:
            sum_ref[...] += part
        else:
            sum_ref[...] = part if sum_in is None else sum_in[...] + part
    if last:
        second_res = h_ref[...] + (sum_ref[...] + vec_ref[9:10])
        normed, inverse = normalized(second_res)
        out_ref[...] = (normed * vec_ref[10:11] + vec_ref[11:12]).astype(BF)
        n_ref[...] = normed
        inv_ref[...] = jnp.broadcast_to(inverse, inv_ref.shape)


def ffn_backward_kernel(last, *refs):
    weights, refs = refs[:4], refs[4:]
    hb_ref, act_ref, slope_ref, n_ref, inv_ref, vec_ref = refs[:6]
    if last:
        grb_ref, sum_in = refs[6:8]
        gu_ref, gd_ref, bias_ref, gr_ref, gr1b_ref, grt_ref, vec_out, sum_ref = refs[8:]
        sum_ref[...] = sum_in[...]
    else:
        cot_ref, mask_ref, gu_ref, gd_ref, bias_ref, grb_ref, vec_out, sum_ref = refs[6:]
        normed = n_ref[...]
        d_result = jnp.where(mask_ref[:, :1] == 0.0, cot_ref[...].astype(F32), 0.0)
        vec_out[0:1] = jnp.sum(d_result * normed, 0, keepdims=True)
        vec_out[1:2] = jnp.sum(d_result, 0, keepdims=True)
        d_second = norm_backward(d_result, normed, inv_ref[:, :1], vec_ref[10:11])
        vec_out[2:3] = jnp.sum(d_second, 0, keepdims=True)
        sum_ref[...] = d_second
        grb_ref[...] = d_second.astype(BF)
    chunk = weights[0].shape[0] // 2
    for step in range(4):
        up, down = ffn_weights(weights, chunk, step)
        columns = slice(step * chunk, (step + 1) * chunk)
        grb = grb_ref[...]
        d_up = dot(grb, down, NT) * slope_ref[:, columns].astype(F32)
        bias_ref[0:1, columns] = jnp.sum(d_up, 0, keepdims=True)
        d_up_b = d_up.astype(BF)
        crossed = (step % 2 * 2 + step // 2) * chunk
        gd_ref[crossed : crossed + chunk] = dot(act_ref[:, columns].T, grb, NN).astype(BF)
        gu_ref[step * chunk : (step + 1) * chunk] = dot(d_up_b.T, hb_ref[...], NN).astype(BF)
        sum_ref[...] += dot(d_up_b, up, NN)
    if last:
        d_hidden = sum_ref[...]
        normed = n_ref[...]
        vec_out[0:1] = jnp.sum(d_hidden * normed, 0, keepdims=True)
        vec_out[1:2] = jnp.sum(d_hidden, 0, keepdims=True)
        d_first = norm_backward(d_hidden, normed, inv_ref[:, :1], vec_ref[3:4])
        vec_out[2:3] = jnp.sum(d_first, 0, keepdims=True)
        gr_ref[...] = d_first
        gr1b_ref[...] = d_first.astype(BF)
        grt_ref[...] = d_first.astype(BF).T


VMEM_SPEC = pl.BlockSpec(memory_space=pltpu.VMEM)


def spread_vectors_kernel(
    owner_ref, heads_ref, own_ref, other_ref, rows_ref, up_ref, bias_ref, units
):
    _, across, _, deep = COUNTS
    unit = units.shape[1]
    for x in range(2):
        for y in range(2):
            for z in range(deep):
                for c in range(2):
                    index = ((c * across + x) * 2 + y) * deep + z
                    start = owner_ref[index] * 3
                    for i in range(3):
                        units[pl.ds(start + i, 1), :] = (own_ref, other_ref)[c][
                            x, y, z, 0:1, i * unit : (i + 1) * unit
                        ]
    per_row = D // unit
    for row in range(12):
        for i in range(per_row):
            rows_ref[row : row + 1, i * unit : (i + 1) * unit] = units[
                row * per_row + i : row * per_row + i + 1, :
            ]
    half = FF // 2
    for index in range(FF // unit):
        start = index * unit
        up_ref[start // half, 0:1, start % half : start % half + unit] = units[
            pl.ds(5 * per_row + owner_ref[index], 1), :
        ]
    width = bias_ref.shape[2]
    for group in range(4):
        for kind in range(2):
            for i in range(width // unit):
                start = kind * per_row + heads_ref[group] * (width // unit) + i
                bias_ref[group, kind : kind + 1, i * unit : (i + 1) * unit] = units[
                    pl.ds(start, 1), :
                ]


def collect_vectors_kernel(
    owner_ref, heads_ref, bias_0, bias_1, up_0, up_1, one_ref, two_ref, out_ref, units
):
    out_ref[...] = jnp.zeros(out_ref.shape, F32)
    unit = units.shape[1]
    per_row = D // unit
    width = bias_0.shape[2]
    for group in range(4):
        source = (bias_0, bias_1)[group // 2]
        for kind in range(2):
            for i in range(width // unit):
                start = kind * per_row + heads_ref[group] * (width // unit) + i
                units[pl.ds(start, 1), :] = source[
                    group % 2, kind : kind + 1, i * unit : (i + 1) * unit
                ]
    half = FF // 2
    for index in range(FF // unit):
        source = (up_0, up_1)[index * unit // half]
        start = index * unit % half
        units[pl.ds(5 * per_row + owner_ref[index], 1), :] = source[0:1, start : start + unit]
    for row, source, line in (
        (2, one_ref, 2),
        (3, one_ref, 0),
        (4, one_ref, 1),
        (9, two_ref, 2),
        (10, two_ref, 0),
        (11, two_ref, 1),
    ):
        for i in range(per_row):
            units[row * per_row + i : row * per_row + i + 1, :] = source[
                line : line + 1, i * unit : (i + 1) * unit
            ]
    for index in range(FF // unit):
        for i in range(3):
            out_ref[index, 0:1, i * unit : (i + 1) * unit] = units[
                pl.ds(owner_ref[index] * 3 + i, 1), :
            ]


COUNTS = (2, 2, 2, 4)


def spread_vectors(owner, heads, own, other, unit, width):
    outs = [like((12, D), F32), like((2, 8, FF // 2), F32), like((4, 8, width), F32)]
    return pl.pallas_call(
        spread_vectors_kernel,
        in_specs=[SMEM_SPEC, SMEM_SPEC] + [pl.BlockSpec(memory_space=pltpu.VMEM)] * 2,
        out_specs=[pl.BlockSpec(memory_space=pltpu.VMEM)] * 3,
        out_shape=outs,
        scratch_shapes=[pltpu.VMEM((12 * D // unit, unit), F32)],
        compiler_params=params(8),
        cost_estimate=cost(0.0, 0.5, 0.0),
        name="spread_vectors",
    )(owner, heads, own, other)


def collect_vectors(owner, heads, unit, pair, *sources):
    return pl.pallas_call(
        collect_vectors_kernel,
        in_specs=[SMEM_SPEC, SMEM_SPEC] + [pl.BlockSpec(memory_space=pltpu.VMEM)] * len(sources),
        out_specs=pl.BlockSpec(memory_space=pltpu.VMEM),
        out_shape=like((FF // unit, 8, pair), F32),
        scratch_shapes=[pltpu.VMEM((12 * D // unit, unit), F32)],
        compiler_params=params(8),
        cost_estimate=cost(0.0, 0.5, 0.0),
        name="collect_vectors",
    )(owner, heads, *sources)


def advance_attention_kernel(rates, count, *refs):
    terms, olds, outs = refs[:count], refs[count : count + 6], refs[count + 6 :]
    whole_sum = terms[0][...]
    for term in terms[1:]:
        whole_sum = whole_sum + term[...].astype(F32)
    rows, width = olds[0].shape[1], olds[0].shape[2]
    parts = [
        whole_sum[:rows, :width],
        whole_sum[:rows, width:],
        whole_sum[rows + 8 :, :width],
    ]
    for i, grad in enumerate(parts):
        new = advance(olds[0][i], grad, olds[1][i], olds[2][i], DECAY, rates[0])
        for ref, value in zip(outs[:4], (grad, *new)):
            ref[i] = value
    grad = whole_sum[rows + 8 :, width:].T
    new = advance(olds[3][...], grad, olds[4][...], olds[5][...], DECAY, rates[1])
    for ref, value in zip(outs[4:8], (grad, *new)):
        ref[...] = value
    outs[8][...] = whole_sum[rows : rows + 8]


def advance_attention(terms, qkv, out, rates, others):
    outs = [like(qkv[0].shape, F32)] * 4 + [like(out[0].shape, F32)] * 4
    outs.append(like((8, terms[0].shape[1]), F32))
    vmem = pl.BlockSpec(memory_space=pltpu.VMEM)
    kernel = functools.partial(advance_attention_kernel, rates, len(terms))
    kernel, corners, _ = waiting(kernel, others)
    return pl.pallas_call(
        kernel,
        in_specs=[vmem] * (len(corners) + len(terms) + 6),
        out_specs=[vmem] * 9,
        out_shape=outs,
        compiler_params=params(16),
        cost_estimate=cost(0.0, 3.0, 0.0),
        name="advance_attention",
    )(*corners, *terms, *qkv, *out)


def waiting(kernel, others):
    corners = [corner(v) for v in jax.tree.leaves(others)]
    count = len(corners)
    return lambda *refs: kernel(*refs[count:]), corners, [VMEM_SPEC] * count


SMEM_SPEC = pl.BlockSpec(memory_space=pltpu.SMEM)
like = jax.ShapeDtypeStruct


def params(mib):
    return pltpu.CompilerParams(vmem_limit_bytes=mib << 20)


def cost(giga_flops, mega_bytes, mega_exps):
    return pl.CostEstimate(
        flops=int(giga_flops * 1e9),
        bytes_accessed=int(mega_bytes * 1e6),
        transcendentals=int(mega_exps * 1e6),
    )


def attention_forward(place, x, weights, biases, half, mask, vec_rows, mix, rows):
    length = x.shape[0]
    pair = weights[0].shape[4]
    width = pair // 2
    last = mix is not None
    row = like((length, D), F32)
    outs = [
        like((2, length, 3 * width), BF),
        like((2, 8, length), F32),
        like((2, length, width), BF),
    ]
    tail = [row]
    scratch = [pltpu.VMEM((D, pair), BF), pltpu.VMEM((D, pair), BF)]
    operands = [*weights, place, x, biases, mask, vec_rows]
    if last:
        low = like((length, D), BF)
        tail = [row, low, row, like((length, 128), F32), like((D, length), BF)]
        operands.append(mix)
        scratch.append(pltpu.VMEM((length, D), F32))
    return pl.pallas_call(
        functools.partial(attention_forward_kernel, rows, half, last),
        in_specs=[SMEM_SPEC if v is place else VMEM_SPEC for v in operands],
        out_specs=[VMEM_SPEC] * len(outs + tail),
        out_shape=outs + tail,
        scratch_shapes=scratch,
        compiler_params=params(14),
        cost_estimate=cost(4.5, 6.0, 3.1),
        name="attention_forward_last" if last else "attention_forward",
    )(*operands)


def attention_backward(place, x_t, gr, gr_t, weights, saved, mask, start, rows, last, others):
    length = gr.shape[0]
    pair = weights[0].shape[4]
    width = pair // 2
    across, _, deep = weights[0].shape[:3]
    qkv, lse, context = saved
    grad_qk = like((across, 2, deep, rows, pair), BF)
    grad_vo = like((2, across, deep, rows, pair), BF)
    outs = [
        grad_qk,
        grad_vo,
        like((2, 8, width), F32),
        like((length, D), BF if last else F32),
    ]
    scratch = [
        pltpu.VMEM((D, pair), BF),
        pltpu.VMEM((D, pair), BF),
        pltpu.VMEM((length, 3 * width), BF),
    ]
    if last:
        scratch.append(pltpu.VMEM((length, D), F32))
    kernel = functools.partial(attention_backward_kernel, rows, last)
    kernel, corners, corner_specs = waiting(kernel, others)
    return pl.pallas_call(
        kernel,
        in_specs=corner_specs + [VMEM_SPEC] * 2 + [SMEM_SPEC] + [VMEM_SPEC] * 8,
        out_specs=[VMEM_SPEC] * 4,
        out_shape=outs,
        scratch_shapes=scratch,
        compiler_params=params(14),
        cost_estimate=cost(0.5, 1.0, 0.1),
        name="attention_backward_last" if last else "attention_backward",
    )(*corners, *weights, place, x_t, gr, gr_t, qkv, lse, context, mask, start)


def ffn_forward(h, hb, up, down, bias, vec_rows, tail_operands):
    length = h.shape[0]
    hidden = 2 * up[0].shape[0]
    last = len(tail_operands) > 0
    row = like((length, D), F32)
    outs = [like((length, hidden), BF), like((length, hidden), BF)]
    tail = [row]
    scratch = []
    if last:
        tail = [like((length, D), BF), row, like((length, 128), F32)]
        scratch = [pltpu.VMEM((length, D), F32)]
    return pl.pallas_call(
        functools.partial(ffn_forward_kernel, last),
        in_specs=[VMEM_SPEC] * (8 + len(tail_operands)),
        out_specs=[VMEM_SPEC] * len(outs + tail),
        out_shape=outs + tail,
        scratch_shapes=scratch,
        compiler_params=params(14),
        cost_estimate=cost(4.9, 12.0, 1.6),
        name="ffn_forward_last" if last else "ffn_forward",
    )(*up, *down, h, hb, bias, vec_rows, *tail_operands)


def ffn_backward(hb, act, slope, up, down, norm, tail_operands, last):
    length = hb.shape[0]
    hidden = 2 * up[0].shape[0]
    row = like((length, D), F32)
    low = like((length, D), BF)
    grad = like((hidden, D), BF)
    outs = [grad, grad, like((8, hidden), F32)]
    vector = like((8, D), F32)
    tail = [row, low, like((D, length), BF), vector] if last else [low, vector, row]
    return pl.pallas_call(
        functools.partial(ffn_backward_kernel, last),
        in_specs=[VMEM_SPEC] * (7 + len(norm) + len(tail_operands)),
        out_specs=[VMEM_SPEC] * len(outs + tail),
        out_shape=outs + tail,
        scratch_shapes=[pltpu.VMEM((length, D), F32)] if last else [],
        compiler_params=params(14),
        cost_estimate=cost(9.7, 16.0, 0.0),
        name="ffn_backward_last" if last else "ffn_backward",
    )(*up, *down, hb, act, slope, *norm, *tail_operands)


def advance(weight, grad, moment, average, decay, rate):
    step_grad = grad + decay * weight
    moment_new = MOMENTUM * moment + step_grad
    weight_new = weight - rate * (step_grad + MOMENTUM * moment_new)
    average_new = AVERAGE * average + (1.0 - AVERAGE) * weight_new
    return (weight_new, moment_new, average_new)


def body(
    layer_input,
    lengths,
    cotangent,
    w_qkv,
    w_out,
    w_up,
    w_down,
    vectors,
    mom_qkv,
    mom_out,
    mom_up,
    mom_down,
    mom_vec,
    avg_qkv,
    avg_out,
    avg_up,
    avg_down,
    avg_vec,
):
    z, x, y, c = (lax.axis_index(a) for a in ("z", "x", "y", "c"))
    deep = lax.axis_size("z")
    blocks = deep * 8
    rows, head_cols = w_qkv.shape[1], w_qkv.shape[2]
    pair = 2 * head_cols
    vec_len = vectors.shape[0]
    ff_rows = w_up.shape[1]
    local = layer_input.shape[0]
    length = 4 * local

    kc, kx, ky, kz = jnp.meshgrid(
        jnp.arange(2), jnp.arange(2), jnp.arange(2), z_order(deep), indexing="ij"
    )
    owner = (((z ^ kz) * 2 + (x ^ kx)) * 4 + (y ^ ky) * 2 + (c ^ kc)).reshape(blocks)
    tz, tx, ty, tc = jnp.meshgrid(
        jnp.arange(deep), jnp.arange(2), jnp.arange(2), jnp.arange(2), indexing="ij"
    )
    seat = ((((c ^ tc) * 2 + (x ^ tx)) * 2 + (y ^ ty)) * deep + z_order(deep)[z ^ tz]).reshape(blocks)
    first, second = jnp.meshgrid(jnp.arange(2), jnp.arange(2), indexing="ij")
    group_head = ((y ^ second) * 2 + (c ^ first)).reshape(4)
    head_group = ((c ^ second) * 2 + (y ^ first)).reshape(4)

    in_kernel = rows % 32 == 0 and deep == COUNTS[3]
    owner, group_head = owner.astype(jnp.int32), group_head.astype(jnp.int32)

    vec_row = jnp.pad(vectors.astype(BF), (0, pair - vec_len))[None]
    vec_rows = jnp.pad(vec_row, ((0, 7), (0, 0)))
    pack_qk = jnp.concatenate([w_qkv[0], w_qkv[1]], 1).astype(BF)
    pack_vo = jnp.concatenate([w_qkv[2], w_out.T], 1).astype(BF)
    pack = jnp.concatenate([pack_qk, vec_rows, pack_vo], 0)
    doc_x, x_y = to_documents(layer_input)
    attn_z, z_first, z_second = gather_z(pack)
    qk, vo = attn_z[:, : rows + 8], attn_z[:, rows + 8 :]
    qk_first, vo_first = send(qk, "y"), send(vo, "x")
    qk = after(jnp.stack([qk, qk_first], 0), vo_first, x_y)
    vo = after(jnp.stack([vo, vo_first], 0), qk_first)
    qk_got, vo_got = send(qk, "x"), send(vo, "y")
    qk, vo = jnp.stack([qk, qk_got], 0), jnp.stack([vo, vo_got], 0)
    qk_other, vo_other = send(qk, "c"), send(vo, "c")

    pack = jnp.concatenate([w_up.T.astype(BF), w_down.astype(BF)], 0)
    ffn_z, _, _ = gather_z(after(pack, z_first), z_second)
    first_got = (qk_first, vo_first)
    up, down = after((ffn_z[:, :ff_rows], ffn_z[:, ff_rows:]), first_got)
    up_got, down_got = send(up, "y"), send(down, "x")
    up, down = (
        after(jnp.stack([up, up_got], 0), down_got, qk_got, vo_got),
        after(jnp.stack([down, down_got], 0), up_got, qk_got, vo_got),
    )
    up_got, down_got = send(up, "x"), send(down, "y")

    vec_own, vec_other = (v[..., rows:, :].astype(F32) for v in (qk, qk_other))
    if in_kernel:
        vec_rows, bias_up, biases = spread_vectors(
            owner, group_head, vec_own, vec_other, ff_rows, head_cols
        )
    else:
        vec_all = jnp.stack([v[..., 0, :vec_len] for v in (vec_own, vec_other)], 0)
        vec_all = vec_all.reshape(blocks, vec_len)
        vec_rows = jnp.take(vec_all, seat, axis=0).reshape(12, D)
        bias_up = jnp.take(vec_rows[5:9].reshape(blocks, ff_rows), owner, axis=0)
        bias_up = jnp.pad(bias_up.reshape(2, 1, FF // 2), ((0, 0), (0, 7), (0, 0)))
        bias_q = jnp.take(vec_rows[0].reshape(4, head_cols), group_head, axis=0)
        bias_v = jnp.take(vec_rows[1].reshape(4, head_cols), group_head, axis=0)
        biases = jnp.pad(jnp.stack([bias_q, bias_v], 1), ((0, 0), (0, 6), (0, 0)))

    row = jnp.arange(length)
    part = row // local
    position = ((y ^ (part % 2)) * 2 + (c ^ (part // 2))) * local + row % local
    doc_len = lax.dynamic_index_in_dim(lengths, y * 2 + c, 0, keepdims=False)
    alive = position < doc_len
    mask = jnp.where(alive, 0.0, -1e30).astype(F32)
    mask_row = jnp.broadcast_to(mask[None, :], (8, length))
    mask_col = jnp.broadcast_to(mask[:, None], (length, 128))

    if in_kernel:
        zs = flip_order("z")[None, :]
        place = (zs * 2 + (x ^ jnp.arange(2)[:, None])).reshape(2 * deep)
        kernel_rows = rows
    else:
        xs = x ^ jnp.arange(2)
        zs = flip_order("z")

        def true_order(qk, vo):
            qk = jnp.take(jnp.take(qk[..., :rows, :], xs, axis=0), zs, axis=2)
            vo = jnp.take(jnp.take(vo, xs, axis=1), zs, axis=2)
            qk, vo = qk.transpose(1, 2, 0, 3, 4), vo.transpose(0, 2, 1, 3, 4)
            return qk.reshape(1, 2, 1, D, pair), vo.reshape(2, 1, 1, D, pair)

        def relative_order(qk, vo):
            qk = qk.reshape(2, deep, 2, rows, pair).transpose(2, 0, 1, 3, 4)
            vo = vo.reshape(2, deep, 2, rows, pair).transpose(0, 2, 1, 3, 4)
            qk = jnp.take(jnp.take(qk, xs, axis=0), zs, axis=2)
            return qk, jnp.take(jnp.take(vo, xs, axis=1), zs, axis=2)

        place = jnp.zeros((1,), jnp.int32)
        qk, vo = true_order(qk, vo)
        qk_other, vo_other = true_order(qk_other, vo_other)
        kernel_rows = D
    place = place.astype(jnp.int32)

    *saved_0, mix = attention_forward(
        place, doc_x, (qk, vo), biases, 0, mask_row, vec_rows, None, kernel_rows
    )
    *saved_1, hidden, hidden_b, normed, inverse, x_t = attention_forward(
        place, doc_x, (qk_other, vo_other), biases, 1, mask_row, vec_rows, mix, kernel_rows
    )
    flat = lambda v: v.reshape(FF // 4, D)
    up_own, down_own = (flat(up), flat(up_got)), (flat(down), flat(down_got))
    up_other = (send(up_own[0], "c"), send(after(up_own[1], hidden_b), "c"))
    down_other = (send(down_own[0], "c"), send(after(down_own[1], hidden_b), "c"))
    act_0, slope_0, mix = ffn_forward(
        hidden, hidden_b, up_own, down_own, bias_up[0], vec_rows, ()
    )
    doc_cot, _ = to_documents(cotangent, hidden_b, mix)
    act_1, slope_1, result, normed_two, inverse_two = ffn_forward(
        hidden, hidden_b, up_other, down_other, bias_up[1], vec_rows, (mix,)
    )
    out_own, out_y = from_documents_y(result, local)

    lead = (2, 2, deep, ff_rows, D)
    norm_two = (normed_two, inverse_two, vec_rows)
    up_1, down_1, d_bias_1, d_second_b, vec_two, d_hidden = ffn_backward(
        hidden_b, act_1, slope_1, up_other, down_other, norm_two, (doc_cot, mask_col), False
    )
    up_1, down_1 = send(up_1, "c"), send(down_1, "c")
    norm_one = (normed, inverse, vec_rows)
    up_0, down_0, d_bias_0, d_first, d_first_b, d_first_t, vec_one = ffn_backward(
        hidden_b, act_0, slope_0, up_own, down_own, norm_one, (d_second_b, d_hidden), True
    )
    grad_up = swap([up_0.reshape(lead), up_1.reshape(lead)], "x")
    grad_down = swap([down_0.reshape(lead), down_1.reshape(lead)], "y")
    ffn_c = (up_1, down_1)
    ffn_big = (grad_up[-1], grad_down[-1])
    grad_up, grad_down = swap(grad_up, "y"), swap(grad_down, "x")
    ffn_second = (grad_up[-1], grad_down[-1])
    grad_ffn, _ = scatter_z([grad_up, grad_down], False)

    qk_1, vo_1, bias_1, d_attn = attention_backward(
        place, x_t, d_first_b, d_first_t, (qk_other, vo_other), saved_1, mask_col, d_first, kernel_rows, False, ffn_c
    )
    qk_0, vo_0, bias_0, d_input = attention_backward(
        place, x_t, d_first_b, d_first_t, (qk, vo), saved_0, mask_col, d_attn, kernel_rows, True, (out_y,)
    )
    if not in_kernel:
        qk_1, vo_1 = relative_order(qk_1, vo_1)
        qk_0, vo_0 = relative_order(qk_0, vo_0)
    qk_1, vo_1 = send(qk_1, "c"), send(vo_1, "c")

    bias_0 = after(bias_0, ffn_big)
    if in_kernel:
        vec_part = collect_vectors(
            owner, group_head, ff_rows, pair, bias_0, bias_1, d_bias_0, d_bias_1, vec_one, vec_two
        ).reshape(2, 2, 2, deep, 8, pair)
    else:
        d_bias = jnp.concatenate([bias_0, bias_1], 0)
        d_bias_q = jnp.take(d_bias[:, 0], head_group, axis=0).reshape(D)
        d_bias_v = jnp.take(d_bias[:, 1], head_group, axis=0).reshape(D)
        d_bias_up = jnp.concatenate([d_bias_0[0], d_bias_1[0]]).reshape(blocks, ff_rows)
        d_bias_up = jnp.take(d_bias_up, seat, axis=0).reshape(FF)
        grad_vec = jnp.concatenate(
            [
                d_bias_q,
                d_bias_v,
                vec_one[2],
                vec_one[0],
                vec_one[1],
                d_bias_up,
                vec_two[2],
                vec_two[0],
                vec_two[1],
            ]
        )
        vec_part = jnp.take(grad_vec.reshape(blocks, vec_len), owner, axis=0)
        vec_part = jnp.pad(vec_part, ((0, 0), (0, pair - vec_len))).reshape(2, 2, 2, deep, 1, pair)
        vec_part = jnp.pad(vec_part, ((0, 0),) * 4 + ((0, 7), (0, 0)))
    vec_part = vec_part[0] + send(vec_part[1], "c")
    sum_qk, vec_terms, sum_vo = [qk_0, qk_1], [vec_part], [vo_0, vo_1]
    for axis_qk, axis_vo in (("x", "y"), ("y", "x")):
        part = jnp.concatenate(
            [total([t[1] for t in sum_qk]), total([t[1] for t in vec_terms])], -2
        )
        got = send(after(part, ffn_second).astype(BF), axis_qk)
        sum_qk = [t[0] for t in sum_qk] + [got[..., :rows, :]]
        vec_terms = [t[0] for t in vec_terms] + [got[..., rows:, :]]
        sum_vo = swap(sum_vo, axis_vo, ffn_second)
    d_input = after(d_input, got, sum_vo[-1])
    grad_attn, sent = scatter_z([sum_qk, vec_terms, sum_vo], True)
    grad_ffn = after(total(grad_ffn), sent)
    grad_up, grad_down = grad_ffn[:ff_rows].T, grad_ffn[ff_rows:]
    layer_output = from_documents(group_head, after(out_own, grad_ffn), out_y, BF)
    grad_input = from_documents(group_head, *from_documents_y(d_input, local), F32)

    slots = length * layer_input.shape[1] * deep * 2
    rate = RATE_BASE / math.sqrt(slots)
    rate_out = rate * math.sqrt(LEN / 8.0)
    olds_qkv, olds_out = (w_qkv, mom_qkv, avg_qkv), (w_out, mom_out, avg_out)
    if in_kernel:
        (
            grad_qkv,
            new_qkv,
            new_mom_qkv,
            new_avg_qkv,
            grad_out,
            new_out,
            new_mom_out,
            new_avg_out,
            grad_vec,
        ) = advance_attention(
            grad_attn, olds_qkv, olds_out, (rate, rate_out), (layer_output, grad_input)
        )
        grad_vec = grad_vec[0, :vec_len]
    else:
        grad_attn = total(grad_attn)
        sum_qk, sum_vo = grad_attn[:rows], grad_attn[rows + 8 :]
        grad_qkv = jnp.stack([sum_qk[:, :head_cols], sum_qk[:, head_cols:], sum_vo[:, :head_cols]])
        grad_out = sum_vo[:, head_cols:].T
        grad_vec = grad_attn[rows, :vec_len]
        new_qkv, new_mom_qkv, new_avg_qkv = advance(
            w_qkv, grad_qkv, mom_qkv, avg_qkv, DECAY, rate
        )
        new_out, new_mom_out, new_avg_out = advance(
            w_out, grad_out, mom_out, avg_out, DECAY, rate_out
        )
    new_up, new_mom_up, new_avg_up = advance(w_up, grad_up, mom_up, avg_up, DECAY, rate)
    new_down, new_mom_down, new_avg_down = advance(
        w_down, grad_down, mom_down, avg_down, DECAY, rate
    )
    new_vec, new_mom_vec, new_avg_vec = advance(vectors, grad_vec, mom_vec, avg_vec, 0.0, rate)
    return (
        layer_output,
        grad_input,
        grad_qkv,
        grad_out,
        grad_up,
        grad_down,
        grad_vec,
        new_qkv,
        new_out,
        new_up,
        new_down,
        new_vec,
        new_mom_qkv,
        new_mom_out,
        new_mom_up,
        new_mom_down,
        new_mom_vec,
        new_avg_qkv,
        new_avg_out,
        new_avg_up,
        new_avg_down,
        new_avg_vec,
    )


def solution(mesh):
    dp, head = mesh.shape["dp"], mesh.shape["head"]
    fine = Mesh(mesh.devices.reshape(dp // 2, 2, head // 2, 2), ("z", "x", "y", "c"))
    dps, heads, every = ("z", "x"), ("y", "c"), ("z", "x", "y", "c")
    acts = P(heads, dps, None)
    weights = (P(None, dps, heads), P(heads, dps), P(None, every), P(every, None), P(every))
    return jax.shard_map(
        body,
        mesh=fine,
        in_specs=(acts, P(dps), acts) + weights * 3,
        out_specs=(acts, acts) + weights * 4,
        check_vma=False,
    )
```

```python
import functools
import math

import jax
import jax.numpy as jnp
from jax import lax
from jax.experimental import pallas as pl
from jax.experimental.pallas import tpu as pltpu
from jax.sharding import Mesh
from jax.sharding import PartitionSpec as P

D = 768
HD = 64
FF = 3072
LEN = 512

EPSILON = 1e-05
MOMENTUM = 0.9
AVERAGE = 0.9
DECAY = 0.01
RATE_BASE = 0.05

BF = jnp.bfloat16
F32 = jnp.float32
NT = (((1,), (1,)), ((), ()))
NN = (((1,), (0,)), ((), ()))


def send(values, axis, bit=1):
    return lax.ppermute(values, axis, [(i, i ^ bit) for i in range(lax.axis_size(axis))])


def corner(array):
    rows, columns = min(8, array.shape[-2]), min(128, array.shape[-1])
    return array.reshape(-1, *array.shape[-2:])[0, :rows, :columns]


def after(values, *others):
    def nothing(other, width):
        row = other.reshape(-1, other.shape[-1])[:1, :width].astype(F32) * 0.0
        return jnp.concatenate([row] * (width // row.shape[1]), 1)[0]

    def later(value):
        others_left = [nothing(v, value.shape[-1]) for v in jax.tree.leaves(others)]
        return value + sum(others_left).astype(value.dtype) if others_left else value

    return jax.tree.map(later, values)


def z_order(size):
    return jnp.array([0, 2, 1, 3]) if size == 4 else jnp.arange(size)


def flip_order(axis):
    size = lax.axis_size(axis)
    return lax.axis_index(axis) ^ z_order(size)


def gather_z(shard, before=()):
    size = lax.axis_size("z")
    if size != 4:
        whole = jnp.take(lax.all_gather(shard, "z"), flip_order("z"), axis=0)
        return whole, whole[0], whole[0]
    first = send(shard, "z", 2)
    pair = after(jnp.stack([shard, first], 0), before)
    second = send(pair, "z", 1)
    return jnp.concatenate([pair, second], 0), first, second


def total(terms):
    result = terms[0].astype(F32)
    for term in terms[1:]:
        result = result + term.astype(F32)
    return result


def swap(terms, axis, others=()):
    part = total([t[1] for t in terms])
    got = send(after(part, others).astype(BF), axis)
    return [t[0] for t in terms] + [got]


def scatter_z(sums, direct):
    joined = lambda index: jnp.concatenate([total([t[index] for t in terms]) for terms in sums], -2)
    if lax.axis_size("z") != 4:
        everything = jnp.take(joined(slice(None)).astype(BF), flip_order("z"), axis=0)
        parts = lax.all_to_all(everything, "z", 0, 0, tiled=True)
        return [total(list(parts[1:])), parts[0]], parts[0]
    if direct:
        parts = [joined(place).astype(BF) for place in (1, 2, 3)]
        return [joined(0)] + [send(part, "z", bit) for part, bit in zip(parts, (2, 1, 3))], parts[2]
    got = send(joined(slice(2, 4)).astype(BF), "z", 1)
    left, start = [], 0
    for terms in sums:
        end = start + terms[0].shape[-2]
        left.append([t[:2] for t in terms] + [got[:, start:end]])
        start = end
    sums = left
    part = joined(1).astype(BF)
    return [joined(0), send(part, "z", 2)], part


def to_documents(*arrays):
    y, c = lax.axis_index("y"), lax.axis_index("c")
    local, _, width = arrays[0].shape
    docs = [v.transpose(1, 0, 2).reshape(2, 2, local, width) for v in arrays]
    of = lambda v, index: lax.dynamic_index_in_dim(v, index, 0, keepdims=False)
    got_y = send(jnp.concatenate([of(v, 1 - y) for v in docs], 0), "y")
    pairs = [(of(v, y), got_y[2 * i : 2 * i + 2]) for i, v in enumerate(docs)]
    got = send(jnp.stack([of(v, 1 - c) for pair in pairs for v in pair], 0), "c")
    whole = [
        jnp.concatenate([of(pair[0], c), of(pair[1], c), got[2 * i], got[2 * i + 1]], 0)
        for i, pair in enumerate(pairs)
    ]
    return whole, got_y


def from_documents_y(values, local):
    values = values.reshape(2, 2, local, values.shape[1])
    return values[:, 0], send(values[:, 1], "y")


def assemble_kernel(seats_ref, own_ref, got_y_ref, got_c_ref, out_ref):
    for place, ref, part in ((0, own_ref, 0), (1, got_y_ref, 0), (2, got_c_ref, 0), (3, got_c_ref, 1)):
        out_ref[seats_ref[place]] = ref[part].astype(out_ref.dtype)


def from_documents(seats, own, got_y, dtype):
    got_c = send(jnp.stack([own[1], got_y[1]], 0), "c")
    vmem = pl.BlockSpec(memory_space=pltpu.VMEM)
    docs = pl.pallas_call(
        assemble_kernel,
        in_specs=[SMEM_SPEC, vmem, vmem, vmem],
        out_specs=vmem,
        out_shape=jax.ShapeDtypeStruct((4, *own.shape[1:]), dtype),
        compiler_params=params(12),
        cost_estimate=cost(0.0, 2.0, 0.0),
        name="assemble",
    )(seats, own, got_y, got_c)
    return docs.transpose(1, 0, 2)


def dot(a, b, dims):
    return lax.dot_general(a, b, dims, preferred_element_type=F32)


def normalized(values):
    center = values - jnp.mean(values, -1, keepdims=True)
    inverse = lax.rsqrt(jnp.mean(center * center, -1, keepdims=True) + EPSILON)
    return center * inverse, inverse


def norm_backward(d_result, normed, inverse, gain):
    d_normed = d_result * gain
    return inverse * (
        d_normed
        - jnp.mean(d_normed, -1, keepdims=True)
        - normed * jnp.mean(d_normed * normed, -1, keepdims=True)
    )


def block_start(place_ref, index, rows):
    start = place_ref[index] * rows
    return pl.multiple_of(start, 32) if rows % 32 == 0 else start


def place_weights(place_ref, group, qk_ref, vo_ref, w_qk, w_vo, rows):
    across, _, deep = qk_ref.shape[:3]
    for i in range(across):
        for k in range(deep):
            start = block_start(place_ref, i * deep + k, rows)
            w_qk[pl.ds(start, rows), :] = qk_ref[i, group, k, :rows]
            w_vo[pl.ds(start, rows), :] = vo_ref[group, i, k]


def attention_forward_kernel(rows, half, last, *refs):
    qk_ref, vo_ref, *refs = refs
    place_ref, x_ref, bias_ref, mask_ref, vec_ref = refs[:5]
    if last:
        mix_in, qkv_ref, lse_ref, context_ref = refs[5:9]
        h_ref, hb_ref, n_ref, inv_ref, xt_ref, w_qk, w_vo, mix_ref = refs[9:]
    else:
        mix_in = None
        qkv_ref, lse_ref, context_ref, mix_ref, w_qk, w_vo = refs[5:]
    x = x_ref[...]
    length = x.shape[0]
    width = w_qk.shape[1] // 2
    mix_ref[...] = jnp.zeros(mix_ref.shape, F32) if mix_in is None else mix_in[...]

    @pl.loop(0, 2)
    def _(group):
        place_weights(place_ref, group, qk_ref, vo_ref, w_qk, w_vo, rows)
        bias = bias_ref[half * 2 + group]
        qk = dot(x, w_qk[...], NN)
        v = (dot(x, w_vo[:, :width], NN) + bias[1:2, :width]).astype(BF)
        q = ((qk[:, :width] + bias[0:1, :width]).astype(BF).astype(F32) * HD ** (-0.5)).astype(BF)
        k = qk[:, width:].astype(BF)
        qkv_ref[group, :, :width] = q
        qkv_ref[group, :, width : 2 * width] = k
        qkv_ref[group, :, 2 * width :] = v
        mask = mask_ref[0:1]
        contexts, logs = [], []
        for head in range(width // HD):
            cols = slice(head * HD, (head + 1) * HD)
            s = dot(q[:, cols], k[:, cols], NT) + mask
            peak = jnp.max(s, -1, keepdims=True)
            total_exp = jnp.sum(jnp.exp(s - peak), -1, keepdims=True)
            log_total = peak + jnp.log(total_exp)
            p = jnp.exp(s - log_total).astype(BF)
            contexts.append(dot(p, v[:, cols], NN).astype(BF))
            logs.append(log_total)
        context = jnp.concatenate(contexts, 1)
        context_ref[group] = context
        lanes = lax.broadcasted_iota(jnp.int32, (length, 128), 1)
        packed = jnp.zeros((length, 128), F32)
        for head, log_total in enumerate(logs):
            packed = jnp.where(lanes == head, log_total, packed)
        lse_ref[group] = packed.T[:8]
        mix_ref[...] += dot(context, w_vo[:, width:], NT)

    if last:
        first_res = x_ref[...].astype(F32) + mix_ref[...] + vec_ref[2:3]
        normed, inverse = normalized(first_res)
        hidden = normed * vec_ref[3:4] + vec_ref[4:5]
        n_ref[...] = normed
        inv_ref[...] = jnp.broadcast_to(inverse, inv_ref.shape)
        h_ref[...] = hidden
        hb_ref[...] = hidden.astype(BF)
        xt_ref[...] = x_ref[...].T


def attention_backward_kernel(rows, last, *refs):
    qk_ref, vo_ref, *refs = refs
    place_ref, xt_ref, gr_ref, grt_ref, qkv_ref, lse_ref, context_ref = refs[:7]
    mask_ref, start_ref = refs[7:9]
    if last:
        grad_ref, bias_ref, out_ref, w_qk, w_vo, g_qkv, gin_ref = refs[9:]
    else:
        grad_ref, bias_ref, gin_ref, w_qk, w_vo, g_qkv = refs[9:]
    width = w_qk.shape[1] // 2
    gin_ref[...] = start_ref[...]

    @pl.loop(0, 2)
    def _(group):
        place_weights(place_ref, group, qk_ref, vo_ref, w_qk, w_vo, rows)
        gc = dot(gr_ref[...], w_vo[:, width:], NN).astype(BF)
        mask = mask_ref[:, :1]
        sums = []
        for head in range(width // HD):
            q = qkv_ref[group, :, head * HD : (head + 1) * HD]
            k = qkv_ref[group, :, width + head * HD : width + (head + 1) * HD]
            v = qkv_ref[group, :, 2 * width + head * HD : 2 * width + (head + 1) * HD]
            g = gc[:, head * HD : (head + 1) * HD]
            p = jnp.exp(dot(k, q, NT) + mask - lse_ref[group, head : head + 1])
            dp = dot(v, g, NT)
            gv = dot(p.astype(BF), g, NN)
            delta = jnp.sum(p * dp, 0, keepdims=True)
            gs = (p * (dp - delta)).astype(BF)
            gk = dot(gs, q, NN)
            gq = dot(gs.T, (k.astype(F32) * HD ** (-0.5)).astype(BF), NN)
            g_qkv[:, head * HD : (head + 1) * HD] = gq.astype(BF)
            g_qkv[:, width + head * HD : width + (head + 1) * HD] = gk.astype(BF)
            g_qkv[:, 2 * width + head * HD : 2 * width + (head + 1) * HD] = gv.astype(BF)
            sums.append((jnp.sum(gq, 0, keepdims=True), jnp.sum(gv, 0, keepdims=True)))
        bias_ref[group, 0:1, :] = jnp.concatenate([s[0] for s in sums], 1)
        bias_ref[group, 1:2, :] = jnp.concatenate([s[1] for s in sums], 1)
        g_qk = g_qkv[:, : 2 * width]
        g_v = g_qkv[:, 2 * width :]
        gin = dot(g_qk, w_qk[...], NT) + dot(g_v, w_vo[:, :width], NT)
        gin_ref[...] += gin

        w_qk[...] = dot(xt_ref[...], g_qk, NN).astype(BF)
        w_vo[:, :width] = dot(xt_ref[...], g_v, NN).astype(BF)
        w_vo[:, width:] = dot(grt_ref[...], context_ref[group], NN).astype(BF)
        across, deep = grad_ref.shape[1] // 2, grad_ref.shape[2]
        for i in range(across):
            for j in range(deep):
                start = block_start(place_ref, i * deep + j, rows)
                grad_ref[0, i * 2 + group, j] = w_qk[pl.ds(start, rows), :]
                grad_ref[1, group * across + i, j] = w_vo[pl.ds(start, rows), :]

    if last:
        out_ref[...] = gin_ref[...].astype(BF)


def ffn_weights(refs, chunk, step):
    x, y = step // 2, step % 2
    up = refs[x][y * chunk : (y + 1) * chunk]
    down = refs[2 + y][x * chunk : (x + 1) * chunk]
    return up, down


def ffn_forward_kernel(last, *refs):
    weights, refs = refs[:4], refs[4:]
    h_ref, hb_ref, bias_ref, vec_ref = refs[:4]
    if last:
        sum_in, act_ref, slope_ref, out_ref, n_ref, inv_ref, sum_ref = refs[4:]
    else:
        sum_in = None
        act_ref, slope_ref, sum_ref = refs[4:]
    chunk = weights[0].shape[0] // 2
    for step in range(4):
        up, down = ffn_weights(weights, chunk, step)
        columns = slice(step * chunk, (step + 1) * chunk)
        u = dot(hb_ref[...], up, NT) + bias_ref[0:1, columns]
        phi = 0.5 + 0.5 * lax.erf(u * 0.7071067811865476)
        act = (u * phi).astype(BF)
        act_ref[:, columns] = act
        slope = phi + u * jnp.exp(-0.5 * u * u) * 0.3989422804014327
        slope_ref[:, columns] = slope.astype(slope_ref.dtype)
        part = dot(act, down, NN)
        if step > 0:
            sum_ref[...] += part
        else:
            sum_ref[...] = part if sum_in is None else sum_in[...] + part
    if last:
        second_res = h_ref[...] + (sum_ref[...] + vec_ref[9:10])
        normed, inverse = normalized(second_res)
        out_ref[...] = (normed * vec_ref[10:11] + vec_ref[11:12]).astype(BF)
        n_ref[...] = normed
        inv_ref[...] = jnp.broadcast_to(inverse, inv_ref.shape)


def ffn_backward_kernel(last, *refs):
    weights, refs = refs[:4], refs[4:]
    hb_ref, act_ref, slope_ref, n_ref, inv_ref, vec_ref = refs[:6]
    if last:
        grb_ref, sum_in = refs[6:8]
        gu_ref, gd_ref, bias_ref, gr_ref, gr1b_ref, grt_ref, vec_out, sum_ref = refs[8:]
        sum_ref[...] = sum_in[...]
    else:
        cot_ref, mask_ref, gu_ref, gd_ref, bias_ref, grb_ref, vec_out, sum_ref = refs[6:]
        normed = n_ref[...]
        d_result = jnp.where(mask_ref[:, :1] == 0.0, cot_ref[...].astype(F32), 0.0)
        vec_out[0:1] = jnp.sum(d_result * normed, 0, keepdims=True)
        vec_out[1:2] = jnp.sum(d_result, 0, keepdims=True)
        d_second = norm_backward(d_result, normed, inv_ref[:, :1], vec_ref[10:11])
        vec_out[2:3] = jnp.sum(d_second, 0, keepdims=True)
        sum_ref[...] = d_second
        grb_ref[...] = d_second.astype(BF)
    chunk = weights[0].shape[0] // 2
    for step in range(4):
        up, down = ffn_weights(weights, chunk, step)
        columns = slice(step * chunk, (step + 1) * chunk)
        grb = grb_ref[...]
        d_up = dot(grb, down, NT) * slope_ref[:, columns].astype(F32)
        bias_ref[0:1, columns] = jnp.sum(d_up, 0, keepdims=True)
        d_up_b = d_up.astype(BF)
        crossed = (step % 2 * 2 + step // 2) * chunk
        gd_ref[crossed : crossed + chunk] = dot(act_ref[:, columns].T, grb, NN).astype(BF)
        gu_ref[step * chunk : (step + 1) * chunk] = dot(d_up_b.T, hb_ref[...], NN).astype(BF)
        sum_ref[...] += dot(d_up_b, up, NN)
    if last:
        d_hidden = sum_ref[...]
        normed = n_ref[...]
        vec_out[0:1] = jnp.sum(d_hidden * normed, 0, keepdims=True)
        vec_out[1:2] = jnp.sum(d_hidden, 0, keepdims=True)
        d_first = norm_backward(d_hidden, normed, inv_ref[:, :1], vec_ref[3:4])
        vec_out[2:3] = jnp.sum(d_first, 0, keepdims=True)
        gr_ref[...] = d_first
        gr1b_ref[...] = d_first.astype(BF)
        grt_ref[...] = d_first.astype(BF).T


VMEM_SPEC = pl.BlockSpec(memory_space=pltpu.VMEM)


def spread_vectors_kernel(
    owner_ref, heads_ref, own_ref, other_ref, rows_ref, up_ref, bias_ref, units
):
    _, across, _, deep = COUNTS
    unit = units.shape[1]
    for x in range(2):
        for y in range(2):
            for z in range(deep):
                for c in range(2):
                    index = ((c * across + x) * 2 + y) * deep + z
                    start = owner_ref[index] * 3
                    for i in range(3):
                        units[pl.ds(start + i, 1), :] = (own_ref, other_ref)[c][
                            x, y, z, 0:1, i * unit : (i + 1) * unit
                        ]
    per_row = D // unit
    for row in range(12):
        for i in range(per_row):
            rows_ref[row : row + 1, i * unit : (i + 1) * unit] = units[
                row * per_row + i : row * per_row + i + 1, :
            ]
    half = FF // 2
    for index in range(FF // unit):
        start = index * unit
        up_ref[start // half, 0:1, start % half : start % half + unit] = units[
            pl.ds(5 * per_row + owner_ref[index], 1), :
        ]
    width = bias_ref.shape[2]
    for group in range(4):
        for kind in range(2):
            for i in range(width // unit):
                start = kind * per_row + heads_ref[group] * (width // unit) + i
                bias_ref[group, kind : kind + 1, i * unit : (i + 1) * unit] = units[
                    pl.ds(start, 1), :
                ]


def collect_vectors_kernel(
    owner_ref, heads_ref, bias_0, bias_1, up_0, up_1, one_ref, two_ref, out_ref, units
):
    out_ref[...] = jnp.zeros(out_ref.shape, F32)
    unit = units.shape[1]
    per_row = D // unit
    width = bias_0.shape[2]
    for group in range(4):
        source = (bias_0, bias_1)[group // 2]
        for kind in range(2):
            for i in range(width // unit):
                start = kind * per_row + heads_ref[group] * (width // unit) + i
                units[pl.ds(start, 1), :] = source[
                    group % 2, kind : kind + 1, i * unit : (i + 1) * unit
                ]
    half = FF // 2
    for index in range(FF // unit):
        source = (up_0, up_1)[index * unit // half]
        start = index * unit % half
        units[pl.ds(5 * per_row + owner_ref[index], 1), :] = source[0:1, start : start + unit]
    for row, source, line in (
        (2, one_ref, 2),
        (3, one_ref, 0),
        (4, one_ref, 1),
        (9, two_ref, 2),
        (10, two_ref, 0),
        (11, two_ref, 1),
    ):
        for i in range(per_row):
            units[row * per_row + i : row * per_row + i + 1, :] = source[
                line : line + 1, i * unit : (i + 1) * unit
            ]
    for index in range(FF // unit):
        for i in range(3):
            out_ref[index, 0:1, i * unit : (i + 1) * unit] = units[
                pl.ds(owner_ref[index] * 3 + i, 1), :
            ]


COUNTS = (2, 2, 2, 4)


def spread_vectors(owner, heads, own, other, unit, width):
    outs = [like((12, D), F32), like((2, 8, FF // 2), F32), like((4, 8, width), F32)]
    return pl.pallas_call(
        spread_vectors_kernel,
        in_specs=[SMEM_SPEC, SMEM_SPEC] + [pl.BlockSpec(memory_space=pltpu.VMEM)] * 2,
        out_specs=[pl.BlockSpec(memory_space=pltpu.VMEM)] * 3,
        out_shape=outs,
        scratch_shapes=[pltpu.VMEM((12 * D // unit, unit), F32)],
        compiler_params=params(8),
        cost_estimate=cost(0.0, 0.5, 0.0),
        name="spread_vectors",
    )(owner, heads, own, other)


def collect_vectors(owner, heads, unit, pair, *sources):
    return pl.pallas_call(
        collect_vectors_kernel,
        in_specs=[SMEM_SPEC, SMEM_SPEC] + [pl.BlockSpec(memory_space=pltpu.VMEM)] * len(sources),
        out_specs=pl.BlockSpec(memory_space=pltpu.VMEM),
        out_shape=like((FF // unit, 8, pair), F32),
        scratch_shapes=[pltpu.VMEM((12 * D // unit, unit), F32)],
        compiler_params=params(8),
        cost_estimate=cost(0.0, 0.5, 0.0),
        name="collect_vectors",
    )(owner, heads, *sources)


def pack_attention_kernel(qkv_ref, out_ref, vec_ref, pack_ref):
    rows, width = qkv_ref.shape[1:]
    vec_len = vec_ref.shape[1]
    pack_ref[:rows, :width] = qkv_ref[0].astype(BF)
    pack_ref[:rows, width:] = qkv_ref[1].astype(BF)
    vec = jnp.concatenate([vec_ref[...], jnp.zeros((1, 2 * width - vec_len), F32)], 1)
    vec = jnp.concatenate([vec, jnp.zeros((7, 2 * width), F32)], 0)
    pack_ref[rows : rows + 8] = vec.astype(BF)
    pack_ref[rows + 8 :, :width] = qkv_ref[2].astype(BF)
    pack_ref[rows + 8 :, width:] = out_ref[...].T.astype(BF)


def pack_attention(qkv, out, vec):
    rows, width = qkv.shape[1:]
    return pl.pallas_call(
        pack_attention_kernel,
        in_specs=[VMEM_SPEC] * 3,
        out_specs=VMEM_SPEC,
        out_shape=like((2 * rows + 8, 2 * width), BF),
        compiler_params=params(8),
        cost_estimate=cost(0.0, 0.5, 0.0),
        name="pack_attention",
    )(qkv, out, vec)


def advance_attention_kernel(rates, count, *refs):
    terms, olds, outs = refs[:count], refs[count : count + 6], refs[count + 6 :]
    whole_sum = terms[0][...]
    for term in terms[1:]:
        whole_sum = whole_sum + term[...].astype(F32)
    rows, width = olds[0].shape[1], olds[0].shape[2]
    parts = [
        whole_sum[:rows, :width],
        whole_sum[:rows, width:],
        whole_sum[rows + 8 :, :width],
    ]
    for i, grad in enumerate(parts):
        new = advance(olds[0][i], grad, olds[1][i], olds[2][i], DECAY, rates[0])
        for ref, value in zip(outs[:4], (grad, *new)):
            ref[i] = value
    grad = whole_sum[rows + 8 :, width:].T
    new = advance(olds[3][...], grad, olds[4][...], olds[5][...], DECAY, rates[1])
    for ref, value in zip(outs[4:8], (grad, *new)):
        ref[...] = value
    outs[8][...] = whole_sum[rows : rows + 8]


def advance_attention(terms, qkv, out, rates, others):
    outs = [like(qkv[0].shape, F32)] * 4 + [like(out[0].shape, F32)] * 4
    outs.append(like((8, terms[0].shape[1]), F32))
    vmem = pl.BlockSpec(memory_space=pltpu.VMEM)
    kernel = functools.partial(advance_attention_kernel, rates, len(terms))
    kernel, corners, _ = waiting(kernel, others)
    return pl.pallas_call(
        kernel,
        in_specs=[vmem] * (len(corners) + len(terms) + 6),
        out_specs=[vmem] * 9,
        out_shape=outs,
        compiler_params=params(16),
        cost_estimate=cost(0.0, 3.0, 0.0),
        name="advance_attention",
    )(*corners, *terms, *qkv, *out)


def waiting(kernel, others):
    corners = [corner(v) for v in jax.tree.leaves(others)]
    count = len(corners)
    return lambda *refs: kernel(*refs[count:]), corners, [VMEM_SPEC] * count


SMEM_SPEC = pl.BlockSpec(memory_space=pltpu.SMEM)
like = jax.ShapeDtypeStruct


def params(mib):
    return pltpu.CompilerParams(vmem_limit_bytes=mib << 20)


def cost(giga_flops, mega_bytes, mega_exps):
    return pl.CostEstimate(
        flops=int(giga_flops * 1e9),
        bytes_accessed=int(mega_bytes * 1e6),
        transcendentals=int(mega_exps * 1e6),
    )


def attention_forward(place, x, weights, biases, half, mask, vec_rows, mix, rows):
    length = x.shape[0]
    pair = weights[0].shape[4]
    width = pair // 2
    last = mix is not None
    row = like((length, D), F32)
    outs = [
        like((2, length, 3 * width), BF),
        like((2, 8, length), F32),
        like((2, length, width), BF),
    ]
    tail = [row]
    scratch = [pltpu.VMEM((D, pair), BF), pltpu.VMEM((D, pair), BF)]
    operands = [*weights, place, x, biases, mask, vec_rows]
    if last:
        low = like((length, D), BF)
        tail = [row, low, row, like((length, 128), F32), like((D, length), BF)]
        operands.append(mix)
        scratch.append(pltpu.VMEM((length, D), F32))
    return pl.pallas_call(
        functools.partial(attention_forward_kernel, rows, half, last),
        in_specs=[SMEM_SPEC if v is place else VMEM_SPEC for v in operands],
        out_specs=[VMEM_SPEC] * len(outs + tail),
        out_shape=outs + tail,
        scratch_shapes=scratch,
        compiler_params=params(14),
        cost_estimate=cost(4.5, 6.0, 3.1),
        name="attention_forward_last" if last else "attention_forward",
    )(*operands)


def attention_backward(place, x_t, gr, gr_t, weights, saved, mask, start, rows, last, others):
    length = gr.shape[0]
    pair = weights[0].shape[4]
    width = pair // 2
    across, _, deep = weights[0].shape[:3]
    qkv, lse, context = saved
    outs = [
        like((2, 2 * across, deep, rows, pair), BF),
        like((2, 8, width), F32),
        like((length, D), BF if last else F32),
    ]
    scratch = [
        pltpu.VMEM((D, pair), BF),
        pltpu.VMEM((D, pair), BF),
        pltpu.VMEM((length, 3 * width), BF),
    ]
    if last:
        scratch.append(pltpu.VMEM((length, D), F32))
    kernel = functools.partial(attention_backward_kernel, rows, last)
    kernel, corners, corner_specs = waiting(kernel, others)
    return pl.pallas_call(
        kernel,
        in_specs=corner_specs + [VMEM_SPEC] * 2 + [SMEM_SPEC] + [VMEM_SPEC] * 8,
        out_specs=[VMEM_SPEC] * 3,
        out_shape=outs,
        scratch_shapes=scratch,
        compiler_params=params(14),
        cost_estimate=cost(0.5, 1.0, 0.1),
        name="attention_backward_last" if last else "attention_backward",
    )(*corners, *weights, place, x_t, gr, gr_t, qkv, lse, context, mask, start)


def ffn_forward(h, hb, up, down, bias, vec_rows, tail_operands):
    length = h.shape[0]
    hidden = 2 * up[0].shape[0]
    last = len(tail_operands) > 0
    row = like((length, D), F32)
    outs = [like((length, hidden), BF), like((length, hidden), BF)]
    tail = [row]
    scratch = []
    if last:
        tail = [like((length, D), BF), row, like((length, 128), F32)]
        scratch = [pltpu.VMEM((length, D), F32)]
    return pl.pallas_call(
        functools.partial(ffn_forward_kernel, last),
        in_specs=[VMEM_SPEC] * (8 + len(tail_operands)),
        out_specs=[VMEM_SPEC] * len(outs + tail),
        out_shape=outs + tail,
        scratch_shapes=scratch,
        compiler_params=params(14),
        cost_estimate=cost(4.9, 12.0, 1.6),
        name="ffn_forward_last" if last else "ffn_forward",
    )(*up, *down, h, hb, bias, vec_rows, *tail_operands)


def ffn_backward(hb, act, slope, up, down, norm, tail_operands, last):
    length = hb.shape[0]
    hidden = 2 * up[0].shape[0]
    row = like((length, D), F32)
    low = like((length, D), BF)
    grad = like((hidden, D), BF)
    outs = [grad, grad, like((8, hidden), F32)]
    vector = like((8, D), F32)
    tail = [row, low, like((D, length), BF), vector] if last else [low, vector, row]
    return pl.pallas_call(
        functools.partial(ffn_backward_kernel, last),
        in_specs=[VMEM_SPEC] * (7 + len(norm) + len(tail_operands)),
        out_specs=[VMEM_SPEC] * len(outs + tail),
        out_shape=outs + tail,
        scratch_shapes=[pltpu.VMEM((length, D), F32)] if last else [],
        compiler_params=params(14),
        cost_estimate=cost(9.7, 16.0, 0.0),
        name="ffn_backward_last" if last else "ffn_backward",
    )(*up, *down, hb, act, slope, *norm, *tail_operands)


def advance(weight, grad, moment, average, decay, rate):
    step_grad = grad + decay * weight
    moment_new = MOMENTUM * moment + step_grad
    weight_new = weight - rate * (step_grad + MOMENTUM * moment_new)
    average_new = AVERAGE * average + (1.0 - AVERAGE) * weight_new
    return (weight_new, moment_new, average_new)


def body(
    layer_input,
    lengths,
    cotangent,
    w_qkv,
    w_out,
    w_up,
    w_down,
    vectors,
    mom_qkv,
    mom_out,
    mom_up,
    mom_down,
    mom_vec,
    avg_qkv,
    avg_out,
    avg_up,
    avg_down,
    avg_vec,
):
    z, x, y, c = (lax.axis_index(a) for a in ("z", "x", "y", "c"))
    deep = lax.axis_size("z")
    blocks = deep * 8
    rows, head_cols = w_qkv.shape[1], w_qkv.shape[2]
    pair = 2 * head_cols
    vec_len = vectors.shape[0]
    ff_rows = w_up.shape[1]
    local = layer_input.shape[0]
    length = 4 * local

    kc, kx, ky, kz = jnp.meshgrid(
        jnp.arange(2), jnp.arange(2), jnp.arange(2), z_order(deep), indexing="ij"
    )
    owner = (((z ^ kz) * 2 + (x ^ kx)) * 4 + (y ^ ky) * 2 + (c ^ kc)).reshape(blocks)
    tz, tx, ty, tc = jnp.meshgrid(
        jnp.arange(deep), jnp.arange(2), jnp.arange(2), jnp.arange(2), indexing="ij"
    )
    seat = ((((c ^ tc) * 2 + (x ^ tx)) * 2 + (y ^ ty)) * deep + z_order(deep)[z ^ tz]).reshape(blocks)
    first, second = jnp.meshgrid(jnp.arange(2), jnp.arange(2), indexing="ij")
    group_head = ((y ^ second) * 2 + (c ^ first)).reshape(4)
    head_group = ((c ^ second) * 2 + (y ^ first)).reshape(4)

    in_kernel = rows % 32 == 0 and deep == COUNTS[3]
    owner, group_head = owner.astype(jnp.int32), group_head.astype(jnp.int32)

    if in_kernel:
        pack = pack_attention(w_qkv, w_out, vectors.reshape(1, vec_len))
    else:
        vec_rows = jnp.pad(vectors.astype(BF)[None], ((0, 7), (0, pair - vec_len)))
        pack_qk = jnp.concatenate([w_qkv[0], w_qkv[1]], 1).astype(BF)
        pack_vo = jnp.concatenate([w_qkv[2], w_out.T], 1).astype(BF)
        pack = jnp.concatenate([pack_qk, vec_rows, pack_vo], 0)
    (doc_x, doc_cot), x_y = to_documents(layer_input, cotangent)
    attn_z, z_first, z_second = gather_z(pack)
    qk, vo = attn_z[:, : rows + 8], attn_z[:, rows + 8 :]
    first_sent = (qk, vo)
    qk_first, vo_first = send(qk, "y"), send(vo, "x")
    qk = after(jnp.stack([qk, qk_first], 0), vo_first, x_y)
    vo = after(jnp.stack([vo, vo_first], 0), qk_first)
    qk_got, vo_got = send(qk, "x"), send(vo, "y")
    qk, vo = jnp.stack([qk, qk_got], 0), jnp.stack([vo, vo_got], 0)
    qk_other, vo_other = send(qk, "c"), send(vo, "c")

    pack = jnp.concatenate([w_up.T.astype(BF), w_down.astype(BF)], 0)
    ffn_z, _, _ = gather_z(after(pack, z_first), first_sent)
    up, down = ffn_z[:, :ff_rows], ffn_z[:, ff_rows:]
    up_got, down_got = send(up, "y"), send(down, "x")
    up, down = (
        after(jnp.stack([up, up_got], 0), down_got, qk_got, vo_got),
        after(jnp.stack([down, down_got], 0), up_got, qk_got, vo_got),
    )
    up_got, down_got = send(up, "x"), send(down, "y")

    vec_own, vec_other = (v[..., rows:, :].astype(F32) for v in (qk, qk_other))
    if in_kernel:
        vec_rows, bias_up, biases = spread_vectors(
            owner, group_head, vec_own, vec_other, ff_rows, head_cols
        )
    else:
        vec_all = jnp.stack([v[..., 0, :vec_len] for v in (vec_own, vec_other)], 0)
        vec_all = vec_all.reshape(blocks, vec_len)
        vec_rows = jnp.take(vec_all, seat, axis=0).reshape(12, D)
        bias_up = jnp.take(vec_rows[5:9].reshape(blocks, ff_rows), owner, axis=0)
        bias_up = jnp.pad(bias_up.reshape(2, 1, FF // 2), ((0, 0), (0, 7), (0, 0)))
        bias_q = jnp.take(vec_rows[0].reshape(4, head_cols), group_head, axis=0)
        bias_v = jnp.take(vec_rows[1].reshape(4, head_cols), group_head, axis=0)
        biases = jnp.pad(jnp.stack([bias_q, bias_v], 1), ((0, 0), (0, 6), (0, 0)))

    row = jnp.arange(length)
    part = row // local
    position = ((y ^ (part % 2)) * 2 + (c ^ (part // 2))) * local + row % local
    doc_len = lax.dynamic_index_in_dim(lengths, y * 2 + c, 0, keepdims=False)
    alive = position < doc_len
    mask = jnp.where(alive, 0.0, -1e30).astype(F32)
    mask_row = jnp.broadcast_to(mask[None, :], (8, length))
    mask_col = jnp.broadcast_to(mask[:, None], (length, 128))

    if in_kernel:
        zs = flip_order("z")[None, :]
        place = (zs * 2 + (x ^ jnp.arange(2)[:, None])).reshape(2 * deep)
        kernel_rows = rows
    else:
        xs = x ^ jnp.arange(2)
        zs = flip_order("z")

        def true_order(qk, vo):
            qk = jnp.take(jnp.take(qk[..., :rows, :], xs, axis=0), zs, axis=2)
            vo = jnp.take(jnp.take(vo, xs, axis=1), zs, axis=2)
            qk, vo = qk.transpose(1, 2, 0, 3, 4), vo.transpose(0, 2, 1, 3, 4)
            return qk.reshape(1, 2, 1, D, pair), vo.reshape(2, 1, 1, D, pair)

        def relative_order(qk, vo):
            qk = qk.reshape(2, deep, 2, rows, pair).transpose(2, 0, 1, 3, 4)
            vo = vo.reshape(2, deep, 2, rows, pair).transpose(0, 2, 1, 3, 4)
            qk = jnp.take(jnp.take(qk, xs, axis=0), zs, axis=2)
            return qk, jnp.take(jnp.take(vo, xs, axis=1), zs, axis=2)

        place = jnp.zeros((1,), jnp.int32)
        qk, vo = true_order(qk, vo)
        qk_other, vo_other = true_order(qk_other, vo_other)
        kernel_rows = D
    place = place.astype(jnp.int32)

    *saved_0, mix = attention_forward(
        place, doc_x, (qk, vo), biases, 0, mask_row, vec_rows, None, kernel_rows
    )
    *saved_1, hidden, hidden_b, normed, inverse, x_t = attention_forward(
        place, doc_x, (qk_other, vo_other), biases, 1, mask_row, vec_rows, mix, kernel_rows
    )
    flat = lambda v: v.reshape(FF // 4, D)
    up_own, down_own = (flat(up), flat(up_got)), (flat(down), flat(down_got))
    up_other = (send(up_own[0], "c"), send(after(up_own[1], hidden_b), "c"))
    down_other = (send(down_own[0], "c"), send(after(down_own[1], hidden_b), "c"))
    act_0, slope_0, mix = ffn_forward(
        hidden, hidden_b, up_own, down_own, bias_up[0], vec_rows, ()
    )
    act_1, slope_1, result, normed_two, inverse_two = ffn_forward(
        hidden, hidden_b, up_other, down_other, bias_up[1], vec_rows, (mix,)
    )
    out_own, out_y = from_documents_y(result, local)

    lead = (2, 2, deep, ff_rows, D)
    norm_two = (normed_two, inverse_two, vec_rows)
    up_1, down_1, d_bias_1, d_second_b, vec_two, d_hidden = ffn_backward(
        hidden_b, act_1, slope_1, up_other, down_other, norm_two, (doc_cot, mask_col), False
    )
    up_1, down_1 = send(up_1, "c"), send(down_1, "c")
    norm_one = (normed, inverse, vec_rows)
    up_0, down_0, d_bias_0, d_first, d_first_b, d_first_t, vec_one = ffn_backward(
        hidden_b, act_0, slope_0, up_own, down_own, norm_one, (d_second_b, d_hidden), True
    )
    grad_up = swap([up_0.reshape(lead), up_1.reshape(lead)], "x")
    grad_down = swap([down_0.reshape(lead), down_1.reshape(lead)], "y")
    ffn_c = (up_1, down_1)
    ffn_big = (grad_up[-1], grad_down[-1])
    grad_up, grad_down = swap(grad_up, "y"), swap(grad_down, "x")
    ffn_second = (grad_up[-1], grad_down[-1])
    grad_ffn, _ = scatter_z([grad_up, grad_down], False)

    attn_1, bias_1, d_attn = attention_backward(
        place, x_t, d_first_b, d_first_t, (qk_other, vo_other), saved_1, mask_col, d_first, kernel_rows, False, ffn_c
    )
    attn_0, bias_0, d_input = attention_backward(
        place, x_t, d_first_b, d_first_t, (qk, vo), saved_0, mask_col, d_attn, kernel_rows, True, (after(corner(out_y), bias_1[0]),)
    )
    attn_1 = send(attn_1, "c")
    if in_kernel:
        pairs = [v.reshape(2, 2, 2, deep, rows, pair) for v in (attn_0, attn_1)]
    else:
        pairs = [relative_order(v[0], v[1]) for v in (attn_0, attn_1)]
    (qk_0, vo_0), (qk_1, vo_1) = pairs

    bias_0 = after(bias_0, ffn_big)
    if in_kernel:
        vec_part = collect_vectors(
            owner, group_head, ff_rows, pair, bias_0, bias_1, d_bias_0, d_bias_1, vec_one, vec_two
        ).reshape(2, 2, 2, deep, 8, pair)
    else:
        d_bias = jnp.concatenate([bias_0, bias_1], 0)
        d_bias_q = jnp.take(d_bias[:, 0], head_group, axis=0).reshape(D)
        d_bias_v = jnp.take(d_bias[:, 1], head_group, axis=0).reshape(D)
        d_bias_up = jnp.concatenate([d_bias_0[0], d_bias_1[0]]).reshape(blocks, ff_rows)
        d_bias_up = jnp.take(d_bias_up, seat, axis=0).reshape(FF)
        grad_vec = jnp.concatenate(
            [
                d_bias_q,
                d_bias_v,
                vec_one[2],
                vec_one[0],
                vec_one[1],
                d_bias_up,
                vec_two[2],
                vec_two[0],
                vec_two[1],
            ]
        )
        vec_part = jnp.take(grad_vec.reshape(blocks, vec_len), owner, axis=0)
        vec_part = jnp.pad(vec_part, ((0, 0), (0, pair - vec_len))).reshape(2, 2, 2, deep, 1, pair)
        vec_part = jnp.pad(vec_part, ((0, 0),) * 4 + ((0, 7), (0, 0)))
    vec_part = vec_part[0] + send(vec_part[1], "c")
    sum_qk, vec_terms, sum_vo = [qk_0, qk_1], [vec_part], [vo_0, vo_1]
    for axis_qk, axis_vo in (("x", "y"), ("y", "x")):
        part = jnp.concatenate(
            [total([t[1] for t in sum_qk]), total([t[1] for t in vec_terms])], -2
        )
        got = send(after(part, ffn_second).astype(BF), axis_qk)
        sum_qk = [t[0] for t in sum_qk] + [got[..., :rows, :]]
        vec_terms = [t[0] for t in vec_terms] + [got[..., rows:, :]]
        sum_vo = swap(sum_vo, axis_vo, ffn_second)
    d_input = after(d_input, got, sum_vo[-1])
    grad_attn, sent = scatter_z([sum_qk, vec_terms, sum_vo], True)
    grad_ffn = after(total(grad_ffn), sent)
    grad_up, grad_down = grad_ffn[:ff_rows].T, grad_ffn[ff_rows:]
    layer_output = from_documents(group_head, after(out_own, grad_ffn), out_y, BF)
    grad_input = from_documents(group_head, *from_documents_y(d_input, local), F32)

    slots = length * layer_input.shape[1] * deep * 2
    rate = RATE_BASE / math.sqrt(slots)
    rate_out = rate * math.sqrt(LEN / 8.0)
    olds_qkv, olds_out = (w_qkv, mom_qkv, avg_qkv), (w_out, mom_out, avg_out)
    if in_kernel:
        (
            grad_qkv,
            new_qkv,
            new_mom_qkv,
            new_avg_qkv,
            grad_out,
            new_out,
            new_mom_out,
            new_avg_out,
            grad_vec,
        ) = advance_attention(
            grad_attn, olds_qkv, olds_out, (rate, rate_out), (layer_output, grad_input)
        )
        grad_vec = grad_vec[0, :vec_len]
    else:
        grad_attn = total(grad_attn)
        sum_qk, sum_vo = grad_attn[:rows], grad_attn[rows + 8 :]
        grad_qkv = jnp.stack([sum_qk[:, :head_cols], sum_qk[:, head_cols:], sum_vo[:, :head_cols]])
        grad_out = sum_vo[:, head_cols:].T
        grad_vec = grad_attn[rows, :vec_len]
        new_qkv, new_mom_qkv, new_avg_qkv = advance(
            w_qkv, grad_qkv, mom_qkv, avg_qkv, DECAY, rate
        )
        new_out, new_mom_out, new_avg_out = advance(
            w_out, grad_out, mom_out, avg_out, DECAY, rate_out
        )
    new_up, new_mom_up, new_avg_up = advance(w_up, grad_up, mom_up, avg_up, DECAY, rate)
    new_down, new_mom_down, new_avg_down = advance(
        w_down, grad_down, mom_down, avg_down, DECAY, rate
    )
    new_vec, new_mom_vec, new_avg_vec = advance(vectors, grad_vec, mom_vec, avg_vec, 0.0, rate)
    return (
        layer_output,
        grad_input,
        grad_qkv,
        grad_out,
        grad_up,
        grad_down,
        grad_vec,
        new_qkv,
        new_out,
        new_up,
        new_down,
        new_vec,
        new_mom_qkv,
        new_mom_out,
        new_mom_up,
        new_mom_down,
        new_mom_vec,
        new_avg_qkv,
        new_avg_out,
        new_avg_up,
        new_avg_down,
        new_avg_vec,
    )


def solution(mesh):
    dp, head = mesh.shape["dp"], mesh.shape["head"]
    fine = Mesh(mesh.devices.reshape(dp // 2, 2, head // 2, 2), ("z", "x", "y", "c"))
    dps, heads, every = ("z", "x"), ("y", "c"), ("z", "x", "y", "c")
    acts = P(heads, dps, None)
    weights = (P(None, dps, heads), P(heads, dps), P(None, every), P(every, None), P(every))
    return jax.shard_map(
        body,
        mesh=fine,
        in_specs=(acts, P(dps), acts) + weights * 3,
        out_specs=(acts, acts) + weights * 4,
        check_vma=False,
    )
```

```python
import functools
import math

import jax
import jax.numpy as jnp
from jax import lax
from jax.experimental import pallas as pl
from jax.experimental.pallas import tpu as pltpu
from jax.sharding import Mesh
from jax.sharding import PartitionSpec as P

D = 768
HD = 64
FF = 3072
LEN = 512

EPSILON = 1e-05
MOMENTUM = 0.9
AVERAGE = 0.9
DECAY = 0.01
RATE_BASE = 0.05

BF = jnp.bfloat16
F32 = jnp.float32
NT = (((1,), (1,)), ((), ()))
NN = (((1,), (0,)), ((), ()))


def send(values, axis, bit=1):
    return lax.ppermute(values, axis, [(i, i ^ bit) for i in range(lax.axis_size(axis))])


def corner(array):
    rows, columns = min(8, array.shape[-2]), min(128, array.shape[-1])
    return array.reshape(-1, *array.shape[-2:])[0, :rows, :columns]


def after(values, *others):
    def nothing(other, width):
        row = other.reshape(-1, other.shape[-1])[:1, :width].astype(F32) * 0.0
        return jnp.concatenate([row] * (width // row.shape[1]), 1)[0]

    def later(value):
        others_left = [nothing(v, value.shape[-1]) for v in jax.tree.leaves(others)]
        return value + sum(others_left).astype(value.dtype) if others_left else value

    return jax.tree.map(later, values)


def z_order(size):
    return jnp.array([0, 2, 1, 3]) if size == 4 else jnp.arange(size)


def flip_order(axis):
    size = lax.axis_size(axis)
    return lax.axis_index(axis) ^ z_order(size)


def gather_z(shard, before=(), apart=False):
    size = lax.axis_size("z")
    if size != 4:
        whole = jnp.take(lax.all_gather(shard, "z"), flip_order("z"), axis=0)
        return ((whole,), whole[0]) if apart else (whole, whole[0], whole[0])
    first = send(shard, "z", 2)
    pair = after(jnp.stack([shard, first], 0), before)
    second = send(pair, "z", 1)
    if apart:
        return (pair, second), first
    return jnp.concatenate([pair, second], 0), first, second


def total(terms):
    result = terms[0].astype(F32)
    for term in terms[1:]:
        result = result + term.astype(F32)
    return result


def swap(terms, axis, others=()):
    part = total([t[1] for t in terms])
    got = send(after(part, others).astype(BF), axis)
    return [t[0] for t in terms] + [got]


def scatter_z(sums, direct):
    joined = lambda index: jnp.concatenate([total([t[index] for t in terms]) for terms in sums], -2)
    if lax.axis_size("z") != 4:
        everything = jnp.take(joined(slice(None)).astype(BF), flip_order("z"), axis=0)
        parts = lax.all_to_all(everything, "z", 0, 0, tiled=True)
        return [total(list(parts[1:])), parts[0]], parts[0]
    if direct:
        parts = [joined(place).astype(BF) for place in (1, 2, 3)]
        return [joined(0)] + [send(part, "z", bit) for part, bit in zip(parts, (2, 1, 3))], parts[2]
    got = send(joined(slice(2, 4)).astype(BF), "z", 1)
    left, start = [], 0
    for terms in sums:
        end = start + terms[0].shape[-2]
        left.append([t[:2] for t in terms] + [got[:, start:end]])
        start = end
    sums = left
    part = joined(1).astype(BF)
    return [joined(0), send(part, "z", 2)], part


def to_documents(*arrays):
    y, c = lax.axis_index("y"), lax.axis_index("c")
    local, _, width = arrays[0].shape
    docs = [v.transpose(1, 0, 2).reshape(2, 2, local, width) for v in arrays]
    of = lambda v, index: lax.dynamic_index_in_dim(v, index, 0, keepdims=False)
    got_y = send(jnp.concatenate([of(v, 1 - y) for v in docs], 0), "y")
    pairs = [(of(v, y), got_y[2 * i : 2 * i + 2]) for i, v in enumerate(docs)]
    got = send(jnp.stack([of(v, 1 - c) for pair in pairs for v in pair], 0), "c")
    whole = [
        jnp.concatenate([of(pair[0], c), of(pair[1], c), got[2 * i], got[2 * i + 1]], 0)
        for i, pair in enumerate(pairs)
    ]
    return whole, got_y


def from_documents_y(values, local):
    values = values.reshape(2, 2, local, values.shape[1])
    return values[:, 0], send(values[:, 1], "y")


def assemble_kernel(seats_ref, own_ref, got_y_ref, got_c_ref, out_ref):
    for place, ref, part in ((0, own_ref, 0), (1, got_y_ref, 0), (2, got_c_ref, 0), (3, got_c_ref, 1)):
        out_ref[seats_ref[place]] = ref[part].astype(out_ref.dtype)


def from_documents(seats, own, got_y, dtype):
    got_c = send(jnp.stack([own[1], got_y[1]], 0), "c")
    vmem = pl.BlockSpec(memory_space=pltpu.VMEM)
    docs = pl.pallas_call(
        assemble_kernel,
        in_specs=[SMEM_SPEC, vmem, vmem, vmem],
        out_specs=vmem,
        out_shape=jax.ShapeDtypeStruct((4, *own.shape[1:]), dtype),
        compiler_params=params(12),
        cost_estimate=cost(0.0, 2.0, 0.0),
        name="assemble",
    )(seats, own, got_y, got_c)
    return docs.transpose(1, 0, 2)


def dot(a, b, dims):
    return lax.dot_general(a, b, dims, preferred_element_type=F32)


def normalized(values):
    center = values - jnp.mean(values, -1, keepdims=True)
    inverse = lax.rsqrt(jnp.mean(center * center, -1, keepdims=True) + EPSILON)
    return center * inverse, inverse


def norm_backward(d_result, normed, inverse, gain):
    d_normed = d_result * gain
    return inverse * (
        d_normed
        - jnp.mean(d_normed, -1, keepdims=True)
        - normed * jnp.mean(d_normed * normed, -1, keepdims=True)
    )


def block_start(place_ref, index, rows):
    start = place_ref[index] * rows
    return pl.multiple_of(start, 32) if rows % 32 == 0 else start


def place_weights(place_ref, group, qk_ref, vo_ref, w_qk, w_vo, rows):
    across, _, deep = qk_ref.shape[:3]
    for i in range(across):
        for k in range(deep):
            start = block_start(place_ref, i * deep + k, rows)
            w_qk[pl.ds(start, rows), :] = qk_ref[i, group, k, :rows]
            w_vo[pl.ds(start, rows), :] = vo_ref[group, i, k]


def attention_forward_kernel(rows, half, last, *refs):
    qk_ref, vo_ref, *refs = refs
    place_ref, x_ref, bias_ref, mask_ref, vec_ref = refs[:5]
    if last:
        mix_in, qkv_ref, lse_ref, context_ref = refs[5:9]
        h_ref, hb_ref, n_ref, inv_ref, xt_ref, w_qk, w_vo, mix_ref = refs[9:]
    else:
        mix_in = None
        qkv_ref, lse_ref, context_ref, mix_ref, w_qk, w_vo = refs[5:]
    x = x_ref[...]
    length = x.shape[0]
    width = w_qk.shape[1] // 2
    mix_ref[...] = jnp.zeros(mix_ref.shape, F32) if mix_in is None else mix_in[...]

    @pl.loop(0, 2)
    def _(group):
        place_weights(place_ref, group, qk_ref, vo_ref, w_qk, w_vo, rows)
        bias = bias_ref[half * 2 + group]
        qk = dot(x, w_qk[...], NN)
        v = (dot(x, w_vo[:, :width], NN) + bias[1:2, :width]).astype(BF)
        q = ((qk[:, :width] + bias[0:1, :width]).astype(BF).astype(F32) * HD ** (-0.5)).astype(BF)
        k = qk[:, width:].astype(BF)
        qkv_ref[group, :, :width] = q
        qkv_ref[group, :, width : 2 * width] = k
        qkv_ref[group, :, 2 * width :] = v
        mask = mask_ref[0:1]
        contexts, logs = [], []
        for head in range(width // HD):
            cols = slice(head * HD, (head + 1) * HD)
            s = dot(q[:, cols], k[:, cols], NT) + mask
            peak = jnp.max(s, -1, keepdims=True)
            total_exp = jnp.sum(jnp.exp(s - peak), -1, keepdims=True)
            log_total = peak + jnp.log(total_exp)
            p = jnp.exp(s - log_total).astype(BF)
            contexts.append(dot(p, v[:, cols], NN).astype(BF))
            logs.append(log_total)
        context = jnp.concatenate(contexts, 1)
        context_ref[group] = context
        lanes = lax.broadcasted_iota(jnp.int32, (length, 128), 1)
        packed = jnp.zeros((length, 128), F32)
        for head, log_total in enumerate(logs):
            packed = jnp.where(lanes == head, log_total, packed)
        lse_ref[group] = packed.T[:8]
        mix_ref[...] += dot(context, w_vo[:, width:], NT)

    if last:
        first_res = x_ref[...].astype(F32) + mix_ref[...] + vec_ref[2:3]
        normed, inverse = normalized(first_res)
        hidden = normed * vec_ref[3:4] + vec_ref[4:5]
        n_ref[...] = normed
        inv_ref[...] = jnp.broadcast_to(inverse, inv_ref.shape)
        h_ref[...] = hidden
        hb_ref[...] = hidden.astype(BF)
        xt_ref[...] = x_ref[...].T


def attention_backward_kernel(rows, last, *refs):
    qk_ref, vo_ref, *refs = refs
    place_ref, xt_ref, gr_ref, grt_ref, qkv_ref, lse_ref, context_ref = refs[:7]
    mask_ref, start_ref = refs[7:9]
    if last:
        grad_ref, bias_ref, out_ref, w_qk, w_vo, g_qkv, gin_ref = refs[9:]
    else:
        grad_ref, bias_ref, gin_ref, w_qk, w_vo, g_qkv = refs[9:]
    width = w_qk.shape[1] // 2
    gin_ref[...] = start_ref[...]

    @pl.loop(0, 2)
    def _(group):
        place_weights(place_ref, group, qk_ref, vo_ref, w_qk, w_vo, rows)
        gc = dot(gr_ref[...], w_vo[:, width:], NN).astype(BF)
        mask = mask_ref[:, :1]
        sums = []
        for head in range(width // HD):
            q = qkv_ref[group, :, head * HD : (head + 1) * HD]
            k = qkv_ref[group, :, width + head * HD : width + (head + 1) * HD]
            v = qkv_ref[group, :, 2 * width + head * HD : 2 * width + (head + 1) * HD]
            g = gc[:, head * HD : (head + 1) * HD]
            p = jnp.exp(dot(k, q, NT) + mask - lse_ref[group, head : head + 1])
            dp = dot(v, g, NT)
            gv = dot(p.astype(BF), g, NN)
            delta = jnp.sum(p * dp, 0, keepdims=True)
            gs = (p * (dp - delta)).astype(BF)
            gk = dot(gs, q, NN)
            gq = dot(gs.T, (k.astype(F32) * HD ** (-0.5)).astype(BF), NN)
            g_qkv[:, head * HD : (head + 1) * HD] = gq.astype(BF)
            g_qkv[:, width + head * HD : width + (head + 1) * HD] = gk.astype(BF)
            g_qkv[:, 2 * width + head * HD : 2 * width + (head + 1) * HD] = gv.astype(BF)
            sums.append((jnp.sum(gq, 0, keepdims=True), jnp.sum(gv, 0, keepdims=True)))
        bias_ref[group, 0:1, :] = jnp.concatenate([s[0] for s in sums], 1)
        bias_ref[group, 1:2, :] = jnp.concatenate([s[1] for s in sums], 1)
        g_qk = g_qkv[:, : 2 * width]
        g_v = g_qkv[:, 2 * width :]
        gin = dot(g_qk, w_qk[...], NT) + dot(g_v, w_vo[:, :width], NT)
        gin_ref[...] += gin

        w_qk[...] = dot(xt_ref[...], g_qk, NN).astype(BF)
        w_vo[:, :width] = dot(xt_ref[...], g_v, NN).astype(BF)
        w_vo[:, width:] = dot(grt_ref[...], context_ref[group], NN).astype(BF)
        across, deep = grad_ref.shape[1] // 2, grad_ref.shape[2]
        for i in range(across):
            for j in range(deep):
                start = block_start(place_ref, i * deep + j, rows)
                grad_ref[0, i * 2 + group, j] = w_qk[pl.ds(start, rows), :]
                grad_ref[1, group * across + i, j] = w_vo[pl.ds(start, rows), :]

    if last:
        out_ref[...] = gin_ref[...].astype(BF)


def ffn_weights(refs, step, w_up, w_down):
    x, y = step // 2, step % 2
    main = refs[0].shape[0] // 2
    extra = refs[4].shape[3] // 2
    w_up[:main] = refs[x][y * main : (y + 1) * main]
    w_down[:main] = refs[2 + y][x * main : (x + 1) * main]
    start = main
    for ref in refs[4:]:
        for k in range(ref.shape[0]):
            w_up[start : start + extra] = ref[k, x, y, :extra]
            w_down[start : start + extra] = ref[k, x, y, extra:]
            start += extra
    return w_up[...], w_down[...]


def ffn_forward_kernel(count, last, *refs):
    weights, refs, (w_up, w_down) = refs[:count], refs[count:-2], refs[-2:]
    h_ref, hb_ref, bias_ref, vec_ref = refs[:4]
    if last:
        sum_in, act_ref, slope_ref, out_ref, n_ref, inv_ref, sum_ref = refs[4:]
    else:
        sum_in = None
        act_ref, slope_ref, sum_ref = refs[4:]
    chunk = w_up.shape[0]
    for step in range(4):
        up, down = ffn_weights(weights, step, w_up, w_down)
        columns = slice(step * chunk, (step + 1) * chunk)
        u = dot(hb_ref[...], up, NT) + bias_ref[0:1, columns]
        phi = 0.5 + 0.5 * lax.erf(u * 0.7071067811865476)
        act = (u * phi).astype(BF)
        act_ref[:, columns] = act
        slope = phi + u * jnp.exp(-0.5 * u * u) * 0.3989422804014327
        slope_ref[:, columns] = slope.astype(slope_ref.dtype)
        part = dot(act, down, NN)
        if step > 0:
            sum_ref[...] += part
        else:
            sum_ref[...] = part if sum_in is None else sum_in[...] + part
    if last:
        second_res = h_ref[...] + (sum_ref[...] + vec_ref[9:10])
        normed, inverse = normalized(second_res)
        out_ref[...] = (normed * vec_ref[10:11] + vec_ref[11:12]).astype(BF)
        n_ref[...] = normed
        inv_ref[...] = jnp.broadcast_to(inverse, inv_ref.shape)


def ffn_backward_kernel(blocks, count, last, *refs):
    weights, refs, (w_up, w_down) = refs[:count], refs[count:-2], refs[-2:]
    hb_ref, act_ref, slope_ref, n_ref, inv_ref, vec_ref = refs[:6]
    if last:
        grb_ref, sum_in = refs[6:8]
        gu_ref, gd_ref, bias_ref, gr_ref, gr1b_ref, grt_ref, vec_out, sum_ref = refs[8:]
        sum_ref[...] = sum_in[...]
    else:
        cot_ref, mask_ref, gu_ref, gd_ref, bias_ref, grb_ref, vec_out, sum_ref = refs[6:]
        normed = n_ref[...]
        d_result = jnp.where(mask_ref[:, :1] == 0.0, cot_ref[...].astype(F32), 0.0)
        vec_out[0:1] = jnp.sum(d_result * normed, 0, keepdims=True)
        vec_out[1:2] = jnp.sum(d_result, 0, keepdims=True)
        d_second = norm_backward(d_result, normed, inv_ref[:, :1], vec_ref[10:11])
        vec_out[2:3] = jnp.sum(d_second, 0, keepdims=True)
        sum_ref[...] = d_second
        grb_ref[...] = d_second.astype(BF)
    chunk = w_up.shape[0]
    for step in range(4):
        up, down = ffn_weights(weights, step, w_up, w_down)
        columns = slice(step * chunk, (step + 1) * chunk)
        grb = grb_ref[...]
        d_up = dot(grb, down, NT) * slope_ref[:, columns].astype(F32)
        bias_ref[0:1, columns] = jnp.sum(d_up, 0, keepdims=True)
        d_up_b = d_up.astype(BF)
        crossed = (step % 2 * 2 + step // 2) * chunk
        grad_down = dot(act_ref[:, columns].T, grb, NN).astype(BF)
        grad_up = dot(d_up_b.T, hb_ref[...], NN).astype(BF)
        main = main_rows(chunk) // blocks
        extra = chunk // blocks - main
        for k in range(blocks):
            for size, source, target in (
                (main, k * main, k * (main + extra)),
                (extra, blocks * main + k * extra, k * (main + extra) + main),
            ):
                rows = slice(source, source + size)
                gd_ref[crossed + target : crossed + target + size] = grad_down[rows]
                target += step * chunk
                gu_ref[target : target + size] = grad_up[rows]
        sum_ref[...] += dot(d_up_b, up, NN)
    if last:
        d_hidden = sum_ref[...]
        normed = n_ref[...]
        vec_out[0:1] = jnp.sum(d_hidden * normed, 0, keepdims=True)
        vec_out[1:2] = jnp.sum(d_hidden, 0, keepdims=True)
        d_first = norm_backward(d_hidden, normed, inv_ref[:, :1], vec_ref[3:4])
        vec_out[2:3] = jnp.sum(d_first, 0, keepdims=True)
        gr_ref[...] = d_first
        gr1b_ref[...] = d_first.astype(BF)
        grt_ref[...] = d_first.astype(BF).T


VMEM_SPEC = pl.BlockSpec(memory_space=pltpu.VMEM)


def main_rows(rows):
    return rows * 2 // 3


def up_places(index, unit):
    deep = COUNTS[3]
    main = main_rows(unit)
    half, chunk = index // (4 * deep), index // deep % 4 * deep * unit
    k = index % deep
    return (
        (half, chunk + k * main, slice(0, main)),
        (half, chunk + deep * main + k * (unit - main), slice(main, unit)),
    )


def spread_vectors_kernel(
    owner_ref, heads_ref, own_ref, other_ref, rows_ref, up_ref, bias_ref, units
):
    _, across, _, deep = COUNTS
    unit = units.shape[1]
    for x in range(2):
        for y in range(2):
            for z in range(deep):
                for c in range(2):
                    index = ((c * across + x) * 2 + y) * deep + z
                    start = owner_ref[index] * 3
                    for i in range(3):
                        units[pl.ds(start + i, 1), :] = (own_ref, other_ref)[c][
                            x, y, z, 0:1, i * unit : (i + 1) * unit
                        ]
    per_row = D // unit
    for row in range(12):
        for i in range(per_row):
            rows_ref[row : row + 1, i * unit : (i + 1) * unit] = units[
                row * per_row + i : row * per_row + i + 1, :
            ]
    for index in range(FF // unit):
        value = units[pl.ds(5 * per_row + owner_ref[index], 1), :]
        for half, start, piece in up_places(index, unit):
            up_ref[half, 0:1, start : start + piece.stop - piece.start] = value[:, piece]
    width = bias_ref.shape[2]
    for group in range(4):
        for kind in range(2):
            for i in range(width // unit):
                start = kind * per_row + heads_ref[group] * (width // unit) + i
                bias_ref[group, kind : kind + 1, i * unit : (i + 1) * unit] = units[
                    pl.ds(start, 1), :
                ]


def collect_vectors_kernel(
    owner_ref, heads_ref, bias_0, bias_1, up_0, up_1, one_ref, two_ref, out_ref, units
):
    out_ref[...] = jnp.zeros(out_ref.shape, F32)
    unit = units.shape[1]
    per_row = D // unit
    width = bias_0.shape[2]
    for group in range(4):
        source = (bias_0, bias_1)[group // 2]
        for kind in range(2):
            for i in range(width // unit):
                start = kind * per_row + heads_ref[group] * (width // unit) + i
                units[pl.ds(start, 1), :] = source[
                    group % 2, kind : kind + 1, i * unit : (i + 1) * unit
                ]
    for index in range(FF // unit):
        row = pl.ds(5 * per_row + owner_ref[index], 1)
        for half, start, piece in up_places(index, unit):
            source = (up_0, up_1)[half]
            units[row, piece] = source[0:1, start : start + piece.stop - piece.start]
    for row, source, line in (
        (2, one_ref, 2),
        (3, one_ref, 0),
        (4, one_ref, 1),
        (9, two_ref, 2),
        (10, two_ref, 0),
        (11, two_ref, 1),
    ):
        for i in range(per_row):
            units[row * per_row + i : row * per_row + i + 1, :] = source[
                line : line + 1, i * unit : (i + 1) * unit
            ]
    for index in range(FF // unit):
        for i in range(3):
            out_ref[index, 0:1, i * unit : (i + 1) * unit] = units[
                pl.ds(owner_ref[index] * 3 + i, 1), :
            ]


COUNTS = (2, 2, 2, 4)


def spread_vectors(owner, heads, own, other, unit, width):
    outs = [like((12, D), F32), like((2, 8, FF // 2), F32), like((4, 8, width), F32)]
    return pl.pallas_call(
        spread_vectors_kernel,
        in_specs=[SMEM_SPEC, SMEM_SPEC] + [pl.BlockSpec(memory_space=pltpu.VMEM)] * 2,
        out_specs=[pl.BlockSpec(memory_space=pltpu.VMEM)] * 3,
        out_shape=outs,
        scratch_shapes=[pltpu.VMEM((12 * D // unit, unit), F32)],
        compiler_params=params(8),
        cost_estimate=cost(0.0, 0.5, 0.0),
        name="spread_vectors",
    )(owner, heads, own, other)


def collect_vectors(owner, heads, unit, pair, *sources):
    return pl.pallas_call(
        collect_vectors_kernel,
        in_specs=[SMEM_SPEC, SMEM_SPEC] + [pl.BlockSpec(memory_space=pltpu.VMEM)] * len(sources),
        out_specs=pl.BlockSpec(memory_space=pltpu.VMEM),
        out_shape=like((FF // unit, 8, pair), F32),
        scratch_shapes=[pltpu.VMEM((12 * D // unit, unit), F32)],
        compiler_params=params(8),
        cost_estimate=cost(0.0, 0.5, 0.0),
        name="collect_vectors",
    )(owner, heads, *sources)


def pack_attention_kernel(qkv_ref, out_ref, vec_ref, pack_ref):
    rows, width = qkv_ref.shape[1:]
    vec_len = vec_ref.shape[1]
    pack_ref[:rows, :width] = qkv_ref[0].astype(BF)
    pack_ref[:rows, width:] = qkv_ref[1].astype(BF)
    vec = jnp.concatenate([vec_ref[...], jnp.zeros((1, 2 * width - vec_len), F32)], 1)
    vec = jnp.concatenate([vec, jnp.zeros((7, 2 * width), F32)], 0)
    pack_ref[rows : rows + 8] = vec.astype(BF)
    pack_ref[rows + 8 :, :width] = qkv_ref[2].astype(BF)
    pack_ref[rows + 8 :, width:] = out_ref[...].T.astype(BF)


def pack_attention(qkv, out, vec):
    rows, width = qkv.shape[1:]
    return pl.pallas_call(
        pack_attention_kernel,
        in_specs=[VMEM_SPEC] * 3,
        out_specs=VMEM_SPEC,
        out_shape=like((2 * rows + 8, 2 * width), BF),
        compiler_params=params(8),
        cost_estimate=cost(0.0, 0.5, 0.0),
        name="pack_attention",
    )(qkv, out, vec)


def advance_attention_kernel(rates, count, *refs):
    terms, olds, outs = refs[:count], refs[count : count + 6], refs[count + 6 :]
    whole_sum = terms[0][...]
    for term in terms[1:]:
        whole_sum = whole_sum + term[...].astype(F32)
    rows, width = olds[0].shape[1], olds[0].shape[2]
    parts = [
        whole_sum[:rows, :width],
        whole_sum[:rows, width:],
        whole_sum[rows + 8 :, :width],
    ]
    for i, grad in enumerate(parts):
        new = advance(olds[0][i], grad, olds[1][i], olds[2][i], DECAY, rates[0])
        for ref, value in zip(outs[:4], (grad, *new)):
            ref[i] = value
    grad = whole_sum[rows + 8 :, width:].T
    new = advance(olds[3][...], grad, olds[4][...], olds[5][...], DECAY, rates[1])
    for ref, value in zip(outs[4:8], (grad, *new)):
        ref[...] = value
    outs[8][...] = whole_sum[rows : rows + 8]


def advance_attention(terms, qkv, out, rates, others):
    outs = [like(qkv[0].shape, F32)] * 4 + [like(out[0].shape, F32)] * 4
    outs.append(like((8, terms[0].shape[1]), F32))
    vmem = pl.BlockSpec(memory_space=pltpu.VMEM)
    kernel = functools.partial(advance_attention_kernel, rates, len(terms))
    kernel, corners, _ = waiting(kernel, others)
    return pl.pallas_call(
        kernel,
        in_specs=[vmem] * (len(corners) + len(terms) + 6),
        out_specs=[vmem] * 9,
        out_shape=outs,
        compiler_params=params(16),
        cost_estimate=cost(0.0, 3.0, 0.0),
        name="advance_attention",
    )(*corners, *terms, *qkv, *out)


def waiting(kernel, others):
    corners = [corner(v) for v in jax.tree.leaves(others)]
    count = len(corners)
    return lambda *refs: kernel(*refs[count:]), corners, [VMEM_SPEC] * count


SMEM_SPEC = pl.BlockSpec(memory_space=pltpu.SMEM)
like = jax.ShapeDtypeStruct


def params(mib):
    return pltpu.CompilerParams(vmem_limit_bytes=mib << 20)


def cost(giga_flops, mega_bytes, mega_exps):
    return pl.CostEstimate(
        flops=int(giga_flops * 1e9),
        bytes_accessed=int(mega_bytes * 1e6),
        transcendentals=int(mega_exps * 1e6),
    )


def attention_forward(place, x, weights, biases, half, mask, vec_rows, mix, rows, others):
    length = x.shape[0]
    pair = weights[0].shape[4]
    width = pair // 2
    last = mix is not None
    row = like((length, D), F32)
    outs = [
        like((2, length, 3 * width), BF),
        like((2, 8, length), F32),
        like((2, length, width), BF),
    ]
    tail = [row]
    scratch = [pltpu.VMEM((D, pair), BF), pltpu.VMEM((D, pair), BF)]
    operands = [*weights, place, x, biases, mask, vec_rows]
    if last:
        low = like((length, D), BF)
        tail = [row, low, row, like((length, 128), F32), like((D, length), BF)]
        operands.append(mix)
        scratch.append(pltpu.VMEM((length, D), F32))
    kernel = functools.partial(attention_forward_kernel, rows, half, last)
    kernel, corners, _ = waiting(kernel, others)
    operands = corners + operands
    return pl.pallas_call(
        kernel,
        in_specs=[SMEM_SPEC if v is place else VMEM_SPEC for v in operands],
        out_specs=[VMEM_SPEC] * len(outs + tail),
        out_shape=outs + tail,
        scratch_shapes=scratch,
        compiler_params=params(14),
        cost_estimate=cost(4.5, 6.0, 3.1),
        name="attention_forward_last" if last else "attention_forward",
    )(*operands)


def attention_backward(place, x_t, gr, gr_t, weights, saved, mask, start, rows, last, others):
    length = gr.shape[0]
    pair = weights[0].shape[4]
    width = pair // 2
    across, _, deep = weights[0].shape[:3]
    qkv, lse, context = saved
    outs = [
        like((2, 2 * across, deep, rows, pair), BF),
        like((2, 8, width), F32),
        like((length, D), BF if last else F32),
    ]
    scratch = [
        pltpu.VMEM((D, pair), BF),
        pltpu.VMEM((D, pair), BF),
        pltpu.VMEM((length, 3 * width), BF),
    ]
    if last:
        scratch.append(pltpu.VMEM((length, D), F32))
    kernel = functools.partial(attention_backward_kernel, rows, last)
    kernel, corners, corner_specs = waiting(kernel, others)
    return pl.pallas_call(
        kernel,
        in_specs=corner_specs + [VMEM_SPEC] * 2 + [SMEM_SPEC] + [VMEM_SPEC] * 8,
        out_specs=[VMEM_SPEC] * 3,
        out_shape=outs,
        scratch_shapes=scratch,
        compiler_params=params(14),
        cost_estimate=cost(0.5, 1.0, 0.1),
        name="attention_backward_last" if last else "attention_backward",
    )(*corners, *weights, place, x_t, gr, gr_t, qkv, lse, context, mask, start)


def ffn_forward(h, hb, weights, bias, vec_rows, tail_operands):
    length = h.shape[0]
    up, down, extra = weights
    count = 4 + len(extra)
    hidden = FF // 2
    assembled = [pltpu.VMEM((hidden // 4, D), BF)] * 2
    last = len(tail_operands) > 0
    row = like((length, D), F32)
    outs = [like((length, hidden), BF), like((length, hidden), BF)]
    tail = [row]
    scratch = []
    if last:
        tail = [like((length, D), BF), row, like((length, 128), F32)]
        scratch = [pltpu.VMEM((length, D), F32)]
    return pl.pallas_call(
        functools.partial(ffn_forward_kernel, count, last),
        in_specs=[VMEM_SPEC] * (count + 4 + len(tail_operands)),
        out_specs=[VMEM_SPEC] * len(outs + tail),
        out_shape=outs + tail,
        scratch_shapes=scratch + assembled,
        compiler_params=params(14),
        cost_estimate=cost(4.9, 12.0, 1.6),
        name="ffn_forward_last" if last else "ffn_forward",
    )(*up, *down, *extra, h, hb, bias, vec_rows, *tail_operands)


def ffn_backward(hb, act, slope, weights, norm, tail_operands, blocks, last):
    length = hb.shape[0]
    up, down, extra = weights
    count = 4 + len(extra)
    hidden = FF // 2
    assembled = [pltpu.VMEM((hidden // 4, D), BF)] * 2
    row = like((length, D), F32)
    low = like((length, D), BF)
    grad = like((hidden, D), BF)
    outs = [grad, grad, like((8, hidden), F32)]
    vector = like((8, D), F32)
    tail = [row, low, like((D, length), BF), vector] if last else [low, vector, row]
    return pl.pallas_call(
        functools.partial(ffn_backward_kernel, blocks, count, last),
        in_specs=[VMEM_SPEC] * (count + 3 + len(norm) + len(tail_operands)),
        out_specs=[VMEM_SPEC] * len(outs + tail),
        out_shape=outs + tail,
        scratch_shapes=([pltpu.VMEM((length, D), F32)] if last else []) + assembled,
        compiler_params=params(14),
        cost_estimate=cost(9.7, 16.0, 0.0),
        name="ffn_backward_last" if last else "ffn_backward",
    )(*up, *down, *extra, hb, act, slope, *norm, *tail_operands)


def advance(weight, grad, moment, average, decay, rate):
    step_grad = grad + decay * weight
    moment_new = MOMENTUM * moment + step_grad
    weight_new = weight - rate * (step_grad + MOMENTUM * moment_new)
    average_new = AVERAGE * average + (1.0 - AVERAGE) * weight_new
    return (weight_new, moment_new, average_new)


def body(
    layer_input,
    lengths,
    cotangent,
    w_qkv,
    w_out,
    w_up,
    w_down,
    vectors,
    mom_qkv,
    mom_out,
    mom_up,
    mom_down,
    mom_vec,
    avg_qkv,
    avg_out,
    avg_up,
    avg_down,
    avg_vec,
):
    z, x, y, c = (lax.axis_index(a) for a in ("z", "x", "y", "c"))
    deep = lax.axis_size("z")
    blocks = deep * 8
    rows, head_cols = w_qkv.shape[1], w_qkv.shape[2]
    pair = 2 * head_cols
    vec_len = vectors.shape[0]
    ff_rows = w_up.shape[1]
    local = layer_input.shape[0]
    length = 4 * local

    kc, kx, ky, kz = jnp.meshgrid(
        jnp.arange(2), jnp.arange(2), jnp.arange(2), z_order(deep), indexing="ij"
    )
    owner = (((z ^ kz) * 2 + (x ^ kx)) * 4 + (y ^ ky) * 2 + (c ^ kc)).reshape(blocks)
    tz, tx, ty, tc = jnp.meshgrid(
        jnp.arange(deep), jnp.arange(2), jnp.arange(2), jnp.arange(2), indexing="ij"
    )
    seat = ((((c ^ tc) * 2 + (x ^ tx)) * 2 + (y ^ ty)) * deep + z_order(deep)[z ^ tz]).reshape(blocks)
    first, second = jnp.meshgrid(jnp.arange(2), jnp.arange(2), indexing="ij")
    group_head = ((y ^ second) * 2 + (c ^ first)).reshape(4)
    head_group = ((c ^ second) * 2 + (y ^ first)).reshape(4)

    in_kernel = rows % 32 == 0 and deep == COUNTS[3]
    owner, group_head = owner.astype(jnp.int32), group_head.astype(jnp.int32)

    if in_kernel:
        pack = pack_attention(w_qkv, w_out, vectors.reshape(1, vec_len))
    else:
        vec_rows = jnp.pad(vectors.astype(BF)[None], ((0, 7), (0, pair - vec_len)))
        pack_qk = jnp.concatenate([w_qkv[0], w_qkv[1]], 1).astype(BF)
        pack_vo = jnp.concatenate([w_qkv[2], w_out.T], 1).astype(BF)
        pack = jnp.concatenate([pack_qk, vec_rows, pack_vo], 0)
    (doc_x, doc_cot), x_y = to_documents(layer_input, cotangent)
    attn_z, z_first, z_second = gather_z(pack)
    qk, vo = attn_z[:, : rows + 8], attn_z[:, rows + 8 :]
    first_sent = (qk, vo)
    qk_first, vo_first = send(qk, "y"), send(vo, "x")
    qk = after(jnp.stack([qk, qk_first], 0), vo_first, x_y)
    vo = after(jnp.stack([vo, vo_first], 0), qk_first)
    qk_got, vo_got = send(qk, "x"), send(vo, "y")
    qk, vo = jnp.stack([qk, qk_got], 0), jnp.stack([vo, vo_got], 0)
    qk_other, vo_other = send(qk, "c"), send(vo, "c")

    main = main_rows(ff_rows)
    up_t, down_b = w_up.T.astype(BF), w_down.astype(BF)
    extra = jnp.concatenate([up_t[main:], down_b[main:]], 0)
    extra = jnp.stack([extra, send(extra, "x")], 0)
    extra_got = send(extra, "y")
    pack = jnp.concatenate([up_t[:main], down_b[:main]], 0)
    ffn_z, z_third, z_fourth = gather_z(after(pack, z_first), first_sent)
    up, down = ffn_z[:, :main], ffn_z[:, main:]
    up_got, down_got = send(up, "y"), send(down, "x")
    up, down = (
        after(jnp.stack([up, up_got], 0), down_got, qk_got, vo_got),
        after(jnp.stack([down, down_got], 0), up_got, qk_got, vo_got),
    )
    extra = after(jnp.stack([extra, extra_got], 1), z_third, first_sent)
    extra, extra_far = gather_z(extra, (z_fourth,), True)
    if False:
        up, down = after(up, extra_far), after(down, extra_far)
    up_got, down_got = send(up, "x"), send(down, "y")

    vec_own, vec_other = (v[..., rows:, :].astype(F32) for v in (qk, qk_other))
    if in_kernel:
        vec_rows, bias_up, biases = spread_vectors(
            owner, group_head, vec_own, vec_other, ff_rows, head_cols
        )
    else:
        vec_all = jnp.stack([v[..., 0, :vec_len] for v in (vec_own, vec_other)], 0)
        vec_all = vec_all.reshape(blocks, vec_len)
        vec_rows = jnp.take(vec_all, seat, axis=0).reshape(12, D)
        bias_up = jnp.take(vec_rows[5:9].reshape(blocks, ff_rows), owner, axis=0)
        bias_up = bias_up.reshape(2, 4, deep, ff_rows)
        bias_up = [v.reshape(2, 4, -1) for v in (bias_up[..., :main], bias_up[..., main:])]
        bias_up = jnp.concatenate(bias_up, 2).reshape(2, 1, FF // 2)
        bias_up = jnp.pad(bias_up, ((0, 0), (0, 7), (0, 0)))
        bias_q = jnp.take(vec_rows[0].reshape(4, head_cols), group_head, axis=0)
        bias_v = jnp.take(vec_rows[1].reshape(4, head_cols), group_head, axis=0)
        biases = jnp.pad(jnp.stack([bias_q, bias_v], 1), ((0, 0), (0, 6), (0, 0)))

    row = jnp.arange(length)
    part = row // local
    position = ((y ^ (part % 2)) * 2 + (c ^ (part // 2))) * local + row % local
    doc_len = lax.dynamic_index_in_dim(lengths, y * 2 + c, 0, keepdims=False)
    alive = position < doc_len
    mask = jnp.where(alive, 0.0, -1e30).astype(F32)
    mask_row = jnp.broadcast_to(mask[None, :], (8, length))
    mask_col = jnp.broadcast_to(mask[:, None], (length, 128))

    if in_kernel:
        zs = flip_order("z")[None, :]
        place = (zs * 2 + (x ^ jnp.arange(2)[:, None])).reshape(2 * deep)
        kernel_rows = rows
    else:
        xs = x ^ jnp.arange(2)
        zs = flip_order("z")

        def true_order(qk, vo):
            qk = jnp.take(jnp.take(qk[..., :rows, :], xs, axis=0), zs, axis=2)
            vo = jnp.take(jnp.take(vo, xs, axis=1), zs, axis=2)
            qk, vo = qk.transpose(1, 2, 0, 3, 4), vo.transpose(0, 2, 1, 3, 4)
            return qk.reshape(1, 2, 1, D, pair), vo.reshape(2, 1, 1, D, pair)

        def relative_order(qk, vo):
            qk = qk.reshape(2, deep, 2, rows, pair).transpose(2, 0, 1, 3, 4)
            vo = vo.reshape(2, deep, 2, rows, pair).transpose(0, 2, 1, 3, 4)
            qk = jnp.take(jnp.take(qk, xs, axis=0), zs, axis=2)
            return qk, jnp.take(jnp.take(vo, xs, axis=1), zs, axis=2)

        place = jnp.zeros((1,), jnp.int32)
        qk, vo = true_order(qk, vo)
        qk_other, vo_other = true_order(qk_other, vo_other)
        kernel_rows = D
        size = 2 * deep * (ff_rows - main)
        extra = extra[0].reshape(deep, 2, 2, 2, ff_rows - main, D).transpose(1, 2, 3, 0, 4, 5)
        extra = (extra.reshape(1, 2, 2, size, D),)
    place = place.astype(jnp.int32)

    *saved_0, mix = attention_forward(
        place, doc_x, (qk, vo), biases, 0, mask_row, vec_rows, None, kernel_rows, ()
    )
    *saved_1, hidden, hidden_b, normed, inverse, x_t = attention_forward(
        place, doc_x, (qk_other, vo_other), biases, 1, mask_row, vec_rows, mix, kernel_rows, (extra[-1],)
    )
    flat = lambda v: v.reshape(2 * deep * main, D)
    ffn_own = (flat(up), flat(up_got)), (flat(down), flat(down_got)), extra
    across = lambda parts, early: tuple(
        send(part if i < early else after(part, hidden_b), "c") for i, part in enumerate(parts)
    )
    ffn_other = tuple(across(parts, early) for parts, early in zip(ffn_own, (1, 1, 0)))
    act_0, slope_0, mix = ffn_forward(
        hidden, hidden_b, ffn_own, bias_up[0], vec_rows, ()
    )
    act_1, slope_1, result, normed_two, inverse_two = ffn_forward(
        hidden, hidden_b, ffn_other, bias_up[1], vec_rows, (mix,)
    )
    out_own, out_y = from_documents_y(result, local)

    lead = (2, 2, deep, ff_rows, D)
    kernel_blocks = deep if in_kernel else 1
    norm_two = (normed_two, inverse_two, vec_rows)
    up_1, down_1, d_bias_1, d_second_b, vec_two, d_hidden = ffn_backward(
        hidden_b, act_1, slope_1, ffn_other, norm_two, (doc_cot, mask_col), kernel_blocks, False
    )
    up_1, down_1 = send(up_1, "c"), send(down_1, "c")
    norm_one = (normed, inverse, vec_rows)
    up_0, down_0, d_bias_0, d_first, d_first_b, d_first_t, vec_one = ffn_backward(
        hidden_b, act_0, slope_0, ffn_own, norm_one, (d_second_b, d_hidden), kernel_blocks, True
    )
    ffn_c = (up_1, down_1)
    if not in_kernel:

        def by_block(grad):
            grad = grad.reshape(4, deep * ff_rows, D)
            parts = (grad[:, : deep * main], grad[:, deep * main :])
            return jnp.concatenate([v.reshape(4, deep, -1, D) for v in parts], 2)

        up_0, up_1, down_0, down_1 = (by_block(v) for v in (up_0, up_1, down_0, down_1))
    grad_up = swap([up_0.reshape(lead), up_1.reshape(lead)], "x")
    grad_down = swap([down_0.reshape(lead), down_1.reshape(lead)], "y")
    ffn_big = (grad_up[-1], grad_down[-1])
    grad_up, grad_down = swap(grad_up, "y"), swap(grad_down, "x")
    ffn_second = (grad_up[-1], grad_down[-1])
    grad_ffn, _ = scatter_z([grad_up, grad_down], False)

    attn_1, bias_1, d_attn = attention_backward(
        place, x_t, d_first_b, d_first_t, (qk_other, vo_other), saved_1, mask_col, d_first, kernel_rows, False, ffn_c
    )
    attn_0, bias_0, d_input = attention_backward(
        place, x_t, d_first_b, d_first_t, (qk, vo), saved_0, mask_col, d_attn, kernel_rows, True, (after(corner(out_y), bias_1[0]),)
    )
    attn_1 = send(attn_1, "c")
    if in_kernel:
        pairs = [v.reshape(2, 2, 2, deep, rows, pair) for v in (attn_0, attn_1)]
    else:
        pairs = [relative_order(v[0], v[1]) for v in (attn_0, attn_1)]
    (qk_0, vo_0), (qk_1, vo_1) = pairs

    bias_0 = after(bias_0, ffn_big)
    if in_kernel:
        vec_part = collect_vectors(
            owner, group_head, ff_rows, pair, bias_0, bias_1, d_bias_0, d_bias_1, vec_one, vec_two
        ).reshape(2, 2, 2, deep, 8, pair)
    else:
        d_bias = jnp.concatenate([bias_0, bias_1], 0)
        d_bias_q = jnp.take(d_bias[:, 0], head_group, axis=0).reshape(D)
        d_bias_v = jnp.take(d_bias[:, 1], head_group, axis=0).reshape(D)
        d_bias_up = jnp.stack([d_bias_0[0], d_bias_1[0]], 0).reshape(2, 4, -1)
        parts = (d_bias_up[..., : deep * main], d_bias_up[..., deep * main :])
        d_bias_up = jnp.concatenate([v.reshape(blocks, -1) for v in parts], 1)
        d_bias_up = jnp.take(d_bias_up, seat, axis=0).reshape(FF)
        grad_vec = jnp.concatenate(
            [
                d_bias_q,
                d_bias_v,
                vec_one[2],
                vec_one[0],
                vec_one[1],
                d_bias_up,
                vec_two[2],
                vec_two[0],
                vec_two[1],
            ]
        )
        vec_part = jnp.take(grad_vec.reshape(blocks, vec_len), owner, axis=0)
        vec_part = jnp.pad(vec_part, ((0, 0), (0, pair - vec_len))).reshape(2, 2, 2, deep, 1, pair)
        vec_part = jnp.pad(vec_part, ((0, 0),) * 4 + ((0, 7), (0, 0)))
    vec_part = vec_part[0] + send(vec_part[1], "c")
    sum_qk, vec_terms, sum_vo = [qk_0, qk_1], [vec_part], [vo_0, vo_1]
    for axis_qk, axis_vo in (("x", "y"), ("y", "x")):
        part = jnp.concatenate(
            [total([t[1] for t in sum_qk]), total([t[1] for t in vec_terms])], -2
        )
        got = send(after(part, ffn_second).astype(BF), axis_qk)
        sum_qk = [t[0] for t in sum_qk] + [got[..., :rows, :]]
        vec_terms = [t[0] for t in vec_terms] + [got[..., rows:, :]]
        sum_vo = swap(sum_vo, axis_vo, ffn_second)
    d_input = after(d_input, got, sum_vo[-1])
    grad_attn, sent = scatter_z([sum_qk, vec_terms, sum_vo], True)
    grad_ffn = after(total(grad_ffn), sent)
    grad_up, grad_down = grad_ffn[:ff_rows].T, grad_ffn[ff_rows:]
    layer_output = from_documents(group_head, after(out_own, grad_ffn), out_y, BF)
    grad_input = from_documents(group_head, *from_documents_y(d_input, local), F32)

    slots = length * layer_input.shape[1] * deep * 2
    rate = RATE_BASE / math.sqrt(slots)
    rate_out = rate * math.sqrt(LEN / 8.0)
    olds_qkv, olds_out = (w_qkv, mom_qkv, avg_qkv), (w_out, mom_out, avg_out)
    if in_kernel:
        (
            grad_qkv,
            new_qkv,
            new_mom_qkv,
            new_avg_qkv,
            grad_out,
            new_out,
            new_mom_out,
            new_avg_out,
            grad_vec,
        ) = advance_attention(
            grad_attn, olds_qkv, olds_out, (rate, rate_out), (layer_output, grad_input)
        )
        grad_vec = grad_vec[0, :vec_len]
    else:
        grad_attn = total(grad_attn)
        sum_qk, sum_vo = grad_attn[:rows], grad_attn[rows + 8 :]
        grad_qkv = jnp.stack([sum_qk[:, :head_cols], sum_qk[:, head_cols:], sum_vo[:, :head_cols]])
        grad_out = sum_vo[:, head_cols:].T
        grad_vec = grad_attn[rows, :vec_len]
        new_qkv, new_mom_qkv, new_avg_qkv = advance(
            w_qkv, grad_qkv, mom_qkv, avg_qkv, DECAY, rate
        )
        new_out, new_mom_out, new_avg_out = advance(
            w_out, grad_out, mom_out, avg_out, DECAY, rate_out
        )
    new_up, new_mom_up, new_avg_up = advance(w_up, grad_up, mom_up, avg_up, DECAY, rate)
    new_down, new_mom_down, new_avg_down = advance(
        w_down, grad_down, mom_down, avg_down, DECAY, rate
    )
    new_vec, new_mom_vec, new_avg_vec = advance(vectors, grad_vec, mom_vec, avg_vec, 0.0, rate)
    return (
        layer_output,
        grad_input,
        grad_qkv,
        grad_out,
        grad_up,
        grad_down,
        grad_vec,
        new_qkv,
        new_out,
        new_up,
        new_down,
        new_vec,
        new_mom_qkv,
        new_mom_out,
        new_mom_up,
        new_mom_down,
        new_mom_vec,
        new_avg_qkv,
        new_avg_out,
        new_avg_up,
        new_avg_down,
        new_avg_vec,
    )


def solution(mesh):
    dp, head = mesh.shape["dp"], mesh.shape["head"]
    fine = Mesh(mesh.devices.reshape(dp // 2, 2, head // 2, 2), ("z", "x", "y", "c"))
    dps, heads, every = ("z", "x"), ("y", "c"), ("z", "x", "y", "c")
    acts = P(heads, dps, None)
    weights = (P(None, dps, heads), P(heads, dps), P(None, every), P(every, None), P(every))
    return jax.shard_map(
        body,
        mesh=fine,
        in_specs=(acts, P(dps), acts) + weights * 3,
        out_specs=(acts, acts) + weights * 4,
        check_vma=False,
    )
```

```python
import functools
import math

import jax
import jax.numpy as jnp
from jax import lax
from jax.experimental import pallas as pl
from jax.experimental.pallas import tpu as pltpu
from jax.sharding import Mesh
from jax.sharding import PartitionSpec as P

D = 768
HD = 64
FF = 3072
LEN = 512

EPSILON = 1e-05
MOMENTUM = 0.9
AVERAGE = 0.9
DECAY = 0.01
RATE_BASE = 0.05

BF = jnp.bfloat16
F32 = jnp.float32
NT = (((1,), (1,)), ((), ()))
NN = (((1,), (0,)), ((), ()))


def send(values, axis, bit=1):
    return lax.ppermute(values, axis, [(i, i ^ bit) for i in range(lax.axis_size(axis))])


def corner(array):
    rows, columns = min(8, array.shape[-2]), min(128, array.shape[-1])
    return array.reshape(-1, *array.shape[-2:])[0, :rows, :columns]


def after(values, *others):
    def nothing(other, width):
        row = other.reshape(-1, other.shape[-1])[:1, :width].astype(F32) * 0.0
        return jnp.concatenate([row] * (width // row.shape[1]), 1)[0]

    def later(value):
        others_left = [nothing(v, value.shape[-1]) for v in jax.tree.leaves(others)]
        return value + sum(others_left).astype(value.dtype) if others_left else value

    return jax.tree.map(later, values)


def z_order(size):
    return jnp.array([0, 2, 1, 3]) if size == 4 else jnp.arange(size)


def flip_order(axis):
    size = lax.axis_size(axis)
    return lax.axis_index(axis) ^ z_order(size)


def gather_z(shard, before=(), apart=False):
    size = lax.axis_size("z")
    if size != 4:
        whole = jnp.take(lax.all_gather(shard, "z"), flip_order("z"), axis=0)
        return ((whole,), whole[0]) if apart else (whole, whole[0], whole[0])
    first = send(shard, "z", 2)
    pair = after(jnp.stack([shard, first], 0), before)
    second = send(pair, "z", 1)
    if apart:
        return (pair, second), first
    return jnp.concatenate([pair, second], 0), first, second


def total(terms):
    result = terms[0].astype(F32)
    for term in terms[1:]:
        result = result + term.astype(F32)
    return result


def swap(terms, axis, others=()):
    part = total([t[1] for t in terms])
    got = send(after(part, others).astype(BF), axis)
    return [t[0] for t in terms] + [got]


def scatter_z(sums, direct):
    joined = lambda index: jnp.concatenate([total([t[index] for t in terms]) for terms in sums], -2)
    if lax.axis_size("z") != 4:
        everything = jnp.take(joined(slice(None)).astype(BF), flip_order("z"), axis=0)
        parts = lax.all_to_all(everything, "z", 0, 0, tiled=True)
        return [total(list(parts[1:])), parts[0]], parts[0]
    if direct:
        parts = [joined(place).astype(BF) for place in (1, 2, 3)]
        return [joined(0)] + [send(part, "z", bit) for part, bit in zip(parts, (2, 1, 3))], parts[2]
    got = send(joined(slice(2, 4)).astype(BF), "z", 1)
    left, start = [], 0
    for terms in sums:
        end = start + terms[0].shape[-2]
        left.append([t[:2] for t in terms] + [got[:, start:end]])
        start = end
    sums = left
    part = joined(1).astype(BF)
    return [joined(0), send(part, "z", 2)], part


def to_documents(*arrays):
    y, c = lax.axis_index("y"), lax.axis_index("c")
    local, _, width = arrays[0].shape
    docs = [v.transpose(1, 0, 2).reshape(2, 2, local, width) for v in arrays]
    of = lambda v, index: lax.dynamic_index_in_dim(v, index, 0, keepdims=False)
    got_y = send(jnp.concatenate([of(v, 1 - y) for v in docs], 0), "y")
    pairs = [(of(v, y), got_y[2 * i : 2 * i + 2]) for i, v in enumerate(docs)]
    got = send(jnp.stack([of(v, 1 - c) for pair in pairs for v in pair], 0), "c")
    whole = [
        jnp.concatenate([of(pair[0], c), of(pair[1], c), got[2 * i], got[2 * i + 1]], 0)
        for i, pair in enumerate(pairs)
    ]
    return whole, got_y


def from_documents_y(values, local):
    values = values.reshape(2, 2, local, values.shape[1])
    return values[:, 0], send(values[:, 1], "y")


def assemble_kernel(seats_ref, own_ref, got_y_ref, got_c_ref, out_ref):
    for place, ref, part in ((0, own_ref, 0), (1, got_y_ref, 0), (2, got_c_ref, 0), (3, got_c_ref, 1)):
        out_ref[seats_ref[place]] = ref[part].astype(out_ref.dtype)


def from_documents(seats, own, got_y, dtype):
    got_c = send(jnp.stack([own[1], got_y[1]], 0), "c")
    vmem = pl.BlockSpec(memory_space=pltpu.VMEM)
    docs = pl.pallas_call(
        assemble_kernel,
        in_specs=[SMEM_SPEC, vmem, vmem, vmem],
        out_specs=vmem,
        out_shape=jax.ShapeDtypeStruct((4, *own.shape[1:]), dtype),
        compiler_params=params(12),
        cost_estimate=cost(0.0, 2.0, 0.0),
        name="assemble",
    )(seats, own, got_y, got_c)
    return docs.transpose(1, 0, 2)


def dot(a, b, dims):
    return lax.dot_general(a, b, dims, preferred_element_type=F32)


def normalized(values):
    center = values - jnp.mean(values, -1, keepdims=True)
    inverse = lax.rsqrt(jnp.mean(center * center, -1, keepdims=True) + EPSILON)
    return center * inverse, inverse


def norm_backward(d_result, normed, inverse, gain):
    d_normed = d_result * gain
    return inverse * (
        d_normed
        - jnp.mean(d_normed, -1, keepdims=True)
        - normed * jnp.mean(d_normed * normed, -1, keepdims=True)
    )


def block_start(place_ref, index, rows):
    start = place_ref[index] * rows
    return pl.multiple_of(start, 32) if rows % 32 == 0 else start


def place_weights(place_ref, group, qk_ref, vo_ref, w_qk, w_vo, rows):
    across, _, deep = qk_ref.shape[:3]
    for i in range(across):
        for k in range(deep):
            start = block_start(place_ref, i * deep + k, rows)
            w_qk[pl.ds(start, rows), :] = qk_ref[i, group, k, :rows]
            w_vo[pl.ds(start, rows), :] = vo_ref[group, i, k]


def attention_forward_kernel(rows, half, last, *refs):
    qk_ref, vo_ref, *refs = refs
    place_ref, x_ref, bias_ref, mask_ref, vec_ref = refs[:5]
    if last:
        mix_in, qkv_ref, lse_ref, context_ref = refs[5:9]
        h_ref, hb_ref, n_ref, inv_ref, xt_ref, w_qk, w_vo, mix_ref = refs[9:]
    else:
        mix_in = None
        qkv_ref, lse_ref, context_ref, mix_ref, w_qk, w_vo = refs[5:]
    x = x_ref[...]
    length = x.shape[0]
    width = w_qk.shape[1] // 2
    mix_ref[...] = jnp.zeros(mix_ref.shape, F32) if mix_in is None else mix_in[...]

    @pl.loop(0, 2)
    def _(group):
        place_weights(place_ref, group, qk_ref, vo_ref, w_qk, w_vo, rows)
        bias = bias_ref[half * 2 + group]
        qk = dot(x, w_qk[...], NN)
        v = (dot(x, w_vo[:, :width], NN) + bias[1:2, :width]).astype(BF)
        q = ((qk[:, :width] + bias[0:1, :width]).astype(BF).astype(F32) * HD ** (-0.5)).astype(BF)
        k = qk[:, width:].astype(BF)
        qkv_ref[group, :, :width] = q
        qkv_ref[group, :, width : 2 * width] = k
        qkv_ref[group, :, 2 * width :] = v
        mask = mask_ref[0:1]
        contexts, logs = [], []
        for head in range(width // HD):
            cols = slice(head * HD, (head + 1) * HD)
            s = dot(q[:, cols], k[:, cols], NT) + mask
            peak = jnp.max(s, -1, keepdims=True)
            weight = jnp.exp(s - peak)
            total_exp = jnp.sum(weight, -1, keepdims=True)
            log_total = peak + jnp.log(total_exp)
            p = (weight * (1.0 / total_exp)).astype(BF)
            contexts.append(dot(p, v[:, cols], NN).astype(BF))
            logs.append(log_total)
        context = jnp.concatenate(contexts, 1)
        context_ref[group] = context
        lanes = lax.broadcasted_iota(jnp.int32, (length, 128), 1)
        packed = jnp.zeros((length, 128), F32)
        for head, log_total in enumerate(logs):
            packed = jnp.where(lanes == head, log_total, packed)
        lse_ref[group] = packed.T[:8]
        mix_ref[...] += dot(context, w_vo[:, width:], NT)

    if last:
        first_res = x_ref[...].astype(F32) + mix_ref[...] + vec_ref[2:3]
        normed, inverse = normalized(first_res)
        hidden = normed * vec_ref[3:4] + vec_ref[4:5]
        n_ref[...] = normed
        inv_ref[...] = jnp.broadcast_to(inverse, inv_ref.shape)
        h_ref[...] = hidden
        hb_ref[...] = hidden.astype(BF)
        xt_ref[...] = x_ref[...].T


def attention_backward_kernel(rows, last, *refs):
    qk_ref, vo_ref, *refs = refs
    place_ref, xt_ref, gr_ref, grt_ref, qkv_ref, lse_ref, context_ref = refs[:7]
    mask_ref, start_ref = refs[7:9]
    if last:
        grad_ref, bias_ref, out_ref, w_qk, w_vo, g_qkv, gin_ref = refs[9:]
    else:
        grad_ref, bias_ref, gin_ref, w_qk, w_vo, g_qkv = refs[9:]
    width = w_qk.shape[1] // 2
    gin_ref[...] = start_ref[...]

    @pl.loop(0, 2)
    def _(group):
        place_weights(place_ref, group, qk_ref, vo_ref, w_qk, w_vo, rows)
        gc = dot(gr_ref[...], w_vo[:, width:], NN).astype(BF)
        mask = mask_ref[:, :1]
        sums = []
        for head in range(width // HD):
            q = qkv_ref[group, :, head * HD : (head + 1) * HD]
            k = qkv_ref[group, :, width + head * HD : width + (head + 1) * HD]
            v = qkv_ref[group, :, 2 * width + head * HD : 2 * width + (head + 1) * HD]
            g = gc[:, head * HD : (head + 1) * HD]
            p = jnp.exp(dot(k, q, NT) + mask - lse_ref[group, head : head + 1])
            dp = dot(v, g, NT)
            gv = dot(p.astype(BF), g, NN)
            delta = jnp.sum(p * dp, 0, keepdims=True)
            gs = (p * (dp - delta)).astype(BF)
            gk = dot(gs, q, NN)
            gq = dot(gs.T, (k.astype(F32) * HD ** (-0.5)).astype(BF), NN)
            g_qkv[:, head * HD : (head + 1) * HD] = gq.astype(BF)
            g_qkv[:, width + head * HD : width + (head + 1) * HD] = gk.astype(BF)
            g_qkv[:, 2 * width + head * HD : 2 * width + (head + 1) * HD] = gv.astype(BF)
            sums.append((jnp.sum(gq, 0, keepdims=True), jnp.sum(gv, 0, keepdims=True)))
        bias_ref[group, 0:1, :] = jnp.concatenate([s[0] for s in sums], 1)
        bias_ref[group, 1:2, :] = jnp.concatenate([s[1] for s in sums], 1)
        g_qk = g_qkv[:, : 2 * width]
        g_v = g_qkv[:, 2 * width :]
        gin = dot(g_qk, w_qk[...], NT) + dot(g_v, w_vo[:, :width], NT)
        gin_ref[...] += gin

        w_qk[...] = dot(xt_ref[...], g_qk, NN).astype(BF)
        w_vo[:, :width] = dot(xt_ref[...], g_v, NN).astype(BF)
        w_vo[:, width:] = dot(grt_ref[...], context_ref[group], NN).astype(BF)
        across, deep = grad_ref.shape[1] // 2, grad_ref.shape[2]
        for i in range(across):
            for j in range(deep):
                start = block_start(place_ref, i * deep + j, rows)
                grad_ref[0, i * 2 + group, j] = w_qk[pl.ds(start, rows), :]
                grad_ref[1, group * across + i, j] = w_vo[pl.ds(start, rows), :]

    if last:
        out_ref[...] = gin_ref[...].astype(BF)


def ffn_weights(refs, step, w_up, w_down):
    x, y = step // 2, step % 2
    main = refs[0].shape[0] // 2
    extra = refs[4].shape[3] // 2
    w_up[:main] = refs[x][y * main : (y + 1) * main]
    w_down[:main] = refs[2 + y][x * main : (x + 1) * main]
    start = main
    for ref in refs[4:]:
        for k in range(ref.shape[0]):
            w_up[start : start + extra] = ref[k, x, y, :extra]
            w_down[start : start + extra] = ref[k, x, y, extra:]
            start += extra
    return w_up[...], w_down[...]


def ffn_forward_kernel(count, last, *refs):
    weights, refs, (w_up, w_down) = refs[:count], refs[count:-2], refs[-2:]
    h_ref, hb_ref, bias_ref, vec_ref = refs[:4]
    if last:
        sum_in, act_ref, slope_ref, out_ref, n_ref, inv_ref, sum_ref = refs[4:]
    else:
        sum_in = None
        act_ref, slope_ref, sum_ref = refs[4:]
    chunk = w_up.shape[0]
    for step in range(4):
        up, down = ffn_weights(weights, step, w_up, w_down)
        columns = slice(step * chunk, (step + 1) * chunk)
        u = dot(hb_ref[...], up, NT) + bias_ref[0:1, columns]
        phi = 0.5 + 0.5 * lax.erf(u * 0.7071067811865476)
        act = (u * phi).astype(BF)
        act_ref[:, columns] = act
        slope = phi + u * jnp.exp(-0.5 * u * u) * 0.3989422804014327
        slope_ref[:, columns] = slope.astype(slope_ref.dtype)
        part = dot(act, down, NN)
        if step > 0:
            sum_ref[...] += part
        else:
            sum_ref[...] = part if sum_in is None else sum_in[...] + part
    if last:
        second_res = h_ref[...] + (sum_ref[...] + vec_ref[9:10])
        normed, inverse = normalized(second_res)
        out_ref[...] = (normed * vec_ref[10:11] + vec_ref[11:12]).astype(BF)
        n_ref[...] = normed
        inv_ref[...] = jnp.broadcast_to(inverse, inv_ref.shape)


def ffn_backward_kernel(blocks, count, last, *refs):
    weights, refs, (w_up, w_down) = refs[:count], refs[count:-2], refs[-2:]
    hb_ref, act_ref, slope_ref, n_ref, inv_ref, vec_ref = refs[:6]
    if last:
        grb_ref, sum_in = refs[6:8]
        gu_ref, gd_ref, bias_ref, gr_ref, gr1b_ref, grt_ref, vec_out, sum_ref = refs[8:]
        sum_ref[...] = sum_in[...]
    else:
        cot_ref, mask_ref, gu_ref, gd_ref, bias_ref, grb_ref, vec_out, sum_ref = refs[6:]
        normed = n_ref[...]
        d_result = jnp.where(mask_ref[:, :1] == 0.0, cot_ref[...].astype(F32), 0.0)
        vec_out[0:1] = jnp.sum(d_result * normed, 0, keepdims=True)
        vec_out[1:2] = jnp.sum(d_result, 0, keepdims=True)
        d_second = norm_backward(d_result, normed, inv_ref[:, :1], vec_ref[10:11])
        vec_out[2:3] = jnp.sum(d_second, 0, keepdims=True)
        sum_ref[...] = d_second
        grb_ref[...] = d_second.astype(BF)
    chunk = w_up.shape[0]
    for step in range(4):
        up, down = ffn_weights(weights, step, w_up, w_down)
        columns = slice(step * chunk, (step + 1) * chunk)
        grb = grb_ref[...]
        d_up = dot(grb, down, NT) * slope_ref[:, columns].astype(F32)
        bias_ref[0:1, columns] = jnp.sum(d_up, 0, keepdims=True)
        d_up_b = d_up.astype(BF)
        crossed = (step % 2 * 2 + step // 2) * chunk
        grad_down = dot(act_ref[:, columns].T, grb, NN).astype(BF)
        grad_up = dot(d_up_b.T, hb_ref[...], NN).astype(BF)
        main = main_rows(chunk) // blocks
        extra = chunk // blocks - main
        for k in range(blocks):
            for size, source, target in (
                (main, k * main, k * (main + extra)),
                (extra, blocks * main + k * extra, k * (main + extra) + main),
            ):
                rows = slice(source, source + size)
                gd_ref[crossed + target : crossed + target + size] = grad_down[rows]
                target += step * chunk
                gu_ref[target : target + size] = grad_up[rows]
        sum_ref[...] += dot(d_up_b, up, NN)
    if last:
        d_hidden = sum_ref[...]
        normed = n_ref[...]
        vec_out[0:1] = jnp.sum(d_hidden * normed, 0, keepdims=True)
        vec_out[1:2] = jnp.sum(d_hidden, 0, keepdims=True)
        d_first = norm_backward(d_hidden, normed, inv_ref[:, :1], vec_ref[3:4])
        vec_out[2:3] = jnp.sum(d_first, 0, keepdims=True)
        gr_ref[...] = d_first
        gr1b_ref[...] = d_first.astype(BF)
        grt_ref[...] = d_first.astype(BF).T


VMEM_SPEC = pl.BlockSpec(memory_space=pltpu.VMEM)


def main_rows(rows):
    return rows * 2 // 3


def up_places(index, unit):
    deep = COUNTS[3]
    main = main_rows(unit)
    half, chunk = index // (4 * deep), index // deep % 4 * deep * unit
    k = index % deep
    return (
        (half, chunk + k * main, slice(0, main)),
        (half, chunk + deep * main + k * (unit - main), slice(main, unit)),
    )


def spread_vectors_kernel(
    owner_ref, heads_ref, own_ref, other_ref, rows_ref, up_ref, bias_ref, units
):
    _, across, _, deep = COUNTS
    unit = units.shape[1]
    for x in range(2):
        for y in range(2):
            for z in range(deep):
                for c in range(2):
                    index = ((c * across + x) * 2 + y) * deep + z
                    start = owner_ref[index] * 3
                    for i in range(3):
                        units[pl.ds(start + i, 1), :] = (own_ref, other_ref)[c][
                            x, y, z, 0:1, i * unit : (i + 1) * unit
                        ]
    per_row = D // unit
    for row in range(12):
        for i in range(per_row):
            rows_ref[row : row + 1, i * unit : (i + 1) * unit] = units[
                row * per_row + i : row * per_row + i + 1, :
            ]
    for index in range(FF // unit):
        value = units[pl.ds(5 * per_row + owner_ref[index], 1), :]
        for half, start, piece in up_places(index, unit):
            up_ref[half, 0:1, start : start + piece.stop - piece.start] = value[:, piece]
    width = bias_ref.shape[2]
    for group in range(4):
        for kind in range(2):
            for i in range(width // unit):
                start = kind * per_row + heads_ref[group] * (width // unit) + i
                bias_ref[group, kind : kind + 1, i * unit : (i + 1) * unit] = units[
                    pl.ds(start, 1), :
                ]


def collect_vectors_kernel(
    owner_ref, heads_ref, bias_0, bias_1, up_0, up_1, one_ref, two_ref, out_ref, units
):
    out_ref[...] = jnp.zeros(out_ref.shape, F32)
    unit = units.shape[1]
    per_row = D // unit
    width = bias_0.shape[2]
    for group in range(4):
        source = (bias_0, bias_1)[group // 2]
        for kind in range(2):
            for i in range(width // unit):
                start = kind * per_row + heads_ref[group] * (width // unit) + i
                units[pl.ds(start, 1), :] = source[
                    group % 2, kind : kind + 1, i * unit : (i + 1) * unit
                ]
    for index in range(FF // unit):
        row = pl.ds(5 * per_row + owner_ref[index], 1)
        for half, start, piece in up_places(index, unit):
            source = (up_0, up_1)[half]
            units[row, piece] = source[0:1, start : start + piece.stop - piece.start]
    for row, source, line in (
        (2, one_ref, 2),
        (3, one_ref, 0),
        (4, one_ref, 1),
        (9, two_ref, 2),
        (10, two_ref, 0),
        (11, two_ref, 1),
    ):
        for i in range(per_row):
            units[row * per_row + i : row * per_row + i + 1, :] = source[
                line : line + 1, i * unit : (i + 1) * unit
            ]
    for index in range(FF // unit):
        for i in range(3):
            out_ref[index, 0:1, i * unit : (i + 1) * unit] = units[
                pl.ds(owner_ref[index] * 3 + i, 1), :
            ]


COUNTS = (2, 2, 2, 4)


def spread_vectors(owner, heads, own, other, unit, width):
    outs = [like((12, D), F32), like((2, 8, FF // 2), F32), like((4, 8, width), F32)]
    return pl.pallas_call(
        spread_vectors_kernel,
        in_specs=[SMEM_SPEC, SMEM_SPEC] + [pl.BlockSpec(memory_space=pltpu.VMEM)] * 2,
        out_specs=[pl.BlockSpec(memory_space=pltpu.VMEM)] * 3,
        out_shape=outs,
        scratch_shapes=[pltpu.VMEM((12 * D // unit, unit), F32)],
        compiler_params=params(8),
        cost_estimate=cost(0.0, 0.5, 0.0),
        name="spread_vectors",
    )(owner, heads, own, other)


def collect_vectors(owner, heads, unit, pair, *sources):
    return pl.pallas_call(
        collect_vectors_kernel,
        in_specs=[SMEM_SPEC, SMEM_SPEC] + [pl.BlockSpec(memory_space=pltpu.VMEM)] * len(sources),
        out_specs=pl.BlockSpec(memory_space=pltpu.VMEM),
        out_shape=like((FF // unit, 8, pair), F32),
        scratch_shapes=[pltpu.VMEM((12 * D // unit, unit), F32)],
        compiler_params=params(8),
        cost_estimate=cost(0.0, 0.5, 0.0),
        name="collect_vectors",
    )(owner, heads, *sources)


def pack_attention_kernel(qkv_ref, out_ref, vec_ref, pack_ref):
    rows, width = qkv_ref.shape[1:]
    vec_len = vec_ref.shape[1]
    pack_ref[:rows, :width] = qkv_ref[0].astype(BF)
    pack_ref[:rows, width:] = qkv_ref[1].astype(BF)
    vec = jnp.concatenate([vec_ref[...], jnp.zeros((1, 2 * width - vec_len), F32)], 1)
    vec = jnp.concatenate([vec, jnp.zeros((7, 2 * width), F32)], 0)
    pack_ref[rows : rows + 8] = vec.astype(BF)
    pack_ref[rows + 8 :, :width] = qkv_ref[2].astype(BF)
    pack_ref[rows + 8 :, width:] = out_ref[...].T.astype(BF)


def pack_attention(qkv, out, vec):
    rows, width = qkv.shape[1:]
    return pl.pallas_call(
        pack_attention_kernel,
        in_specs=[VMEM_SPEC] * 3,
        out_specs=VMEM_SPEC,
        out_shape=like((2 * rows + 8, 2 * width), BF),
        compiler_params=params(8),
        cost_estimate=cost(0.0, 0.5, 0.0),
        name="pack_attention",
    )(qkv, out, vec)


def advance_attention_kernel(rates, count, *refs):
    terms, olds, outs = refs[:count], refs[count : count + 6], refs[count + 6 :]
    whole_sum = terms[0][...]
    for term in terms[1:]:
        whole_sum = whole_sum + term[...].astype(F32)
    rows, width = olds[0].shape[1], olds[0].shape[2]
    parts = [
        whole_sum[:rows, :width],
        whole_sum[:rows, width:],
        whole_sum[rows + 8 :, :width],
    ]
    for i, grad in enumerate(parts):
        new = advance(olds[0][i], grad, olds[1][i], olds[2][i], DECAY, rates[0])
        for ref, value in zip(outs[:4], (grad, *new)):
            ref[i] = value
    grad = whole_sum[rows + 8 :, width:].T
    new = advance(olds[3][...], grad, olds[4][...], olds[5][...], DECAY, rates[1])
    for ref, value in zip(outs[4:8], (grad, *new)):
        ref[...] = value
    outs[8][...] = whole_sum[rows : rows + 8]


def advance_attention(terms, qkv, out, rates, others):
    outs = [like(qkv[0].shape, F32)] * 4 + [like(out[0].shape, F32)] * 4
    outs.append(like((8, terms[0].shape[1]), F32))
    vmem = pl.BlockSpec(memory_space=pltpu.VMEM)
    kernel = functools.partial(advance_attention_kernel, rates, len(terms))
    kernel, corners, _ = waiting(kernel, others)
    return pl.pallas_call(
        kernel,
        in_specs=[vmem] * (len(corners) + len(terms) + 6),
        out_specs=[vmem] * 9,
        out_shape=outs,
        compiler_params=params(16),
        cost_estimate=cost(0.0, 3.0, 0.0),
        name="advance_attention",
    )(*corners, *terms, *qkv, *out)


def waiting(kernel, others):
    corners = [corner(v) for v in jax.tree.leaves(others)]
    count = len(corners)
    return lambda *refs: kernel(*refs[count:]), corners, [VMEM_SPEC] * count


SMEM_SPEC = pl.BlockSpec(memory_space=pltpu.SMEM)
like = jax.ShapeDtypeStruct


def params(mib):
    return pltpu.CompilerParams(vmem_limit_bytes=mib << 20)


def cost(giga_flops, mega_bytes, mega_exps):
    return pl.CostEstimate(
        flops=int(giga_flops * 1e9),
        bytes_accessed=int(mega_bytes * 1e6),
        transcendentals=int(mega_exps * 1e6),
    )


def attention_forward(place, x, weights, biases, half, mask, vec_rows, mix, rows, others):
    length = x.shape[0]
    pair = weights[0].shape[4]
    width = pair // 2
    last = mix is not None
    row = like((length, D), F32)
    outs = [
        like((2, length, 3 * width), BF),
        like((2, 8, length), F32),
        like((2, length, width), BF),
    ]
    tail = [row]
    scratch = [pltpu.VMEM((D, pair), BF), pltpu.VMEM((D, pair), BF)]
    operands = [*weights, place, x, biases, mask, vec_rows]
    if last:
        low = like((length, D), BF)
        tail = [row, low, row, like((length, 128), F32), like((D, length), BF)]
        operands.append(mix)
        scratch.append(pltpu.VMEM((length, D), F32))
    kernel = functools.partial(attention_forward_kernel, rows, half, last)
    kernel, corners, _ = waiting(kernel, others)
    operands = corners + operands
    return pl.pallas_call(
        kernel,
        in_specs=[SMEM_SPEC if v is place else VMEM_SPEC for v in operands],
        out_specs=[VMEM_SPEC] * len(outs + tail),
        out_shape=outs + tail,
        scratch_shapes=scratch,
        compiler_params=params(14),
        cost_estimate=cost(0.5, 1.0, 0.1),
        name="attention_forward_last" if last else "attention_forward",
    )(*operands)


def attention_backward(place, x_t, gr, gr_t, weights, saved, mask, start, rows, last, others):
    length = gr.shape[0]
    pair = weights[0].shape[4]
    width = pair // 2
    across, _, deep = weights[0].shape[:3]
    qkv, lse, context = saved
    outs = [
        like((2, 2 * across, deep, rows, pair), BF),
        like((2, 8, width), F32),
        like((length, D), BF if last else F32),
    ]
    scratch = [
        pltpu.VMEM((D, pair), BF),
        pltpu.VMEM((D, pair), BF),
        pltpu.VMEM((length, 3 * width), BF),
    ]
    if last:
        scratch.append(pltpu.VMEM((length, D), F32))
    kernel = functools.partial(attention_backward_kernel, rows, last)
    kernel, corners, corner_specs = waiting(kernel, others)
    return pl.pallas_call(
        kernel,
        in_specs=corner_specs + [VMEM_SPEC] * 2 + [SMEM_SPEC] + [VMEM_SPEC] * 8,
        out_specs=[VMEM_SPEC] * 3,
        out_shape=outs,
        scratch_shapes=scratch,
        compiler_params=params(14),
        cost_estimate=cost(0.5, 1.0, 0.1),
        name="attention_backward_last" if last else "attention_backward",
    )(*corners, *weights, place, x_t, gr, gr_t, qkv, lse, context, mask, start)


def ffn_forward(h, hb, weights, bias, vec_rows, tail_operands):
    length = h.shape[0]
    up, down, extra = weights
    count = 4 + len(extra)
    hidden = FF // 2
    assembled = [pltpu.VMEM((hidden // 4, D), BF)] * 2
    last = len(tail_operands) > 0
    row = like((length, D), F32)
    outs = [like((length, hidden), BF), like((length, hidden), BF)]
    tail = [row]
    scratch = []
    if last:
        tail = [like((length, D), BF), row, like((length, 128), F32)]
        scratch = [pltpu.VMEM((length, D), F32)]
    return pl.pallas_call(
        functools.partial(ffn_forward_kernel, count, last),
        in_specs=[VMEM_SPEC] * (count + 4 + len(tail_operands)),
        out_specs=[VMEM_SPEC] * len(outs + tail),
        out_shape=outs + tail,
        scratch_shapes=scratch + assembled,
        compiler_params=params(14),
        cost_estimate=cost(4.9, 12.0, 1.6),
        name="ffn_forward_last" if last else "ffn_forward",
    )(*up, *down, *extra, h, hb, bias, vec_rows, *tail_operands)


def ffn_backward(hb, act, slope, weights, norm, tail_operands, blocks, last):
    length = hb.shape[0]
    up, down, extra = weights
    count = 4 + len(extra)
    hidden = FF // 2
    assembled = [pltpu.VMEM((hidden // 4, D), BF)] * 2
    row = like((length, D), F32)
    low = like((length, D), BF)
    grad = like((hidden, D), BF)
    outs = [grad, grad, like((8, hidden), F32)]
    vector = like((8, D), F32)
    tail = [row, low, like((D, length), BF), vector] if last else [low, vector, row]
    return pl.pallas_call(
        functools.partial(ffn_backward_kernel, blocks, count, last),
        in_specs=[VMEM_SPEC] * (count + 3 + len(norm) + len(tail_operands)),
        out_specs=[VMEM_SPEC] * len(outs + tail),
        out_shape=outs + tail,
        scratch_shapes=([pltpu.VMEM((length, D), F32)] if last else []) + assembled,
        compiler_params=params(14),
        cost_estimate=cost(9.7, 16.0, 0.0),
        name="ffn_backward_last" if last else "ffn_backward",
    )(*up, *down, *extra, hb, act, slope, *norm, *tail_operands)


def advance(weight, grad, moment, average, decay, rate):
    step_grad = grad + decay * weight
    moment_new = MOMENTUM * moment + step_grad
    weight_new = weight - rate * (step_grad + MOMENTUM * moment_new)
    average_new = AVERAGE * average + (1.0 - AVERAGE) * weight_new
    return (weight_new, moment_new, average_new)


def body(
    layer_input,
    lengths,
    cotangent,
    w_qkv,
    w_out,
    w_up,
    w_down,
    vectors,
    mom_qkv,
    mom_out,
    mom_up,
    mom_down,
    mom_vec,
    avg_qkv,
    avg_out,
    avg_up,
    avg_down,
    avg_vec,
):
    z, x, y, c = (lax.axis_index(a) for a in ("z", "x", "y", "c"))
    deep = lax.axis_size("z")
    blocks = deep * 8
    rows, head_cols = w_qkv.shape[1], w_qkv.shape[2]
    pair = 2 * head_cols
    vec_len = vectors.shape[0]
    ff_rows = w_up.shape[1]
    local = layer_input.shape[0]
    length = 4 * local

    kc, kx, ky, kz = jnp.meshgrid(
        jnp.arange(2), jnp.arange(2), jnp.arange(2), z_order(deep), indexing="ij"
    )
    owner = (((z ^ kz) * 2 + (x ^ kx)) * 4 + (y ^ ky) * 2 + (c ^ kc)).reshape(blocks)
    tz, tx, ty, tc = jnp.meshgrid(
        jnp.arange(deep), jnp.arange(2), jnp.arange(2), jnp.arange(2), indexing="ij"
    )
    seat = ((((c ^ tc) * 2 + (x ^ tx)) * 2 + (y ^ ty)) * deep + z_order(deep)[z ^ tz]).reshape(blocks)
    first, second = jnp.meshgrid(jnp.arange(2), jnp.arange(2), indexing="ij")
    group_head = ((y ^ second) * 2 + (c ^ first)).reshape(4)
    head_group = ((c ^ second) * 2 + (y ^ first)).reshape(4)

    in_kernel = rows % 32 == 0 and deep == COUNTS[3]
    owner, group_head = owner.astype(jnp.int32), group_head.astype(jnp.int32)

    if in_kernel:
        pack = pack_attention(w_qkv, w_out, vectors.reshape(1, vec_len))
    else:
        vec_rows = jnp.pad(vectors.astype(BF)[None], ((0, 7), (0, pair - vec_len)))
        pack_qk = jnp.concatenate([w_qkv[0], w_qkv[1]], 1).astype(BF)
        pack_vo = jnp.concatenate([w_qkv[2], w_out.T], 1).astype(BF)
        pack = jnp.concatenate([pack_qk, vec_rows, pack_vo], 0)
    (doc_x, doc_cot), x_y = to_documents(layer_input, cotangent)
    attn_z, z_first, z_second = gather_z(pack)
    qk, vo = attn_z[:, : rows + 8], attn_z[:, rows + 8 :]
    first_sent = (qk, vo)
    qk_first, vo_first = send(qk, "y"), send(vo, "x")
    qk = after(jnp.stack([qk, qk_first], 0), vo_first, x_y)
    vo = after(jnp.stack([vo, vo_first], 0), qk_first)
    qk_got, vo_got = send(qk, "x"), send(vo, "y")
    qk, vo = jnp.stack([qk, qk_got], 0), jnp.stack([vo, vo_got], 0)
    qk_other, vo_other = send(qk, "c"), send(vo, "c")

    main = main_rows(ff_rows)
    up_t, down_b = w_up.T.astype(BF), w_down.astype(BF)
    extra = jnp.concatenate([up_t[main:], down_b[main:]], 0)
    extra = jnp.stack([extra, send(extra, "x")], 0)
    extra_got = send(extra, "y")
    pack = jnp.concatenate([up_t[:main], down_b[:main]], 0)
    ffn_z, z_third, z_fourth = gather_z(after(pack, z_first), first_sent)
    up, down = ffn_z[:, :main], ffn_z[:, main:]
    up_got, down_got = send(up, "y"), send(down, "x")
    up, down = (
        after(jnp.stack([up, up_got], 0), down_got, qk_got, vo_got),
        after(jnp.stack([down, down_got], 0), up_got, qk_got, vo_got),
    )
    extra = after(jnp.stack([extra, extra_got], 1), z_third, first_sent)
    extra, extra_far = gather_z(extra, (z_fourth,), True)
    if False:
        up, down = after(up, extra_far), after(down, extra_far)
    up_got, down_got = send(up, "x"), send(down, "y")

    vec_own, vec_other = (v[..., rows:, :].astype(F32) for v in (qk, qk_other))
    if in_kernel:
        vec_rows, bias_up, biases = spread_vectors(
            owner, group_head, vec_own, vec_other, ff_rows, head_cols
        )
    else:
        vec_all = jnp.stack([v[..., 0, :vec_len] for v in (vec_own, vec_other)], 0)
        vec_all = vec_all.reshape(blocks, vec_len)
        vec_rows = jnp.take(vec_all, seat, axis=0).reshape(12, D)
        bias_up = jnp.take(vec_rows[5:9].reshape(blocks, ff_rows), owner, axis=0)
        bias_up = bias_up.reshape(2, 4, deep, ff_rows)
        bias_up = [v.reshape(2, 4, -1) for v in (bias_up[..., :main], bias_up[..., main:])]
        bias_up = jnp.concatenate(bias_up, 2).reshape(2, 1, FF // 2)
        bias_up = jnp.pad(bias_up, ((0, 0), (0, 7), (0, 0)))
        bias_q = jnp.take(vec_rows[0].reshape(4, head_cols), group_head, axis=0)
        bias_v = jnp.take(vec_rows[1].reshape(4, head_cols), group_head, axis=0)
        biases = jnp.pad(jnp.stack([bias_q, bias_v], 1), ((0, 0), (0, 6), (0, 0)))

    row = jnp.arange(length)
    part = row // local
    position = ((y ^ (part % 2)) * 2 + (c ^ (part // 2))) * local + row % local
    doc_len = lax.dynamic_index_in_dim(lengths, y * 2 + c, 0, keepdims=False)
    alive = position < doc_len
    mask = jnp.where(alive, 0.0, -1e30).astype(F32)
    mask_row = jnp.broadcast_to(mask[None, :], (8, length))
    mask_col = jnp.broadcast_to(mask[:, None], (length, 128))

    if in_kernel:
        zs = flip_order("z")[None, :]
        place = (zs * 2 + (x ^ jnp.arange(2)[:, None])).reshape(2 * deep)
        kernel_rows = rows
    else:
        xs = x ^ jnp.arange(2)
        zs = flip_order("z")

        def true_order(qk, vo):
            qk = jnp.take(jnp.take(qk[..., :rows, :], xs, axis=0), zs, axis=2)
            vo = jnp.take(jnp.take(vo, xs, axis=1), zs, axis=2)
            qk, vo = qk.transpose(1, 2, 0, 3, 4), vo.transpose(0, 2, 1, 3, 4)
            return qk.reshape(1, 2, 1, D, pair), vo.reshape(2, 1, 1, D, pair)

        def relative_order(qk, vo):
            qk = qk.reshape(2, deep, 2, rows, pair).transpose(2, 0, 1, 3, 4)
            vo = vo.reshape(2, deep, 2, rows, pair).transpose(0, 2, 1, 3, 4)
            qk = jnp.take(jnp.take(qk, xs, axis=0), zs, axis=2)
            return qk, jnp.take(jnp.take(vo, xs, axis=1), zs, axis=2)

        place = jnp.zeros((1,), jnp.int32)
        qk, vo = true_order(qk, vo)
        qk_other, vo_other = true_order(qk_other, vo_other)
        kernel_rows = D
        size = 2 * deep * (ff_rows - main)
        extra = extra[0].reshape(deep, 2, 2, 2, ff_rows - main, D).transpose(1, 2, 3, 0, 4, 5)
        extra = (extra.reshape(1, 2, 2, size, D),)
    place = place.astype(jnp.int32)

    *saved_0, mix = attention_forward(
        place, doc_x, (qk, vo), biases, 0, mask_row, vec_rows, None, kernel_rows, ()
    )
    *saved_1, hidden, hidden_b, normed, inverse, x_t = attention_forward(
        place, doc_x, (qk_other, vo_other), biases, 1, mask_row, vec_rows, mix, kernel_rows, (extra[-1],)
    )
    flat = lambda v: v.reshape(2 * deep * main, D)
    ffn_own = (flat(up), flat(up_got)), (flat(down), flat(down_got)), extra
    across = lambda parts, early: tuple(
        send(part if i < early else after(part, hidden_b), "c") for i, part in enumerate(parts)
    )
    ffn_other = tuple(across(parts, early) for parts, early in zip(ffn_own, (1, 1, 0)))
    act_0, slope_0, mix = ffn_forward(
        hidden, hidden_b, ffn_own, bias_up[0], vec_rows, ()
    )
    act_1, slope_1, result, normed_two, inverse_two = ffn_forward(
        hidden, hidden_b, ffn_other, bias_up[1], vec_rows, (mix,)
    )
    out_own, out_y = from_documents_y(result, local)

    lead = (2, 2, deep, ff_rows, D)
    kernel_blocks = deep if in_kernel else 1
    norm_two = (normed_two, inverse_two, vec_rows)
    up_1, down_1, d_bias_1, d_second_b, vec_two, d_hidden = ffn_backward(
        hidden_b, act_1, slope_1, ffn_other, norm_two, (doc_cot, mask_col), kernel_blocks, False
    )
    up_1, down_1 = send(up_1, "c"), send(down_1, "c")
    norm_one = (normed, inverse, vec_rows)
    up_0, down_0, d_bias_0, d_first, d_first_b, d_first_t, vec_one = ffn_backward(
        hidden_b, act_0, slope_0, ffn_own, norm_one, (d_second_b, d_hidden), kernel_blocks, True
    )
    ffn_c = (up_1, down_1)
    if not in_kernel:

        def by_block(grad):
            grad = grad.reshape(4, deep * ff_rows, D)
            parts = (grad[:, : deep * main], grad[:, deep * main :])
            return jnp.concatenate([v.reshape(4, deep, -1, D) for v in parts], 2)

        up_0, up_1, down_0, down_1 = (by_block(v) for v in (up_0, up_1, down_0, down_1))
    grad_up = swap([up_0.reshape(lead), up_1.reshape(lead)], "x")
    grad_down = swap([down_0.reshape(lead), down_1.reshape(lead)], "y")
    ffn_big = (grad_up[-1], grad_down[-1])
    grad_up, grad_down = swap(grad_up, "y"), swap(grad_down, "x")
    ffn_second = (grad_up[-1], grad_down[-1])
    grad_ffn, _ = scatter_z([grad_up, grad_down], False)

    attn_1, bias_1, d_attn = attention_backward(
        place, x_t, d_first_b, d_first_t, (qk_other, vo_other), saved_1, mask_col, d_first, kernel_rows, False, ffn_c
    )
    attn_0, bias_0, d_input = attention_backward(
        place, x_t, d_first_b, d_first_t, (qk, vo), saved_0, mask_col, d_attn, kernel_rows, True, (after(corner(out_y), bias_1[0]),)
    )
    attn_1 = send(attn_1, "c")
    if in_kernel:
        pairs = [v.reshape(2, 2, 2, deep, rows, pair) for v in (attn_0, attn_1)]
    else:
        pairs = [relative_order(v[0], v[1]) for v in (attn_0, attn_1)]
    (qk_0, vo_0), (qk_1, vo_1) = pairs

    bias_0 = after(bias_0, ffn_big)
    if in_kernel:
        vec_part = collect_vectors(
            owner, group_head, ff_rows, pair, bias_0, bias_1, d_bias_0, d_bias_1, vec_one, vec_two
        ).reshape(2, 2, 2, deep, 8, pair)
    else:
        d_bias = jnp.concatenate([bias_0, bias_1], 0)
        d_bias_q = jnp.take(d_bias[:, 0], head_group, axis=0).reshape(D)
        d_bias_v = jnp.take(d_bias[:, 1], head_group, axis=0).reshape(D)
        d_bias_up = jnp.stack([d_bias_0[0], d_bias_1[0]], 0).reshape(2, 4, -1)
        parts = (d_bias_up[..., : deep * main], d_bias_up[..., deep * main :])
        d_bias_up = jnp.concatenate([v.reshape(blocks, -1) for v in parts], 1)
        d_bias_up = jnp.take(d_bias_up, seat, axis=0).reshape(FF)
        grad_vec = jnp.concatenate(
            [
                d_bias_q,
                d_bias_v,
                vec_one[2],
                vec_one[0],
                vec_one[1],
                d_bias_up,
                vec_two[2],
                vec_two[0],
                vec_two[1],
            ]
        )
        vec_part = jnp.take(grad_vec.reshape(blocks, vec_len), owner, axis=0)
        vec_part = jnp.pad(vec_part, ((0, 0), (0, pair - vec_len))).reshape(2, 2, 2, deep, 1, pair)
        vec_part = jnp.pad(vec_part, ((0, 0),) * 4 + ((0, 7), (0, 0)))
    vec_part = vec_part[0] + send(vec_part[1], "c")
    sum_qk, vec_terms, sum_vo = [qk_0, qk_1], [vec_part], [vo_0, vo_1]
    for axis_qk, axis_vo in (("x", "y"), ("y", "x")):
        part = jnp.concatenate(
            [total([t[1] for t in sum_qk]), total([t[1] for t in vec_terms])], -2
        )
        got = send(after(part, ffn_second).astype(BF), axis_qk)
        sum_qk = [t[0] for t in sum_qk] + [got[..., :rows, :]]
        vec_terms = [t[0] for t in vec_terms] + [got[..., rows:, :]]
        sum_vo = swap(sum_vo, axis_vo, ffn_second)
    d_input = after(d_input, got, sum_vo[-1])
    grad_attn, sent = scatter_z([sum_qk, vec_terms, sum_vo], True)
    grad_ffn = after(total(grad_ffn), sent)
    grad_up, grad_down = grad_ffn[:ff_rows].T, grad_ffn[ff_rows:]
    layer_output = from_documents(group_head, after(out_own, grad_ffn), out_y, BF)
    grad_input = from_documents(group_head, *from_documents_y(d_input, local), F32)

    slots = length * layer_input.shape[1] * deep * 2
    rate = RATE_BASE / math.sqrt(slots)
    rate_out = rate * math.sqrt(LEN / 8.0)
    olds_qkv, olds_out = (w_qkv, mom_qkv, avg_qkv), (w_out, mom_out, avg_out)
    if in_kernel:
        (
            grad_qkv,
            new_qkv,
            new_mom_qkv,
            new_avg_qkv,
            grad_out,
            new_out,
            new_mom_out,
            new_avg_out,
            grad_vec,
        ) = advance_attention(
            grad_attn, olds_qkv, olds_out, (rate, rate_out), (layer_output, grad_input)
        )
        grad_vec = grad_vec[0, :vec_len]
    else:
        grad_attn = total(grad_attn)
        sum_qk, sum_vo = grad_attn[:rows], grad_attn[rows + 8 :]
        grad_qkv = jnp.stack([sum_qk[:, :head_cols], sum_qk[:, head_cols:], sum_vo[:, :head_cols]])
        grad_out = sum_vo[:, head_cols:].T
        grad_vec = grad_attn[rows, :vec_len]
        new_qkv, new_mom_qkv, new_avg_qkv = advance(
            w_qkv, grad_qkv, mom_qkv, avg_qkv, DECAY, rate
        )
        new_out, new_mom_out, new_avg_out = advance(
            w_out, grad_out, mom_out, avg_out, DECAY, rate_out
        )
    new_up, new_mom_up, new_avg_up = advance(w_up, grad_up, mom_up, avg_up, DECAY, rate)
    new_down, new_mom_down, new_avg_down = advance(
        w_down, grad_down, mom_down, avg_down, DECAY, rate
    )
    new_vec, new_mom_vec, new_avg_vec = advance(vectors, grad_vec, mom_vec, avg_vec, 0.0, rate)
    return (
        layer_output,
        grad_input,
        grad_qkv,
        grad_out,
        grad_up,
        grad_down,
        grad_vec,
        new_qkv,
        new_out,
        new_up,
        new_down,
        new_vec,
        new_mom_qkv,
        new_mom_out,
        new_mom_up,
        new_mom_down,
        new_mom_vec,
        new_avg_qkv,
        new_avg_out,
        new_avg_up,
        new_avg_down,
        new_avg_vec,
    )


def solution(mesh):
    dp, head = mesh.shape["dp"], mesh.shape["head"]
    fine = Mesh(mesh.devices.reshape(dp // 2, 2, head // 2, 2), ("z", "x", "y", "c"))
    dps, heads, every = ("z", "x"), ("y", "c"), ("z", "x", "y", "c")
    acts = P(heads, dps, None)
    weights = (P(None, dps, heads), P(heads, dps), P(None, every), P(every, None), P(every))
    return jax.shard_map(
        body,
        mesh=fine,
        in_specs=(acts, P(dps), acts) + weights * 3,
        out_specs=(acts, acts) + weights * 4,
        check_vma=False,
    )
```
